128 devices in a mesh: lat: 4 (over y_lo, core), lon: 32 (over z, x, y_hi).
Axes of the slice: x: 4, y: 4 (y_hi: 2, y_lo: 2; y = y_hi * 2 + y_lo), z: 4, core: 2. Of those that a mesh axis runs over, the one named last changes fastest.
Arguments:
- query_vectors: bfloat16 [128, 512, 512], P('lat', 'lon'), may hold values from -6 to 6
- key_vectors: bfloat16 [128, 512, 512], P('lat', 'lon'), may hold values from -6 to 6
- value_vectors: bfloat16 [128, 512, 512], P('lat', 'lon'), may hold values from -6 to 6
- output_grads: bfloat16 [128, 512, 512], P('lat', 'lon'), may hold values from -6 to 6
Outputs:
- query_grads: bfloat16 [128, 512, 512], P('lat', 'lon')
- key_grads: bfloat16 [128, 512, 512], P('lat', 'lon')
- value_grads: bfloat16 [128, 512, 512], P('lat', 'lon')
The draws below stay inside these ranges and needn't reach their ends.
All inputs are finite; a program needn't handle non-finite values.
Results may differ from the reference program's by a relative error of at most 0.0084.
Values may be sent and summed in bfloat16 or wider, within the bound.
No kernel may reach another device: no remote copies, remote signals or barrier semaphores. Data moves between devices by JAX's collectives and lax.ppermute only.
A program may use at most 128 MiB of HBM per device.

```python
import jax
import jax.numpy as jnp
from jax import lax

TILE = 8
HEADS = 8
HEAD_DIM = 64
FEAT = 512
NLAT = 128
NLON = 512


def base_draw(key):
    grid_shape = (NLAT, NLON, FEAT)
    return jnp.clip(jax.random.normal(key, grid_shape, jnp.float32), -6.0, 6.0)


def draw_query_vectors(key, part):
    base_values = base_draw(jax.random.fold_in(key, 1))
    return base_values.astype(jnp.bfloat16)


def draw_key_vectors(key, part):
    base_values = base_draw(jax.random.fold_in(key, 2))
    return base_values.astype(jnp.bfloat16)


def block_levels(own_key, shape, split, smallest, top_value):
    def one(position, shards_of):
        steps = jax.random.uniform(jax.random.fold_in(jax.random.fold_in(own_key, 6), position), (shards_of,), jnp.float32, smallest / len(split), top_value / len(split))
        return jnp.repeat(jnp.exp(steps), shape[position] // shards_of).reshape((-1,) + (1,) * (len(shape) - position - 1))

    gain = one(*split[0])
    for cut in split[1:]:
        gain = gain * one(*cut)
    return gain


def gaussian(rng, dims, spread, limit, cuts=(), kind=jnp.bfloat16):
    values = jax.random.normal(rng, dims, jnp.float32) * spread
    if len(cuts) > 0:
        values = block_levels(rng, dims, cuts, -0.22, 0.18) * values
    return jnp.clip(values, min=-limit, max=limit).astype(kind)


def setup_inputs(seed: int = 0) -> dict:
    keys = jax.random.split(jax.random.key(seed), 5)
    return {
        "query_vectors": draw_query_vectors(jax.random.fold_in(keys[4], 71), 0),
        "key_vectors": draw_key_vectors(jax.random.fold_in(keys[4], 71), 0),
        "value_vectors": gaussian(keys[2], (NLAT, NLON, FEAT), 1.0, 6.0, ((0, 4), (1, 32))),
        "output_grads": gaussian(keys[3], (NLAT, NLON, FEAT), 1.0, 6.0, ((0, 4), (1, 32))),
    }


MASKED = -1.0e30


def rounded(array_in):
    return lax.optimization_barrier(array_in.astype(jnp.bfloat16)).astype(jnp.float32)


def to_tiles(grid_array):
    grid_rows, grid_cols, features = grid_array.shape
    shaped = grid_array.reshape(grid_rows // TILE, TILE, grid_cols // TILE, TILE, features)
    return shaped.transpose(0, 2, 1, 3, 4).reshape(grid_rows // TILE, grid_cols // TILE, TILE * TILE, features)


def from_tiles(tile_array):
    row_tiles, col_tiles, tile_cells, features = tile_array.shape
    shaped = tile_array.reshape(row_tiles, col_tiles, TILE, TILE, features).transpose(0, 2, 1, 3, 4)
    return shaped.reshape(row_tiles * TILE, col_tiles * TILE, features)


def extend(grid_array):
    wrapped = jnp.concatenate([grid_array[:, -TILE:], grid_array, grid_array[:, :TILE]], axis=1)
    return jnp.pad(wrapped, ((TILE, TILE), (0, 0), (0, 0)))


def neighbours(window, row_tiles):
    col_tiles = window.shape[1] - 2
    pieces = [window[row_off:row_off + row_tiles, col_off:col_off + col_tiles] for row_off in range(3) for col_off in range(3)]
    stacked = jnp.stack(pieces, axis=2)
    return stacked.reshape(row_tiles * col_tiles, 9 * window.shape[2], window.shape[3])


def block_mask(first_row, row_tiles, col_tiles, tile_cells, total_rows):
    offsets = (lax.broadcasted_iota(jnp.int32, (row_tiles, 3), 0)
               + lax.broadcasted_iota(jnp.int32, (row_tiles, 3), 1) - 1 + first_row)
    inside = (offsets >= 0) & (offsets < total_rows)
    inside = jnp.broadcast_to(inside[:, None, :, None, None], (row_tiles, col_tiles, 3, 3, tile_cells))
    return inside.reshape(row_tiles * col_tiles, 9 * tile_cells)


def split_heads(array_in):
    return array_in.reshape(array_in.shape[0], array_in.shape[1], HEADS, HEAD_DIM)


def query_side(query_block, key_block, value_block, grad_block, inside, score_scale):
    q_heads = split_heads(query_block)
    k_heads = split_heads(key_block)
    v_heads = split_heads(value_block)
    g_heads = split_heads(grad_block)
    high = lax.Precision.HIGHEST
    scores = jnp.einsum("tqhe,tkhe->thqk", q_heads, k_heads, precision=high) * score_scale
    scores = jnp.where(inside[:, None, None, :], scores, MASKED)
    row_max = jnp.max(scores, axis=-1)
    row_total = jnp.sum(jnp.exp(scores - row_max[..., None]), axis=-1)
    log_total = row_max + jnp.log(row_total)
    prob_weights = jnp.exp(scores - log_total[..., None])
    dprobs = jnp.einsum("tqhe,tkhe->thqk", g_heads, v_heads, precision=high)
    row_delta = jnp.sum(prob_weights * dprobs, axis=-1)
    dscores = rounded(prob_weights * (dprobs - row_delta[..., None]))
    query_grad = jnp.einsum("thqk,tkhe->tqhe", dscores, k_heads, precision=high) * score_scale
    return query_grad.reshape(query_block.shape), log_total, row_delta


def key_side(key_block, value_block, query_near, grad_near, log_near, delta_near, inside, score_scale):
    k_heads = split_heads(key_block)
    v_heads = split_heads(value_block)
    q_heads = split_heads(query_near)
    g_heads = split_heads(grad_near)
    high = lax.Precision.HIGHEST
    scores = jnp.einsum("tkhe,tqhe->thkq", k_heads, q_heads, precision=high) * score_scale
    shifted = jnp.where(inside[:, None, None, :], scores - log_near.transpose(0, 2, 1)[:, :, None, :], MASKED)
    prob_weights = jnp.exp(shifted)
    dprobs = jnp.einsum("tkhe,tqhe->thkq", v_heads, g_heads, precision=high)
    dscores = rounded(prob_weights * (dprobs - delta_near.transpose(0, 2, 1)[:, :, None, :]))
    key_grad = jnp.einsum("thkq,tqhe->tkhe", dscores, q_heads, precision=high) * score_scale
    value_grad = jnp.einsum("thkq,tqhe->tkhe", rounded(prob_weights), g_heads, precision=high)
    return key_grad.reshape(key_block.shape), value_grad.reshape(key_block.shape)


def reference(query_vectors, key_vectors, value_vectors, output_grads):
    score_scale = HEAD_DIM ** -0.5
    band_rows = NLAT // TILE
    sector_cols = NLON // TILE
    tile_cells = TILE * TILE
    query_full = query_vectors.astype(jnp.float32)
    key_full = key_vectors.astype(jnp.float32)
    value_full = value_vectors.astype(jnp.float32)
    grad_full = output_grads.astype(jnp.float32)
    key_tiles = to_tiles(extend(key_full))
    value_tiles = to_tiles(extend(value_full))
    query_tiles = to_tiles(query_full)
    grad_tiles = to_tiles(grad_full)

    def front(tile_row):
        key_near = neighbours(lax.dynamic_slice_in_dim(key_tiles, tile_row, 3, 0), 1)
        value_near = neighbours(lax.dynamic_slice_in_dim(value_tiles, tile_row, 3, 0), 1)
        query_block = lax.dynamic_index_in_dim(query_tiles, tile_row, 0, keepdims=False)
        grad_block = lax.dynamic_index_in_dim(grad_tiles, tile_row, 0, keepdims=False)
        inside = block_mask(tile_row, 1, sector_cols, tile_cells, band_rows)
        return query_side(query_block, key_near, value_near, grad_block, inside, score_scale)

    query_grad, log_total, row_delta = lax.map(front, jnp.arange(band_rows, dtype=jnp.int32))
    log_grid = from_tiles(log_total.transpose(0, 1, 3, 2))
    delta_grid = from_tiles(row_delta.transpose(0, 1, 3, 2))
    query_near_tiles = to_tiles(extend(query_full))
    grad_near_tiles = to_tiles(extend(grad_full))
    log_tiles = to_tiles(extend(log_grid))
    delta_tiles = to_tiles(extend(delta_grid))
    own_keys = to_tiles(key_full)
    own_values = to_tiles(value_full)

    def back(tile_row):
        key_block = lax.dynamic_index_in_dim(own_keys, tile_row, 0, keepdims=False)
        value_block = lax.dynamic_index_in_dim(own_values, tile_row, 0, keepdims=False)
        query_near = neighbours(lax.dynamic_slice_in_dim(query_near_tiles, tile_row, 3, 0), 1)
        grad_near = neighbours(lax.dynamic_slice_in_dim(grad_near_tiles, tile_row, 3, 0), 1)
        log_near = neighbours(lax.dynamic_slice_in_dim(log_tiles, tile_row, 3, 0), 1)
        delta_near = neighbours(lax.dynamic_slice_in_dim(delta_tiles, tile_row, 3, 0), 1)
        inside = block_mask(tile_row, 1, sector_cols, tile_cells, band_rows)
        return key_side(key_block, value_block, query_near, grad_near, log_near, delta_near, inside, score_scale)

    key_grad, value_grad = lax.map(back, jnp.arange(band_rows, dtype=jnp.int32))
    return (from_tiles(query_grad).astype(jnp.bfloat16),
            from_tiles(key_grad).astype(jnp.bfloat16),
            from_tiles(value_grad).astype(jnp.bfloat16))
```

```python
import functools

import jax
import jax.numpy as jnp
from jax import lax
from jax.experimental import pallas as pl
from jax.experimental.pallas import tpu as pltpu
from jax.sharding import PartitionSpec as P

ROWS = 4
CELLS = 64
OWN = ROWS * CELLS
EXT = (ROWS + 2) * CELLS
PAIR = 128
PAIRS = 4
FEAT = 512
SCALE = 64 ** -0.5
LOG2E = 1.4426950408889634
MASKED = -1e30
F32 = jnp.float32
BF16 = jnp.bfloat16
VMEM_LIMIT = 48 * 1024 * 1024


def matmul(a, b, contract):
    return lax.dot_general(a, b, ((contract[:1], contract[1:]), ((), ())), preferred_element_type=F32)


def params():
    return pltpu.CompilerParams(vmem_limit_bytes=VMEM_LIMIT)


def cost(flops, size):
    return pl.CostEstimate(flops=int(flops), bytes_accessed=int(size), transcendentals=0)


def struct(shape, dtype):
    return jax.ShapeDtypeStruct(shape, dtype)


def split_columns(block):
    wide = block.astype(F32)
    return [wide[:, c * 8:(c + 1) * 8].reshape(CELLS, FEAT).astype(BF16) for c in range(2)]


def pack_kernel(q_ref, k_ref, v_ref, g_ref, west_ref, east_ref, kd_ref, vd_ref, north_ref, south_ref):
    step = pl.program_id(0)
    q0, q1 = split_columns(q_ref[...])
    g0, g1 = split_columns(g_ref[...])
    west_ref[0] = q0
    west_ref[1] = g0
    east_ref[0] = q1
    east_ref[1] = g1
    keys = split_columns(k_ref[...])
    values = split_columns(v_ref[...])
    for c in range(2):
        kd_ref[c] = keys[c]
        vd_ref[c] = values[c]

    @pl.when(step == 0)
    def _():
        for c in range(2):
            north_ref[0, c] = keys[c]
            north_ref[1, c] = values[c]

    @pl.when(step == ROWS - 1)
    def _():
        for c in range(2):
            south_ref[0, c] = keys[c]
            south_ref[1, c] = values[c]


def pack(q, k, v, g):
    grid_spec = pl.BlockSpec((8, 16, FEAT), lambda t: (t, 0, 0))
    tile_spec = pl.BlockSpec((2, CELLS, FEAT), lambda t: (0, t, 0))
    edge_spec = pl.BlockSpec((2, 2, CELLS, FEAT), lambda t: (0, 0, 0, 0))
    tiles = struct((2, OWN, FEAT), BF16)
    edge = struct((2, 2, CELLS, FEAT), BF16)
    return pl.pallas_call(
        pack_kernel,
        grid=(ROWS,),
        in_specs=[grid_spec] * 4,
        out_specs=[tile_spec] * 4 + [edge_spec] * 2,
        out_shape=[tiles] * 4 + [edge] * 2,
        compiler_params=params(),
        cost_estimate=cost(0, 5 << 20),
        name="pack",
    )(q, k, v, g)


def head_masks():
    lane = lax.broadcasted_iota(jnp.int32, (1, PAIR), 1)
    first = jnp.where(lane < 64, 1.0, 0.0).astype(F32)
    return first.astype(BF16), (1.0 - first).astype(BF16)


def stacked(parts, masks):
    return jnp.concatenate([part * mask for part in parts for mask in masks], axis=0)


def pole_biases():
    lat = lax.axis_index("lat")
    count = lax.axis_size("lat")
    return (jnp.where(lat == 0, MASKED, 0.0).astype(F32),
            jnp.where(lat == count - 1, MASKED, 0.0).astype(F32))


def fill_keys(ext, own, north, south, which):
    for c in range(2):
        ext[c, 0:CELLS] = north[which, c]
        ext[c, CELLS:CELLS + OWN] = own[c]
        ext[c, CELLS + OWN:EXT] = south[which, c]


def window(ext, columns, t, first=0, last=3):
    parts = [ext[c, (t + first) * CELLS:(t + last) * CELLS] for c in columns]
    return parts[0] if len(parts) == 1 else jnp.concatenate(parts, axis=0)


def score_block(keys, queries, columns, t, biases, first=0, last=3):
    scores = matmul(keys, queries, (1, 1)) * (SCALE * LOG2E)
    if t + first > 0 and t + last < ROWS + 2:
        return scores
    parts = []
    span = (last - first) * CELLS
    for c in range(columns):
        for r in range(first, last):
            base = c * span + (r - first) * CELLS
            part = scores[base:base + CELLS]
            if t + r == 0:
                part = part + biases[0]
            if t + r == ROWS + 1:
                part = part + biases[1]
            parts.append(part)
    return jnp.concatenate(parts, axis=0)


def row_stats(scores, dprobs):
    top = jnp.max(scores, axis=0, keepdims=True)
    weights = jnp.exp2(scores - top)
    total = jnp.sum(weights, axis=0, keepdims=True)
    delta = jnp.sum(weights * dprobs, axis=0, keepdims=True) / total
    return top + jnp.log(total) * LOG2E, delta


def merged(log_a, delta_a, log_b, delta_b):
    top = jnp.maximum(log_a, log_b)
    weight_a = jnp.exp2(log_a - top)
    weight_b = jnp.exp2(log_b - top)
    total = weight_a + weight_b
    return top + jnp.log(total) * LOG2E, (weight_a * delta_a + weight_b * delta_b) / total


def own_heads(lane, x):
    return jnp.where(lane < 64, x[0:CELLS], x[CELLS:2 * CELLS])


def stats_kernel(west, east, kd, vd, north, south, st0, st1, kx, vx):
    masks = head_masks()
    biases = pole_biases()
    fill_keys(kx, kd, north, south, 0)
    fill_keys(vx, vd, north, south, 1)
    for t in range(ROWS):
        at = slice(t * CELLS, (t + 1) * CELLS)
        queries = stacked([west[0, at], east[0, at]], masks)
        grads = stacked([west[1, at], east[1, at]], masks)
        scores = score_block(window(kx, (0, 1), t), queries, 2, t, biases)
        dprobs = matmul(window(vx, (0, 1), t), grads, (1, 1))
        log_total, delta = row_stats(scores, dprobs)
        st0[0, t:t + 1] = log_total[:, :PAIR]
        st1[0, t:t + 1] = log_total[:, PAIR:]
        st0[0, ROWS + t:ROWS + t + 1] = delta[:, :PAIR]
        st1[0, ROWS + t:ROWS + t + 1] = delta[:, PAIR:]


tokens_spec = pl.BlockSpec((2, OWN, PAIR), lambda p: (0, 0, p))
edge_spec = pl.BlockSpec((2, 2, CELLS, PAIR), lambda p: (0, 0, 0, p))
stats_spec = pl.BlockSpec((1, 8, PAIR), lambda p: (p, 0, 0))
stats_shape = struct((PAIRS, 8, PAIR), F32)
key_scratch = [pltpu.VMEM((2, EXT, PAIR), BF16)] * 2


def own_stats(west, east, kd, vd, north, south):
    return pl.pallas_call(
        stats_kernel,
        grid=(PAIRS,),
        in_specs=[tokens_spec] * 4 + [edge_spec] * 2,
        out_specs=[stats_spec] * 2,
        out_shape=[stats_shape] * 2,
        scratch_shapes=key_scratch,
        compiler_params=params(),
        cost_estimate=cost(3e9, 3 << 20),
        name="own_stats",
    )(west, east, kd, vd, north, south)


def halo_kernel(q_west, q_east, kd, vd, north, south, in_west, in_east,
                dq_west, dq_east, out_west, out_east, fin_west, fin_east, kx, vx):
    masks = head_masks()
    biases = pole_biases()
    lane = lax.broadcasted_iota(jnp.int32, (1, PAIR), 1)
    fill_keys(kx, kd, north, south, 0)
    fill_keys(vx, vd, north, south, 1)
    sides = ((q_west, in_west, dq_west, out_west, fin_west), (q_east, in_east, dq_east, out_east, fin_east))
    for c, (q_in, st_in, dq_out, st_out, st_fin) in enumerate(sides):
        for t in range(ROWS):
            at = slice(t * CELLS, (t + 1) * CELLS)
            row, low = slice(t, t + 1), slice(ROWS + t, ROWS + t + 1)
            queries = stacked([q_in[0, at]], masks)
            grads = stacked([q_in[1, at]], masks)
            keys = window(kx, (c,), t)
            scores = score_block(keys, queries, 1, t, biases)
            dprobs = matmul(window(vx, (c,), t), grads, (1, 1))
            log_part, delta_part = row_stats(scores, dprobs)
            log_total, delta = merged(log_part, delta_part, st_in[0, row], st_in[0, low])
            dscores = (jnp.exp2(scores - log_total) * (dprobs - delta)).astype(BF16)
            grad = matmul(dscores, keys, (0, 0)) * SCALE
            dq_out[at] = own_heads(lane, grad).astype(BF16)
            st_out[0, row] = log_part
            st_out[0, low] = delta_part
            st_fin[0, row] = log_total
            st_fin[0, low] = delta


def halo(q_west, q_east, kd, vd, north, south, in_west, in_east):
    grad_spec = pl.BlockSpec((OWN, PAIR), lambda p: (0, p))
    return pl.pallas_call(
        halo_kernel,
        grid=(PAIRS,),
        in_specs=[tokens_spec] * 4 + [edge_spec] * 2 + [stats_spec] * 2,
        out_specs=[grad_spec] * 2 + [stats_spec] * 4,
        out_shape=[struct((OWN, FEAT), BF16)] * 2 + [stats_shape] * 4,
        scratch_shapes=key_scratch,
        compiler_params=params(),
        cost_estimate=cost(3e9, 4 << 20),
        name="halo",
    )(q_west, q_east, kd, vd, north, south, in_west, in_east)


def grads_kernel(west, east, q_west, q_east, kd, vd, north, south, st0, st1, add0, add1, fin_west, fin_east,
                 dq_ref, dk_ref, dv_ref, dnorth, dsouth, kx, vx, dkx, dvx):
    masks = head_masks()
    biases = pole_biases()
    lane = lax.broadcasted_iota(jnp.int32, (1, PAIR), 1)
    fill_keys(kx, kd, north, south, 0)
    fill_keys(vx, vd, north, south, 1)
    dkx[...] = jnp.zeros_like(dkx)
    dvx[...] = jnp.zeros_like(dvx)

    def work(columns, q_parts, g_parts, log_total, delta, t):
        queries = stacked(q_parts, masks)
        grads = stacked(g_parts, masks)
        keys = window(kx, columns, t)
        scores = score_block(keys, queries, len(columns), t, biases)
        dprobs = matmul(window(vx, columns, t), grads, (1, 1))
        probs = jnp.exp2(scores - log_total)
        dscores = (probs * (dprobs - delta)).astype(BF16)
        key_part = matmul(dscores, queries, (1, 0))
        value_part = matmul(probs.astype(BF16), grads, (1, 0))
        for i, c in enumerate(columns):
            here = slice(t * CELLS, (t + 3) * CELLS)
            there = slice(i * 3 * CELLS, (i + 1) * 3 * CELLS)
            dkx[c, here] += key_part[there]
            dvx[c, here] += value_part[there]
        return dscores, keys

    for t in range(ROWS):
        at = slice(t * CELLS, (t + 1) * CELLS)
        row, low = slice(t, t + 1), slice(ROWS + t, ROWS + t + 1)
        log0, delta0 = merged(st0[0, row], st0[0, low], add0[0, row], add0[0, low])
        log1, delta1 = merged(st1[0, row], st1[0, low], add1[0, row], add1[0, low])
        dscores, keys = work((0, 1), [west[0, at], east[0, at]], [west[1, at], east[1, at]],
                             jnp.concatenate([log0, log1], axis=1), jnp.concatenate([delta0, delta1], axis=1), t)
        grad = matmul(dscores, keys, (0, 0)) * SCALE
        dq_ref[0, at] = own_heads(lane, grad[:PAIR])
        dq_ref[1, at] = own_heads(lane, grad[PAIR:])
        work((0,), [q_west[0, at]], [q_west[1, at]], fin_west[0, row], fin_west[0, low], t)
        work((1,), [q_east[0, at]], [q_east[1, at]], fin_east[0, row], fin_east[0, low], t)
    for c in range(2):
        dk_ref[c] = dkx[c, CELLS:CELLS + OWN] * SCALE
        dv_ref[c] = dvx[c, CELLS:CELLS + OWN]
        dnorth[0, c] = (dkx[c, 0:CELLS] * SCALE).astype(BF16)
        dnorth[1, c] = dvx[c, 0:CELLS].astype(BF16)
        dsouth[0, c] = (dkx[c, CELLS + OWN:EXT] * SCALE).astype(BF16)
        dsouth[1, c] = dvx[c, CELLS + OWN:EXT].astype(BF16)


def gradients(*operands):
    return pl.pallas_call(
        grads_kernel,
        grid=(PAIRS,),
        in_specs=[tokens_spec] * 6 + [edge_spec] * 2 + [stats_spec] * 6,
        out_specs=[tokens_spec] * 3 + [edge_spec] * 2,
        out_shape=[struct((2, OWN, FEAT), F32)] * 3 + [struct((2, 2, CELLS, FEAT), BF16)] * 2,
        scratch_shapes=key_scratch + [pltpu.VMEM((2, EXT, PAIR), F32)] * 2,
        compiler_params=params(),
        cost_estimate=cost(8e9, 8 << 20),
        name="gradients",
    )(*operands)


def join_columns(parts):
    return jnp.concatenate([part.reshape(8, 8, FEAT) for part in parts], axis=1).astype(BF16)


def finish_kernel(dq, dk, dv, dq0, dq1, from_north, from_south, q_ref, k_ref, v_ref):
    step = pl.program_id(0)
    first = jnp.where(step == 0, 1.0, 0.0).astype(F32)
    last = jnp.where(step == ROWS - 1, 1.0, 0.0).astype(F32)
    q_ref[...] = join_columns([dq[0] + dq0[...].astype(F32), dq[1] + dq1[...].astype(F32)])
    for which, (own, out) in enumerate(((dk, k_ref), (dv, v_ref))):
        out[...] = join_columns([
            own[c] + from_north[which, c].astype(F32) * first + from_south[which, c].astype(F32) * last
            for c in range(2)
        ])


def finish(*operands):
    grid_spec = pl.BlockSpec((8, 16, FEAT), lambda t: (t, 0, 0))
    tile_spec = pl.BlockSpec((2, CELLS, FEAT), lambda t: (0, t, 0))
    part_spec = pl.BlockSpec((CELLS, FEAT), lambda t: (t, 0))
    edge = pl.BlockSpec((2, 2, CELLS, FEAT), lambda t: (0, 0, 0, 0))
    return pl.pallas_call(
        finish_kernel,
        grid=(ROWS,),
        in_specs=[tile_spec] * 3 + [part_spec] * 2 + [edge] * 2,
        out_specs=[grid_spec] * 3,
        out_shape=[struct((8 * ROWS, 16, FEAT), BF16)] * 3,
        compiler_params=params(),
        cost_estimate=cost(0, 6 << 20),
        name="finish",
    )(*operands)


def shift(x, axis, by, wrap):
    count = lax.axis_size(axis)
    pairs = [(i, (i + by) % count) for i in range(count) if wrap or 0 <= i + by < count]
    return lax.ppermute(x, axis, pairs)


def on_device(query_vectors, key_vectors, value_vectors, output_grads):
    to_east = functools.partial(shift, axis="lon", by=1, wrap=True)
    to_west = functools.partial(shift, axis="lon", by=-1, wrap=True)
    to_south = functools.partial(shift, axis="lat", by=1, wrap=False)
    to_north = functools.partial(shift, axis="lat", by=-1, wrap=False)
    west, east, kd, vd, north_edge, south_edge = pack(query_vectors, key_vectors, value_vectors, output_grads)
    q_west = to_east(east)
    q_east = to_west(west)
    north = to_south(south_edge)
    south = to_north(north_edge)
    st0, st1 = own_stats(west, east, kd, vd, north, south)
    in_west = to_east(st1)
    in_east = to_west(st0)
    dq_west, dq_east, out_west, out_east, fin_west, fin_east = halo(
        q_west, q_east, kd, vd, north, south, in_west, in_east)
    add1 = to_west(out_west)
    add0 = to_east(out_east)
    dq1 = to_west(dq_west)
    dq0 = to_east(dq_east)
    dq, dk, dv, dnorth, dsouth = gradients(
        west, east, q_west, q_east, kd, vd, north, south, st0, st1, add0, add1, fin_west, fin_east)
    from_south = to_north(dnorth)
    from_north = to_south(dsouth)
    return tuple(finish(dq, dk, dv, dq0, dq1, from_north, from_south))


def solution(mesh):
    spec = P("lat", "lon", None)
    return jax.shard_map(on_device, mesh=mesh, in_specs=(spec,) * 4, out_specs=(spec,) * 3, check_vma=False)
```

```python
import functools

import jax
import jax.numpy as jnp
from jax import lax
from jax.experimental import pallas as pl
from jax.experimental.pallas import tpu as pltpu
from jax.sharding import PartitionSpec as P

ROWS = 4
CELLS = 64
OWN = ROWS * CELLS
PAIR = 128
PAIRS = 4
FEAT = 512
SCALE = 64 ** -0.5
LOG2E = 1.4426950408889634
MASKED = -1e30
F32 = jnp.float32
BF16 = jnp.bfloat16
VMEM_LIMIT = 20 * 1024 * 1024
PACK_LIMIT = 62 * 1024 * 1024


def matmul(a, b, contract):
    return lax.dot_general(a, b, ((contract[:1], contract[1:]), ((), ())), preferred_element_type=F32)


def params(limit=VMEM_LIMIT):
    return pltpu.CompilerParams(vmem_limit_bytes=limit)


def cost(flops, size):
    return pl.CostEstimate(flops=int(flops), bytes_accessed=int(size), transcendentals=0)


def struct(shape, dtype):
    return jax.ShapeDtypeStruct(shape, dtype)


def split_columns(block):
    wide = block.astype(F32)
    return [wide[:, c * 8:(c + 1) * 8].reshape(CELLS, FEAT).astype(BF16) for c in range(2)]


def fetch(refs, buffers, sems):
    copies = [[pltpu.make_async_copy(ref.at[pl.ds(8 * t, 8)], buffers.at[i, t], sems.at[i, t])
               for t in range(ROWS)] for i, ref in enumerate(refs)]
    for t in range(ROWS):
        for copy in copies:
            copy[t].start()
    return copies


def pack_queries_kernel(q_ref, g_ref, west, east, buffers, sems):
    copies = fetch((q_ref, g_ref), buffers, sems)
    for t in range(ROWS):
        for i in range(2):
            copies[i][t].wait()
            first, second = split_columns(buffers[i, t])
            west[i, t * CELLS:(t + 1) * CELLS] = first
            east[i, t * CELLS:(t + 1) * CELLS] = second


def pack_keys_kernel(k_ref, v_ref, kd, vd, north, south, buffers, sems):
    copies = fetch((k_ref, v_ref), buffers, sems)
    for t in range(ROWS):
        for i, out in enumerate((kd, vd)):
            copies[i][t].wait()
            tile = jnp.concatenate(split_columns(buffers[i, t]), axis=0)
            out[t * PAIR:(t + 1) * PAIR] = tile
            if t == 0:
                north[i] = tile
            if t == ROWS - 1:
                south[i] = tile


def pack(kernel, x, y, out_shape, name):
    return pl.pallas_call(
        kernel,
        in_specs=[pl.BlockSpec(memory_space=pltpu.HBM)] * 2,
        out_shape=out_shape,
        scratch_shapes=[pltpu.VMEM((2, ROWS, 8, 16, FEAT), BF16), pltpu.SemaphoreType.DMA((2, ROWS))],
        compiler_params=params(PACK_LIMIT),
        cost_estimate=cost(0, 3 << 20),
        name=name,
    )(x, y)


def head_masks(lanes):
    lane = lax.broadcasted_iota(jnp.int32, (1, lanes), 1)
    return [jnp.where((lane >= 64 * h) & (lane < 64 * (h + 1)), 1.0, 0.0).astype(F32).astype(BF16)
            for h in range(lanes // 64)]


def stacked(parts, masks):
    return jnp.concatenate([part * mask for part in parts for mask in masks], axis=0)


def pole_biases():
    lat = lax.axis_index("lat")
    count = lax.axis_size("lat")
    return (jnp.where(lat == 0, MASKED, 0.0).astype(F32),
            jnp.where(lat == count - 1, MASKED, 0.0).astype(F32))


def key_row(own, north, south, which, row):
    if row == 0:
        return north[which]
    if row == ROWS + 1:
        return south[which]
    return own[(row - 1) * PAIR:row * PAIR]


def window(own, north, south, which, t, column=None):
    rows = [key_row(own, north, south, which, t + i) for i in range(3)]
    if column is not None:
        rows = [row[column * CELLS:(column + 1) * CELLS] for row in rows]
    return jnp.concatenate(rows, axis=0)


def score_block(keys, queries, t, biases):
    scores = matmul(keys, queries, (1, 1)) * (SCALE * LOG2E)
    span = keys.shape[0] // 3
    if t == 0:
        scores = jnp.concatenate([scores[:span] + biases[0], scores[span:]], axis=0)
    if t == ROWS - 1:
        scores = jnp.concatenate([scores[:2 * span], scores[2 * span:] + biases[1]], axis=0)
    return scores


def row_stats(scores, dprobs):
    top = jnp.max(scores, axis=0, keepdims=True)
    weights = jnp.exp2(scores - top)
    total = jnp.sum(weights, axis=0, keepdims=True)
    delta = jnp.sum(weights * dprobs, axis=0, keepdims=True) / total
    return top + jnp.log(total) * LOG2E, delta


def merged(log_a, delta_a, log_b, delta_b):
    top = jnp.maximum(log_a, log_b)
    weight_a = jnp.exp2(log_a - top)
    weight_b = jnp.exp2(log_b - top)
    total = weight_a + weight_b
    return top + jnp.log(total) * LOG2E, (weight_a * delta_a + weight_b * delta_b) / total


def query_part(keys, dscores, lane):
    turned = matmul(keys, dscores, (0, 0)).T * SCALE
    return jnp.where(lane < 64, turned[:CELLS], turned[CELLS:])


EDGE_ROWS = (0, 3)
MID_ROWS = (1, 2)
tokens_spec = pl.BlockSpec((2, OWN, PAIR), lambda p: (0, 0, p))
keys_spec = pl.BlockSpec((ROWS * PAIR, PAIR), lambda p: (0, p))
edge_spec = pl.BlockSpec((2, PAIR, PAIR), lambda p: (0, 0, p))
stats_spec = pl.BlockSpec((1, 8, PAIR), lambda p: (p, 0, 0))
stats_shape = struct((PAIRS, 8, PAIR), F32)
held_spec = pl.BlockSpec((1, 2, 3 * PAIR, 2 * PAIR), lambda p: (p, 0, 0, 0))
held_shape = struct((PAIRS, 2, 3 * PAIR, 2 * PAIR), F32)


def stats_kernel(west, east, kd, vd, north, south, st0, st1, s_edge, d_edge, s_mid, d_mid):
    masks = head_masks(PAIR)
    biases = pole_biases()
    for t in range(ROWS):
        at = slice(t * CELLS, (t + 1) * CELLS)
        queries = stacked([west[0, at], east[0, at]], masks)
        grads = stacked([west[1, at], east[1, at]], masks)
        scores = score_block(window(kd, north, south, 0, t), queries, t, biases)
        dprobs = matmul(window(vd, north, south, 1, t), grads, (1, 1))
        s_out, d_out, place = (s_edge, d_edge, t // 3) if t in EDGE_ROWS else (s_mid, d_mid, t - 1)
        s_out[0, place] = scores
        d_out[0, place] = dprobs
        log_total, delta = row_stats(scores, dprobs)
        st0[0, t:t + 1] = log_total[:, :PAIR]
        st1[0, t:t + 1] = log_total[:, PAIR:]
        st0[0, ROWS + t:ROWS + t + 1] = delta[:, :PAIR]
        st1[0, ROWS + t:ROWS + t + 1] = delta[:, PAIR:]


def own_stats(*operands):
    return pl.pallas_call(
        stats_kernel,
        grid=(PAIRS,),
        in_specs=[tokens_spec] * 2 + [keys_spec] * 2 + [edge_spec] * 2,
        out_specs=[stats_spec] * 2 + [held_spec] * 4,
        out_shape=[stats_shape] * 2 + [held_shape] * 4,
        compiler_params=params(),
        cost_estimate=cost(0, 1 << 10),
        name="own_stats",
    )(*operands)


def halo_kernel(q_west, q_east, kd, vd, north, south, in_west, in_east,
                dq_west, dq_east, out_west, out_east, dkx, dvx):
    masks = head_masks(2 * PAIR)
    biases = pole_biases()
    lane = lax.broadcasted_iota(jnp.int32, (1, PAIR), 1)
    dkx[...] = jnp.zeros_like(dkx)
    dvx[...] = jnp.zeros_like(dvx)
    sides = ((q_west, in_west, dq_west, out_west), (q_east, in_east, dq_east, out_east))
    for t in range(ROWS):
        at = slice(t * CELLS, (t + 1) * CELLS)
        row, low = slice(t, t + 1), slice(ROWS + t, ROWS + t + 1)
        for c, (q_in, st_in, dq_out, st_out) in enumerate(sides):
            queries = stacked([q_in[0, at]], masks)
            grads = stacked([q_in[1, at]], masks)
            keys = window(kd, north, south, 0, t, c)
            scores = score_block(keys, queries, t, biases)
            dprobs = matmul(window(vd, north, south, 1, t, c), grads, (1, 1))
            log_part, delta_part = row_stats(scores, dprobs)
            for j in range(2):
                st_out[j, row] = log_part[:, j * PAIR:(j + 1) * PAIR]
                st_out[j, low] = delta_part[:, j * PAIR:(j + 1) * PAIR]
            log_home = jnp.concatenate([st_in[j, row] for j in range(2)], axis=1)
            delta_home = jnp.concatenate([st_in[j, low] for j in range(2)], axis=1)
            log_total, delta = merged(log_part, delta_part, log_home, delta_home)
            probs = jnp.exp2(scores - log_total)
            dscores = (probs * (dprobs - delta)).astype(BF16)
            for j in range(2):
                lanes = slice(j * PAIR, (j + 1) * PAIR)
                dq_out[at, lanes] = query_part(keys[:, lanes], dscores[:, lanes], lane).astype(BF16)
            key_part = matmul(dscores, queries, (1, 0))
            value_part = matmul(probs.astype(BF16), grads, (1, 0))
            for i in range(3):
                here = slice((t + i) * PAIR + c * CELLS, (t + i) * PAIR + (c + 1) * CELLS)
                dkx[here] += key_part[i * CELLS:(i + 1) * CELLS]
                dvx[here] += value_part[i * CELLS:(i + 1) * CELLS]


def halo(*operands):
    wide = 2 * PAIR
    tokens = pl.BlockSpec((2, OWN, wide), lambda p: (0, 0, p))
    keys = pl.BlockSpec((ROWS * PAIR, wide), lambda p: (0, p))
    edge = pl.BlockSpec((2, PAIR, wide), lambda p: (0, 0, p))
    stats = pl.BlockSpec((2, 8, PAIR), lambda p: (p, 0, 0))
    grads = pl.BlockSpec((OWN, wide), lambda p: (0, p))
    sums = pl.BlockSpec(((ROWS + 2) * PAIR, wide), lambda p: (0, p))
    return pl.pallas_call(
        halo_kernel,
        grid=(2,),
        in_specs=[tokens] * 2 + [keys] * 2 + [edge] * 2 + [stats] * 2,
        out_specs=[grads] * 2 + [stats] * 2 + [sums] * 2,
        out_shape=[struct((OWN, FEAT), BF16)] * 2 + [stats_shape] * 2 + [struct(((ROWS + 2) * PAIR, FEAT), F32)] * 2,
        compiler_params=params(),
        cost_estimate=cost(3e9, 4 << 20),
        name="halo",
    )(*operands)


def own_work(t, place, west, east, kd, north, south, st0, st1, add0, add1, s_in, d_in, masks, lane, dq_ref):
    at = slice(t * CELLS, (t + 1) * CELLS)
    row, low = slice(t, t + 1), slice(ROWS + t, ROWS + t + 1)
    queries = stacked([west[0, at], east[0, at]], masks)
    grads = stacked([west[1, at], east[1, at]], masks)
    log0, delta0 = merged(st0[0, row], st0[0, low], add0[0, row], add0[0, low])
    log1, delta1 = merged(st1[0, row], st1[0, low], add1[0, row], add1[0, low])
    probs = jnp.exp2(s_in[0, place] - jnp.concatenate([log0, log1], axis=1))
    dscores = (probs * (d_in[0, place] - jnp.concatenate([delta0, delta1], axis=1))).astype(BF16)
    keys = window(kd, north, south, 0, t)
    for c in range(2):
        dq_ref[c, at] = query_part(keys, dscores[:, c * PAIR:(c + 1) * PAIR], lane)
    return matmul(dscores, queries, (1, 0)), matmul(probs.astype(BF16), grads, (1, 0))


def edge_kernel(west, east, kd, north, south, st0, st1, add0, add1, s_in, d_in, dkx, dvx,
                dq_ref, dk_ref, dv_ref, dnorth, dsouth):
    masks = head_masks(PAIR)
    lane = lax.broadcasted_iota(jnp.int32, (1, PAIR), 1)
    last = ROWS * PAIR
    parts = [own_work(t, i, west, east, kd, north, south, st0, st1, add0, add1, s_in, d_in, masks, lane, dq_ref)
             for i, t in enumerate(EDGE_ROWS)]
    for which, (sums, out, scale) in enumerate(((dkx, dk_ref, SCALE), (dvx, dv_ref, 1.0))):
        top, bottom = parts[0][which], parts[1][which]
        out[0:2 * PAIR] = sums[PAIR:3 * PAIR] + top[PAIR:]
        out[2 * PAIR:last] = sums[3 * PAIR:PAIR + last] + bottom[:2 * PAIR]
        dnorth[which] = ((sums[0:PAIR] + top[:PAIR]) * scale).astype(BF16)
        dsouth[which] = ((sums[PAIR + last:] + bottom[2 * PAIR:]) * scale).astype(BF16)


def mid_kernel(west, east, kd, north, south, st0, st1, add0, add1, s_in, d_in, dq_in, dk_in, dv_in,
               dq_ref, dk_ref, dv_ref):
    masks = head_masks(PAIR)
    lane = lax.broadcasted_iota(jnp.int32, (1, PAIR), 1)
    parts = [own_work(t, i, west, east, kd, north, south, st0, st1, add0, add1, s_in, d_in, masks, lane, dq_ref)
             for i, t in enumerate(MID_ROWS)]
    for t in EDGE_ROWS:
        at = slice(t * CELLS, (t + 1) * CELLS)
        for c in range(2):
            dq_ref[c, at] = dq_in[c, at]
    for which, (sums, out, scale) in enumerate(((dk_in, dk_ref, SCALE), (dv_in, dv_ref, 1.0))):
        upper, lower = parts[0][which], parts[1][which]
        out[0:PAIR] = (sums[0:PAIR] + upper[:PAIR]) * scale
        out[PAIR:3 * PAIR] = (sums[PAIR:3 * PAIR] + upper[PAIR:] + lower[:2 * PAIR]) * scale
        out[3 * PAIR:] = (sums[3 * PAIR:] + lower[2 * PAIR:]) * scale


OWN_SPECS = [tokens_spec] * 2 + [keys_spec] + [edge_spec] * 2 + [stats_spec] * 4 + [held_spec] * 2
GRAD_SPECS = [tokens_spec] + [keys_spec] * 2
GRAD_SHAPES = [struct((2, OWN, FEAT), F32)] + [struct((ROWS * PAIR, FEAT), F32)] * 2


def edge_gradients(*operands):
    sums = pl.BlockSpec(((ROWS + 2) * PAIR, PAIR), lambda p: (0, p))
    return pl.pallas_call(
        edge_kernel,
        grid=(PAIRS,),
        in_specs=OWN_SPECS + [sums] * 2,
        out_specs=GRAD_SPECS + [edge_spec] * 2,
        out_shape=GRAD_SHAPES + [struct((2, PAIR, FEAT), BF16)] * 2,
        compiler_params=params(),
        cost_estimate=cost(3e9, 8 << 20),
        name="edge_gradients",
    )(*operands)


def mid_gradients(*operands):
    return pl.pallas_call(
        mid_kernel,
        grid=(PAIRS,),
        in_specs=OWN_SPECS + GRAD_SPECS,
        out_specs=GRAD_SPECS,
        out_shape=GRAD_SHAPES,
        compiler_params=params(),
        cost_estimate=cost(3e9, 8 << 20),
        name="mid_gradients",
    )(*operands)


def join_columns(parts):
    return jnp.concatenate([part.reshape(8, 8, FEAT) for part in parts], axis=1).astype(BF16)


def finish_kernel(dq, dk, dv, dq0, dq1, from_north, from_south, q_ref, k_ref, v_ref):
    step = pl.program_id(0)
    first = jnp.where(step == 0, 1.0, 0.0).astype(F32)
    last = jnp.where(step == ROWS - 1, 1.0, 0.0).astype(F32)
    q_ref[...] = join_columns([dq[0] + dq0[...].astype(F32), dq[1] + dq1[...].astype(F32)])
    for which, (own, out) in enumerate(((dk, k_ref), (dv, v_ref))):
        full = own[...] + from_north[which].astype(F32) * first + from_south[which].astype(F32) * last
        out[...] = join_columns([full[:CELLS], full[CELLS:]])


def finish(*operands):
    grid_spec = pl.BlockSpec((8, 16, FEAT), lambda t: (t, 0, 0))
    tile_spec = pl.BlockSpec((2, CELLS, FEAT), lambda t: (0, t, 0))
    row_spec = pl.BlockSpec((PAIR, FEAT), lambda t: (t, 0))
    part_spec = pl.BlockSpec((CELLS, FEAT), lambda t: (t, 0))
    edge = pl.BlockSpec((2, PAIR, FEAT), lambda t: (0, 0, 0))
    return pl.pallas_call(
        finish_kernel,
        grid=(ROWS,),
        in_specs=[tile_spec] + [row_spec] * 2 + [part_spec] * 2 + [edge] * 2,
        out_specs=[grid_spec] * 3,
        out_shape=[struct((8 * ROWS, 16, FEAT), BF16)] * 3,
        compiler_params=params(),
        cost_estimate=cost(0, 6 << 20),
        name="finish",
    )(*operands)


def shift(x, axis, by, wrap):
    count = lax.axis_size(axis)
    pairs = [(i, (i + by) % count) for i in range(count) if wrap or 0 <= i + by < count]
    return lax.ppermute(x, axis, pairs)


def on_device(query_vectors, key_vectors, value_vectors, output_grads):
    to_east = functools.partial(shift, axis="lon", by=1, wrap=True)
    to_west = functools.partial(shift, axis="lon", by=-1, wrap=True)
    to_south = functools.partial(shift, axis="lat", by=1, wrap=False)
    to_north = functools.partial(shift, axis="lat", by=-1, wrap=False)
    tokens = struct((2, OWN, FEAT), BF16)
    tiles = struct((ROWS * PAIR, FEAT), BF16)
    edge = struct((2, PAIR, FEAT), BF16)
    west, east = pack(pack_queries_kernel, query_vectors, output_grads, [tokens] * 2, "pack_queries")
    kd, vd, north_edge, south_edge = pack(pack_keys_kernel, key_vectors, value_vectors,
                                          [tiles] * 2 + [edge] * 2, "pack_keys")
    q_west = to_east(east)
    q_east = to_west(west)
    north = to_south(south_edge)
    south = to_north(north_edge)
    st0, st1, s_edge, d_edge, s_mid, d_mid = own_stats(west, east, kd, vd, north, south)
    in_west = to_east(st1)
    in_east = to_west(st0)
    dq_west, dq_east, out_west, out_east, dkx, dvx = halo(q_west, q_east, kd, vd, north, south, in_west, in_east)
    add1 = to_west(out_west)
    add0 = to_east(out_east)
    dq1 = to_west(dq_west)
    dq0 = to_east(dq_east)
    own = (west, east, kd, north, south, st0, st1, add0, add1)
    dq, dk, dv, dnorth, dsouth = edge_gradients(*own, s_edge, d_edge, dkx, dvx)
    from_south = to_north(dnorth)
    from_north = to_south(dsouth)
    dq, dk, dv = mid_gradients(*own, s_mid, d_mid, dq, dk, dv)
    return tuple(finish(dq, dk, dv, dq0, dq1, from_north, from_south))


def solution(mesh):
    spec = P("lat", "lon", None)
    return jax.shard_map(on_device, mesh=mesh, in_specs=(spec,) * 4, out_specs=(spec,) * 3, check_vma=False)
```

```python
import jax
import jax.numpy as jnp
from jax import lax
from jax.experimental import pallas as pl
from jax.experimental.pallas import tpu as pltpu
from jax.sharding import PartitionSpec as P

ROWS = 4
CELLS = 64
OWN = ROWS * CELLS
PAIR = 128
WIDE = 256
PAIRS = 4
GROUPS = 2
FEAT = 512
SCALE = 64 ** -0.5
LOG2E = 1.4426950408889634
MASKED = -1e30
F32 = jnp.float32
BF16 = jnp.bfloat16
VMEM_LIMIT = 20 * 1024 * 1024
PACK_LIMIT = 62 * 1024 * 1024
EDGE_ROWS = (0, 3)
MID_ROWS = (1, 2)


def matmul(a, b, contract):
    return lax.dot_general(a, b, ((contract[:1], contract[1:]), ((), ())), preferred_element_type=F32)


def params(limit=VMEM_LIMIT):
    return pltpu.CompilerParams(vmem_limit_bytes=limit)


def cost(flops, size):
    return pl.CostEstimate(flops=int(flops), bytes_accessed=int(size), transcendentals=0)


def struct(shape, dtype):
    return jax.ShapeDtypeStruct(shape, dtype)


def grid_row(t):
    return jnp.where(lax.axis_index("lat") % 2 == 0, ROWS - 1 - t, t)


def ordered(first, second):
    swap = lax.axis_index("lon") % 2 == 0
    return jnp.where(swap, second, first), jnp.where(swap, first, second)


def split_columns(block):
    wide = block.astype(F32)
    parts = ordered(*[wide[:, c * 8:(c + 1) * 8].reshape(CELLS, FEAT) for c in range(2)])
    return [part.astype(BF16) for part in parts]


def fetch(refs, buffers, sems):
    copies = [[pltpu.make_async_copy(ref.at[pl.ds(8 * grid_row(t), 8)], buffers.at[i, t], sems.at[i, t])
               for t in range(ROWS)] for i, ref in enumerate(refs)]
    for t in range(ROWS):
        for copy in copies:
            copy[t].start()
    return copies


def pack_queries_kernel(q_ref, g_ref, side_a, side_b, buffers, sems):
    copies = fetch((q_ref, g_ref), buffers, sems)
    for t in range(ROWS):
        for i in range(2):
            copies[i][t].wait()
            first, second = split_columns(buffers[i, t])
            side_a[i, t * CELLS:(t + 1) * CELLS] = first
            side_b[i, t * CELLS:(t + 1) * CELLS] = second


def pack_keys_kernel(k_ref, v_ref, kd, vd, edge_a, edge_b, buffers, sems):
    copies = fetch((k_ref, v_ref), buffers, sems)
    for t in range(ROWS):
        for i, out in enumerate((kd, vd)):
            copies[i][t].wait()
            tile = jnp.concatenate(split_columns(buffers[i, t]), axis=0)
            out[t * PAIR:(t + 1) * PAIR] = tile
            if t == 0:
                edge_a[i] = tile
            if t == ROWS - 1:
                edge_b[i] = tile


def pack(kernel, x, y, out_shape, name, limit):
    return pl.pallas_call(
        kernel,
        in_specs=[pl.BlockSpec(memory_space=pl.ANY)] * 2,
        out_shape=out_shape,
        scratch_shapes=[pltpu.VMEM((2, ROWS, 8, 16, FEAT), BF16), pltpu.SemaphoreType.DMA((2, ROWS))],
        compiler_params=params(limit),
        cost_estimate=cost(0, 3 << 20),
        name=name,
    )(x, y)


def head_masks(lanes):
    lane = lax.broadcasted_iota(jnp.int32, (1, lanes), 1)
    return [jnp.where((lane >= 64 * h) & (lane < 64 * (h + 1)), 1.0, 0.0).astype(F32).astype(BF16)
            for h in range(lanes // 64)]


def stacked(parts, masks):
    return jnp.concatenate([part * mask for part in parts for mask in masks], axis=0)


def key_rows(own, edge_a, edge_b, which, t, lanes=slice(None)):
    rows = []
    for row in range(t, t + 3):
        if row == 0:
            rows.append(edge_a[which, :, lanes])
        elif row == ROWS + 1:
            rows.append(edge_b[which, :, lanes])
        else:
            rows.append(own[(row - 1) * PAIR:row * PAIR, lanes])
    return rows


def window(*where):
    return jnp.concatenate(key_rows(*where), axis=0)


def column_window(column, *where):
    return jnp.concatenate([row[column * CELLS:(column + 1) * CELLS] for row in key_rows(*where)], axis=0)


def score_block(keys, queries, t):
    scores = matmul(keys, queries, (1, 1)) * (SCALE * LOG2E)
    if t == ROWS - 1:
        lat = lax.axis_index("lat")
        outside = (lat == 0) | (lat == lax.axis_size("lat") - 1)
        cut = 2 * (keys.shape[0] // 3)
        bias = jnp.where(outside, MASKED, 0.0).astype(F32)
        scores = jnp.concatenate([scores[:cut], scores[cut:] + bias], axis=0)
    return scores


def row_stats(scores, dprobs):
    top = jnp.max(scores, axis=0, keepdims=True)
    weights = jnp.exp2(scores - top)
    total = jnp.sum(weights, axis=0, keepdims=True)
    delta = jnp.sum(weights * dprobs, axis=0, keepdims=True) / total
    return top + jnp.log(total) * LOG2E, delta


def merged(log_a, delta_a, log_b, delta_b):
    top = jnp.maximum(log_a, log_b)
    weight_a = jnp.exp2(log_a - top)
    weight_b = jnp.exp2(log_b - top)
    total = weight_a + weight_b
    return top + jnp.log(total) * LOG2E, (weight_a * delta_a + weight_b * delta_b) / total


def from_both(mine, theirs, pair, base, t):
    mine_at, theirs_at = base + 2 * t, 8 - base + 2 * t
    return merged(mine[pair, mine_at:mine_at + 1], mine[pair, mine_at + 1:mine_at + 2],
                  theirs[pair, theirs_at:theirs_at + 1], theirs[pair, theirs_at + 1:theirs_at + 2])


def query_part(keys, dscores, lane):
    turned = matmul(keys, dscores, (0, 0)).T * SCALE
    return jnp.where(lane < 64, turned[:CELLS], turned[CELLS:])


def at_tokens(t):
    return slice(t * CELLS, (t + 1) * CELLS)


tokens_spec = pl.BlockSpec((2, OWN, PAIR), lambda p: (0, 0, p))
keys_spec = pl.BlockSpec((ROWS * PAIR, PAIR), lambda p: (0, p))
edge_spec = pl.BlockSpec((2, PAIR, PAIR), lambda p: (0, 0, p))
part_spec = pl.BlockSpec((1, 8, PAIR), lambda p: (p, 0, 0))
held_spec = pl.BlockSpec((1, 2, 3 * PAIR, WIDE), lambda p: (p, 0, 0, 0))
part_shape = struct((PAIRS, 8, PAIR), F32)
held_shape = struct((PAIRS, 2, 3 * PAIR, WIDE), F32)

tokens_wide = pl.BlockSpec((2, OWN, WIDE), lambda g: (0, 0, g))
keys_wide = pl.BlockSpec((ROWS * PAIR, WIDE), lambda g: (0, g))
edge_wide = pl.BlockSpec((2, PAIR, WIDE), lambda g: (0, 0, g))
part_wide = pl.BlockSpec((2, 8, PAIR), lambda g: (g, 0, 0))
stats_wide = pl.BlockSpec((2, 16, PAIR), lambda g: (g, 0, 0))
held_wide = pl.BlockSpec((2, 2, 3 * PAIR, WIDE), lambda g: (g, 0, 0, 0))
halo_wide = pl.BlockSpec((1, 2, 2, 3 * CELLS, WIDE), lambda g: (g, 0, 0, 0, 0))
stats_shape = struct((PAIRS, 16, PAIR), F32)
halo_shape = struct((GROUPS, 2, 2, 3 * CELLS, WIDE), F32)


def own_scores(rows, side_a, side_b, kd, vd, edge_a, edge_b, part, s_out, d_out):
    masks = head_masks(PAIR)
    for place, t in enumerate(rows):
        at = at_tokens(t)
        queries = stacked([side_a[0, at], side_b[0, at]], masks)
        grads = stacked([side_a[1, at], side_b[1, at]], masks)
        scores = score_block(window(kd, edge_a, edge_b, 0, t), queries, t)
        dprobs = matmul(window(vd, edge_a, edge_b, 1, t), grads, (1, 1))
        s_out[0, place] = scores
        d_out[0, place] = dprobs
        for w, values in enumerate(row_stats(scores, dprobs)):
            for c in range(2):
                index = 4 * c + 2 * place + w
                part[0, index:index + 1] = values[:, c * PAIR:(c + 1) * PAIR]


def mid_scores_kernel(side_a, side_b, kd, vd, part, s_out, d_out):
    own_scores(MID_ROWS, side_a, side_b, kd, vd, None, None, part, s_out, d_out)


def edge_scores_kernel(side_a, side_b, kd, vd, edge_a, edge_b, part, s_out, d_out):
    own_scores(EDGE_ROWS, side_a, side_b, kd, vd, edge_a, edge_b, part, s_out, d_out)


def scores_call(kernel, operands, name):
    return pl.pallas_call(
        kernel,
        grid=(PAIRS,),
        in_specs=[tokens_spec] * 2 + [keys_spec] * 2 + [edge_spec] * (len(operands) - 4),
        out_specs=[part_spec] + [held_spec] * 2,
        out_shape=[part_shape] + [held_shape] * 2,
        compiler_params=params(),
        cost_estimate=cost(2e9, 3 << 20),
        name=name,
    )(*operands)


def halo_scores_kernel(q_a, q_b, kd, vd, edge_a, edge_b, part_edge, part_mid,
                       send_a, send_b, s_edge, d_edge, s_mid, d_mid):
    masks = head_masks(WIDE)
    for t in range(ROWS):
        at = at_tokens(t)
        held = (s_edge, d_edge) if t in EDGE_ROWS else (s_mid, d_mid)
        place = t // 3 if t in EDGE_ROWS else t - 1
        part = part_edge if t in EDGE_ROWS else part_mid
        for c, (q_in, send) in enumerate(((q_a, send_a), (q_b, send_b))):
            queries = stacked([q_in[0, at]], masks)
            grads = stacked([q_in[1, at]], masks)
            scores = score_block(column_window(c, kd, edge_a, edge_b, 0, t), queries, t)
            dprobs = matmul(column_window(c, vd, edge_a, edge_b, 1, t), grads, (1, 1))
            held[0][0, place, c] = scores
            held[1][0, place, c] = dprobs
            for w, values in enumerate(row_stats(scores, dprobs)):
                for j in range(2):
                    index = 2 * t + w
                    source = 4 * c + 2 * place + w
                    send[j, index:index + 1] = part[j, source:source + 1]
                    send[j, 8 + index:9 + index] = values[:, j * PAIR:(j + 1) * PAIR]


def halo_scores(*operands):
    return pl.pallas_call(
        halo_scores_kernel,
        grid=(GROUPS,),
        in_specs=[tokens_wide] * 2 + [keys_wide] * 2 + [edge_wide] * 2 + [part_wide] * 2,
        out_specs=[stats_wide] * 2 + [halo_wide] * 4,
        out_shape=[stats_shape] * 2 + [halo_shape] * 4,
        compiler_params=params(),
        cost_estimate=cost(2e9, 3 << 20),
        name="halo_scores",
    )(*operands)


def halo_weights(mine, theirs, s_in, d_in, place, c, t):
    both = [from_both(mine, theirs, j, 8, t) for j in range(2)]
    log_total = jnp.concatenate([one[0] for one in both], axis=1)
    delta = jnp.concatenate([one[1] for one in both], axis=1)
    probs = jnp.exp2(s_in[0, place, c] - log_total)
    return probs.astype(BF16), (probs * (d_in[0, place, c] - delta)).astype(BF16)


def halo_queries_kernel(kd, edge_a, edge_b, send_a, send_b, recv_a, recv_b, s_edge, d_edge, s_mid, d_mid, dq_a, dq_b):
    lane = lax.broadcasted_iota(jnp.int32, (1, PAIR), 1)
    for t in range(ROWS):
        held = (s_edge, d_edge) if t in EDGE_ROWS else (s_mid, d_mid)
        place = t // 3 if t in EDGE_ROWS else t - 1
        for c, (mine, theirs, out) in enumerate(((send_a, recv_a, dq_a), (send_b, recv_b, dq_b))):
            _, dscores = halo_weights(mine, theirs, *held, place, c, t)
            keys = column_window(c, kd, edge_a, edge_b, 0, t)
            for j in range(2):
                lanes = slice(j * PAIR, (j + 1) * PAIR)
                out[at_tokens(t), lanes] = query_part(keys[:, lanes], dscores[:, lanes], lane).astype(BF16)


def halo_queries(*operands):
    grads = pl.BlockSpec((OWN, WIDE), lambda g: (0, g))
    return pl.pallas_call(
        halo_queries_kernel,
        grid=(GROUPS,),
        in_specs=[keys_wide] + [edge_wide] * 2 + [stats_wide] * 4 + [halo_wide] * 4,
        out_specs=[grads] * 2,
        out_shape=[struct((OWN, FEAT), BF16)] * 2,
        compiler_params=params(),
        cost_estimate=cost(2e9, 3 << 20),
        name="halo_queries",
    )(*operands)


def row_gradients(place, t, side_a, side_b, q_a, q_b, kd, edge_a, edge_b, send_a, send_b, recv_a, recv_b,
                  s_own, d_own, s_halo, d_halo, dq_ref):
    at = at_tokens(t)
    masks, wide_masks = head_masks(PAIR), head_masks(WIDE)
    lane = lax.broadcasted_iota(jnp.int32, (1, PAIR), 1)
    key_parts, value_parts = [], []
    for j in range(2):
        lanes = slice(j * PAIR, (j + 1) * PAIR)
        queries = stacked([side_a[0, at, lanes], side_b[0, at, lanes]], masks)
        grads = stacked([side_a[1, at, lanes], side_b[1, at, lanes]], masks)
        both = [from_both(send_a, recv_a, j, 0, t), from_both(send_b, recv_b, j, 0, t)]
        probs = jnp.exp2(s_own[j, place] - jnp.concatenate([one[0] for one in both], axis=1))
        delta = jnp.concatenate([one[1] for one in both], axis=1)
        dscores = (probs * (d_own[j, place] - delta)).astype(BF16)
        keys = window(kd, edge_a, edge_b, 0, t, lanes)
        for c in range(2):
            dq_ref[c, at, lanes] = query_part(keys, dscores[:, c * PAIR:(c + 1) * PAIR], lane)
        key_parts.append(matmul(dscores, queries, (1, 0)))
        value_parts.append(matmul(probs.astype(BF16), grads, (1, 0)))
    sums = [jnp.concatenate(key_parts, axis=1), jnp.concatenate(value_parts, axis=1)]
    halo = []
    for c, (q_in, mine, theirs) in enumerate(((q_a, send_a, recv_a), (q_b, send_b, recv_b))):
        probs, dscores = halo_weights(mine, theirs, s_halo, d_halo, place, c, t)
        halo.append((matmul(dscores, stacked([q_in[0, at]], wide_masks), (1, 0)),
                     matmul(probs, stacked([q_in[1, at]], wide_masks), (1, 0))))
    return [jnp.concatenate([sums[which][(2 * i + c) * CELLS:(2 * i + c + 1) * CELLS]
                             + halo[c][which][i * CELLS:(i + 1) * CELLS] for i in range(3) for c in range(2)], axis=0)
            for which in range(2)]


OPERANDS = 15


def edge_kernel(*refs):
    operands, (_, dq_ref, dk_ref, dv_ref, out_a, out_b) = refs[:OPERANDS], refs[OPERANDS:]
    for place, t in enumerate(EDGE_ROWS):
        parts = row_gradients(place, t, *operands, dq_ref)
        for which, (out, scale) in enumerate(((dk_ref, SCALE), (dv_ref, 1.0))):
            part = parts[which] * scale
            if t == 0:
                out_a[which] = part[:PAIR].astype(BF16)
                out[0:2 * PAIR] = part[PAIR:]
            else:
                out_b[which] = part[2 * PAIR:].astype(BF16)
                out[2 * PAIR:] = part[:2 * PAIR]


def mid_kernel(*refs):
    operands, (dq_in, dk_in, dv_in, dq_ref, dk_ref, dv_ref) = refs[:OPERANDS], refs[OPERANDS:]
    upper, lower = [row_gradients(place, t, *operands, dq_ref) for place, t in enumerate(MID_ROWS)]
    for t in EDGE_ROWS:
        for c in range(2):
            dq_ref[c, at_tokens(t)] = dq_in[c, at_tokens(t)]
    for which, (sums, out, scale) in enumerate(((dk_in, dk_ref, SCALE), (dv_in, dv_ref, 1.0))):
        out[0:PAIR] = sums[0:PAIR] + upper[which][:PAIR] * scale
        out[PAIR:3 * PAIR] = sums[PAIR:3 * PAIR] + (upper[which][PAIR:] + lower[which][:2 * PAIR]) * scale
        out[3 * PAIR:] = sums[3 * PAIR:] + lower[which][2 * PAIR:] * scale


ROW_SPECS = [tokens_wide] * 4 + [keys_wide] + [edge_wide] * 2 + [stats_wide] * 4 + [held_wide] * 2 + [halo_wide] * 2
GRAD_SPECS = [tokens_wide] + [keys_wide] * 2
GRAD_SHAPES = [struct((2, OWN, FEAT), F32)] + [struct((ROWS * PAIR, FEAT), F32)] * 2


def edge_gradients(*operands):
    return pl.pallas_call(
        edge_kernel,
        grid=(GROUPS,),
        in_specs=ROW_SPECS + [pl.BlockSpec(memory_space=pl.ANY)],
        out_specs=GRAD_SPECS + [edge_wide] * 2,
        out_shape=GRAD_SHAPES + [struct((2, PAIR, FEAT), BF16)] * 2,
        compiler_params=params(),
        cost_estimate=cost(3e9, 1 << 10),
        name="edge_gradients",
    )(*operands)


def mid_gradients(*operands):
    return pl.pallas_call(
        mid_kernel,
        grid=(GROUPS,),
        in_specs=ROW_SPECS + GRAD_SPECS,
        out_specs=GRAD_SPECS,
        out_shape=GRAD_SHAPES,
        compiler_params=params(),
        cost_estimate=cost(3e9, 1 << 10),
        name="mid_gradients",
    )(*operands)


def join_columns(side_a, side_b):
    parts = ordered(side_a, side_b)
    return jnp.concatenate([part.reshape(8, 8, FEAT) for part in parts], axis=1).astype(BF16)


def finish_kernel(dq, dk, dv, dq_a, dq_b, from_a, from_b, q_ref, k_ref, v_ref, buffers, sems):
    copies = []
    for t in range(ROWS):
        at = at_tokens(t)
        buffers[0, t] = join_columns(dq[0, at] + dq_a[at].astype(F32), dq[1, at] + dq_b[at].astype(F32))
        for which, own in enumerate((dk, dv)):
            full = own[t * PAIR:(t + 1) * PAIR]
            if t == 0:
                full = full + from_a[which].astype(F32)
            if t == ROWS - 1:
                full = full + from_b[which].astype(F32)
            buffers[1 + which, t] = join_columns(full[:CELLS], full[CELLS:])
        for i, out in enumerate((q_ref, k_ref, v_ref)):
            copies.append(pltpu.make_async_copy(buffers.at[i, t], out.at[pl.ds(8 * grid_row(t), 8)], sems.at[i, t]))
            copies[-1].start()
    for copy in copies:
        copy.wait()


def finish(*operands):
    return pl.pallas_call(
        finish_kernel,
        out_specs=[pl.BlockSpec(memory_space=pl.ANY)] * 3,
        out_shape=[struct((8 * ROWS, 16, FEAT), BF16)] * 3,
        scratch_shapes=[pltpu.VMEM((3, ROWS, 8, 16, FEAT), BF16), pltpu.SemaphoreType.DMA((3, ROWS))],
        compiler_params=params(),
        cost_estimate=cost(0, 6 << 20),
        name="finish",
    )(*operands)


def swap_a(x, axis):
    return lax.ppermute(x, axis, [(i, i ^ 1) for i in range(lax.axis_size(axis))])


def swap_b(x, axis, wrap):
    count = lax.axis_size(axis)
    pairs = []
    for i in range(1, count if wrap else count - 1, 2):
        pairs += [(i, (i + 1) % count), ((i + 1) % count, i)]
    return lax.ppermute(x, axis, pairs)


def over_lon(side_a, side_b):
    return swap_a(side_a, "lon"), swap_b(side_b, "lon", True)


def over_lat(side_a, side_b):
    return swap_a(side_a, "lat"), swap_b(side_b, "lat", False)


def on_device(query_vectors, key_vectors, value_vectors, output_grads):
    tokens = struct((2, OWN, FEAT), BF16)
    tiles = struct((ROWS * PAIR, FEAT), BF16)
    edge = struct((2, PAIR, FEAT), BF16)
    sides = pack(pack_queries_kernel, query_vectors, output_grads, [tokens] * 2, "pack_queries", PACK_LIMIT)
    kd, vd, own_edge_a, own_edge_b = pack(pack_keys_kernel, key_vectors, value_vectors,
                                          [tiles] * 2 + [edge] * 2, "pack_keys", VMEM_LIMIT)
    halos = over_lon(*sides)
    edges = over_lat(own_edge_a, own_edge_b)
    part_mid, *own_mid = scores_call(mid_scores_kernel, (*sides, kd, vd), "mid_scores")
    part_edge, *own_edge = scores_call(edge_scores_kernel, (*sides, kd, vd, *edges), "edge_scores")
    send_a, send_b, *held = halo_scores(*halos, kd, vd, *edges, part_edge, part_mid)
    stats = (send_a, send_b, *over_lon(send_a, send_b))
    halo_dq = halo_queries(kd, *edges, *stats, *held)
    dq_parts = over_lon(*halo_dq)
    shared = (*sides, *halos, kd, *edges, *stats)
    dq, dk, dv, out_a, out_b = edge_gradients(*shared, *own_edge, *held[:2], halo_dq[0])
    key_parts = over_lat(out_a, out_b)
    dq, dk, dv = mid_gradients(*shared, *own_mid, *held[2:], dq, dk, dv)
    return tuple(finish(dq, dk, dv, *dq_parts, *key_parts))


def solution(mesh):
    spec = P("lat", "lon", None)
    return jax.shard_map(on_device, mesh=mesh, in_specs=(spec,) * 4, out_specs=(spec,) * 3, check_vma=False)
```

```python
import functools

import jax
import jax.numpy as jnp
from jax import lax
from jax.experimental import pallas as pl
from jax.experimental.pallas import tpu as pltpu
from jax.sharding import PartitionSpec as P

ROWS = 4
CELLS = 64
CHUNK = 2 * CELLS
PAIR = 128
WIDE = 256
PAIRS = 4
GROUPS = 2
FEAT = 512
SCALE = 64 ** -0.5
LOG2E = 1.4426950408889634
MASKED = -1e30
F32 = jnp.float32
BF16 = jnp.bfloat16
VMEM_LIMIT = 20 * 1024 * 1024
PACK_LIMIT = 62 * 1024 * 1024
EDGE_ROWS = (0, 3)
MID_ROWS = (1, 2)


def matmul(a, b, contract):
    return lax.dot_general(a, b, ((contract[:1], contract[1:]), ((), ())), preferred_element_type=F32)


def params(limit=VMEM_LIMIT):
    return pltpu.CompilerParams(vmem_limit_bytes=limit)


def cost(flops, size):
    return pl.CostEstimate(flops=int(flops), bytes_accessed=int(size), transcendentals=0)


def struct(shape, dtype):
    return jax.ShapeDtypeStruct(shape, dtype)


def grid_row(t):
    return jnp.where(lax.axis_index("lat") % 2 == 0, ROWS - 1 - t, t)


def ordered(first, second):
    swap = lax.axis_index("lon") % 2 == 0
    return jnp.where(swap, second, first), jnp.where(swap, first, second)


def split_columns(block):
    wide = block.astype(F32)
    parts = ordered(*[wide[:, c * 8:(c + 1) * 8].reshape(CELLS, FEAT) for c in range(2)])
    return [part.astype(BF16) for part in parts]


def fetch(refs, rows, buffers, sems):
    copies = [[pltpu.make_async_copy(ref.at[pl.ds(8 * grid_row(t), 8)], buffers.at[i, place], sems.at[i, place])
               for place, t in enumerate(rows)] for i, ref in enumerate(refs)]
    for place in range(len(rows)):
        for copy in copies:
            copy[place].start()
    return copies


def pack_queries_kernel(rows, q_ref, g_ref, *refs):
    side_a, side_b, buffers, sems = refs[-4:]
    copies = fetch((q_ref, g_ref), rows, buffers, sems)
    for place in range(2):
        for i in range(2):
            copies[i][place].wait()
            side_a[i, at_tokens(place)], side_b[i, at_tokens(place)] = split_columns(buffers[i, place])


def pack_keys_kernel(rows, k_ref, v_ref, _, kd, vd, edge_a, edge_b, buffers, sems):
    copies = fetch((k_ref, v_ref), rows, buffers, sems)
    for t in rows:
        for i, out in enumerate((kd, vd)):
            copies[i][t].wait()
            tile = jnp.concatenate(split_columns(buffers[i, t]), axis=0)
            out[t * PAIR:(t + 1) * PAIR] = tile
            if t == 0:
                edge_a[i] = tile
            if t == ROWS - 1:
                edge_b[i] = tile


def pack(kernel, rows, operands, out_shape, name, limit):
    return pl.pallas_call(
        functools.partial(kernel, rows),
        in_specs=[pl.BlockSpec(memory_space=pl.ANY)] * len(operands),
        out_shape=out_shape,
        scratch_shapes=[pltpu.VMEM((2, len(rows), 8, 16, FEAT), BF16), pltpu.SemaphoreType.DMA((2, len(rows)))],
        compiler_params=params(limit),
        cost_estimate=cost(0, 0),
        name=name,
    )(*operands)


def head_masks(lanes):
    lane = lax.broadcasted_iota(jnp.int32, (1, lanes), 1)
    return [jnp.where((lane >= 64 * h) & (lane < 64 * (h + 1)), 1.0, 0.0).astype(F32).astype(BF16)
            for h in range(lanes // 64)]


def stacked(parts, masks):
    return jnp.concatenate([part * mask for part in parts for mask in masks], axis=0)


def key_rows(own, edges, which, t, lanes=slice(None)):
    rows = []
    for row in range(t, t + 3):
        if row == 0:
            rows.append(edges[0][which, :, lanes])
        elif row == ROWS + 1:
            rows.append(edges[1][which, :, lanes])
        else:
            rows.append(own[(row - 1) * PAIR:row * PAIR, lanes])
    return rows


def window(*where):
    return jnp.concatenate(key_rows(*where), axis=0)


def column_window(column, *where):
    return jnp.concatenate([row[column * CELLS:(column + 1) * CELLS] for row in key_rows(*where)], axis=0)


def score_block(keys, queries, t):
    scores = matmul(keys, queries, (1, 1)) * (SCALE * LOG2E)
    if t == ROWS - 1:
        lat = lax.axis_index("lat")
        outside = (lat == 0) | (lat == lax.axis_size("lat") - 1)
        cut = 2 * (keys.shape[0] // 3)
        bias = jnp.where(outside, MASKED, 0.0).astype(F32)
        scores = jnp.concatenate([scores[:cut], scores[cut:] + bias], axis=0)
    return scores


def row_stats(scores, dprobs):
    top = jnp.max(scores, axis=0, keepdims=True)
    weights = jnp.exp2(scores - top)
    total = jnp.sum(weights, axis=0, keepdims=True)
    delta = jnp.sum(weights * dprobs, axis=0, keepdims=True) / total
    return top + jnp.log(total) * LOG2E, delta


def merged(log_a, delta_a, log_b, delta_b):
    top = jnp.maximum(log_a, log_b)
    weight_a = jnp.exp2(log_a - top)
    weight_b = jnp.exp2(log_b - top)
    total = weight_a + weight_b
    return top + jnp.log(total) * LOG2E, (weight_a * delta_a + weight_b * delta_b) / total


def both_parts(mine, theirs, pair, base):
    other = 4 - base
    return merged(mine[pair, base:base + 2], mine[pair, base + 2:base + 4],
                  theirs[pair, other:other + 2], theirs[pair, other + 2:other + 4])


def turned_window(own_turned, edges_turned, t, j):
    at = slice(j * PAIR, (j + 1) * PAIR)
    rows = []
    for row in range(t, t + 3):
        if row in (0, ROWS + 1):
            rows.append(edges_turned[row // (ROWS + 1), at])
        else:
            rows.append(own_turned[at, (row - 1) * PAIR:row * PAIR])
    return jnp.concatenate(rows, axis=1)


def query_parts(keys_turned, dscores, lane):
    turned = matmul(keys_turned, dscores, (1, 0)) * SCALE
    parts = [turned[:, c * PAIR:(c + 1) * PAIR].T for c in range(2)]
    return [jnp.where(lane < 64, part[:CELLS], part[CELLS:]) for part in parts]


def at_tokens(place):
    return slice(place * CELLS, (place + 1) * CELLS)


def pair_lanes(j):
    return slice(j * PAIR, (j + 1) * PAIR)


tokens_spec = pl.BlockSpec((2, CHUNK, PAIR), lambda p: (0, 0, p))
keys_spec = pl.BlockSpec((ROWS * PAIR, PAIR), lambda p: (0, p))
edge_spec = pl.BlockSpec((2, PAIR, PAIR), lambda p: (0, 0, p))
stats_spec = pl.BlockSpec((1, 8, PAIR), lambda p: (p, 0, 0))
held_spec = pl.BlockSpec((1, 2, 3 * PAIR, WIDE), lambda p: (p, 0, 0, 0))
stats_shape = struct((PAIRS, 8, PAIR), F32)
held_shape = struct((PAIRS, 2, 3 * PAIR, WIDE), F32)

tokens_wide = pl.BlockSpec((2, CHUNK, WIDE), lambda g: (0, 0, g))
part_wide = pl.BlockSpec((CHUNK, WIDE), lambda g: (0, g))
keys_wide = pl.BlockSpec((ROWS * PAIR, WIDE), lambda g: (0, g))
edge_wide = pl.BlockSpec((2, PAIR, WIDE), lambda g: (0, 0, g))
turned_wide = pl.BlockSpec((WIDE, ROWS * PAIR), lambda g: (g, 0))
edge_turned_wide = pl.BlockSpec((2, WIDE, PAIR), lambda g: (0, g, 0))
stats_wide = pl.BlockSpec((2, 8, PAIR), lambda g: (g, 0, 0))
held_wide = pl.BlockSpec((2, 2, 3 * PAIR, WIDE), lambda g: (g, 0, 0, 0))
halo_wide = pl.BlockSpec((1, 2, 2, 3 * CELLS, WIDE), lambda g: (g, 0, 0, 0, 0))
halo_shape = struct((GROUPS, 2, 2, 3 * CELLS, WIDE), F32)
any_spec = pl.BlockSpec(memory_space=pl.ANY)


def own_scores(rows, side_a, side_b, kd, vd, edges, part, s_out, d_out):
    masks = head_masks(PAIR)
    for place, t in enumerate(rows):
        at = at_tokens(place)
        queries = stacked([side_a[0, at], side_b[0, at]], masks)
        grads = stacked([side_a[1, at], side_b[1, at]], masks)
        scores = score_block(window(kd, edges, 0, t), queries, t)
        dprobs = matmul(window(vd, edges, 1, t), grads, (1, 1))
        s_out[0, place] = scores
        d_out[0, place] = dprobs
        for w, values in enumerate(row_stats(scores, dprobs)):
            for c in range(2):
                index = 4 * c + 2 * w + place
                part[0, index:index + 1] = values[:, pair_lanes(c)]


def mid_scores_kernel(side_a, side_b, kd, vd, part, s_out, d_out, turned):
    own_scores(MID_ROWS, side_a, side_b, kd, vd, None, part, s_out, d_out)
    turned[...] = kd[...].T


def edge_scores_kernel(side_a, side_b, kd, vd, edge_a, edge_b, part, s_out, d_out, turned):
    own_scores(EDGE_ROWS, side_a, side_b, kd, vd, (edge_a, edge_b), part, s_out, d_out)
    turned[0] = edge_a[0].T
    turned[1] = edge_b[0].T


def scores_call(kernel, operands, turned_spec, turned_shape, name):
    return pl.pallas_call(
        kernel,
        grid=(PAIRS,),
        in_specs=[tokens_spec] * 2 + [keys_spec] * 2 + [edge_spec] * (len(operands) - 4),
        out_specs=[stats_spec] + [held_spec] * 2 + [turned_spec],
        out_shape=[stats_shape] + [held_shape] * 2 + [struct(turned_shape, BF16)],
        compiler_params=params(),
        cost_estimate=cost(0, 0),
        name=name,
    )(*operands)


def mid_scores(*operands):
    spec = pl.BlockSpec((PAIR, ROWS * PAIR), lambda p: (p, 0))
    return scores_call(mid_scores_kernel, operands, spec, (FEAT, ROWS * PAIR), "mid_scores")


def edge_scores(*operands):
    spec = pl.BlockSpec((2, PAIR, PAIR), lambda p: (0, p, 0))
    return scores_call(edge_scores_kernel, operands, spec, (2, FEAT, PAIR), "edge_scores")


def halo_scores_kernel(rows, *refs):
    q_a, q_b, kd, vd, part, _, *edges = refs[:-4]
    send_a, send_b, s_out, d_out = refs[-4:]
    masks = head_masks(WIDE)
    for c, (q_in, send) in enumerate(((q_a, send_a), (q_b, send_b))):
        for j in range(2):
            send[j, 0:4] = part[j, 4 * c:4 * c + 4]
        for place, t in enumerate(rows):
            at = at_tokens(place)
            queries = stacked([q_in[0, at]], masks)
            grads = stacked([q_in[1, at]], masks)
            scores = score_block(column_window(c, kd, edges, 0, t), queries, t)
            dprobs = matmul(column_window(c, vd, edges, 1, t), grads, (1, 1))
            s_out[0, place, c] = scores
            d_out[0, place, c] = dprobs
            for w, values in enumerate(row_stats(scores, dprobs)):
                index = 4 + 2 * w + place
                for j in range(2):
                    send[j, index:index + 1] = values[:, pair_lanes(j)]


def halo_scores(rows, halos, kd, vd, part, edges, before, name):
    return pl.pallas_call(
        functools.partial(halo_scores_kernel, rows),
        grid=(GROUPS,),
        in_specs=[tokens_wide] * 2 + [keys_wide] * 2 + [stats_wide, any_spec] + [edge_wide] * len(edges),
        out_specs=[stats_wide] * 2 + [halo_wide] * 2,
        out_shape=[stats_shape] * 2 + [halo_shape] * 2,
        compiler_params=params(),
        cost_estimate=cost(0, 0),
        name=name,
    )(*halos, kd, vd, part, before, *edges)


def halo_weights(mine, theirs, s_in, d_in, c):
    both = [both_parts(mine, theirs, j, 4) for j in range(2)]
    log_total = jnp.concatenate([one[0] for one in both], axis=1)
    delta = jnp.concatenate([one[1] for one in both], axis=1)
    weights = []
    for place in range(2):
        probs = jnp.exp2(s_in[0, place, c] - log_total[place:place + 1])
        dscores = probs * (d_in[0, place, c] - delta[place:place + 1])
        weights.append((probs.astype(BF16), dscores.astype(BF16)))
    return weights


def halo_queries_kernel(rows, *refs):
    send_a, send_b, recv_a, recv_b, s_in, d_in, own_turned, *edges_turned = refs[:-2]
    outs = refs[-2:]
    lane = lax.broadcasted_iota(jnp.int32, (1, PAIR), 1)
    weights = [halo_weights(mine, theirs, s_in, d_in, c)
               for c, (mine, theirs) in enumerate(((send_a, recv_a), (send_b, recv_b)))]
    none = jnp.zeros((CELLS, PAIR), BF16)
    for place, t in enumerate(rows):
        for j in range(2):
            pieces = []
            for i in range(3):
                part_a, part_b = [weights[c][place][1][at_tokens(i), pair_lanes(j)] for c in range(2)]
                pieces += [jnp.concatenate([part_a, none], axis=1), jnp.concatenate([none, part_b], axis=1)]
            keys_turned = turned_window(own_turned, edges_turned[0] if edges_turned else None, t, j)
            for out, part in zip(outs, query_parts(keys_turned, jnp.concatenate(pieces, axis=0), lane)):
                out[at_tokens(place), pair_lanes(j)] = part.astype(BF16)


def halo_queries(rows, stats, held, turned, name):
    return pl.pallas_call(
        functools.partial(halo_queries_kernel, rows),
        grid=(GROUPS,),
        in_specs=[stats_wide] * 4 + [halo_wide] * 2 + [turned_wide] + [edge_turned_wide] * (len(turned) - 1),
        out_specs=[part_wide] * 2,
        out_shape=[struct((CHUNK, FEAT), BF16)] * 2,
        compiler_params=params(),
        cost_estimate=cost(0, 0),
        name=name,
    )(*stats, *held, *turned)


def row_gradients(rows, side_a, side_b, q_a, q_b, send_a, send_b, recv_a, recv_b, s_own, d_own, s_halo, d_halo,
                  own_turned, edges_turned, dq_ref):
    masks, wide_masks = head_masks(PAIR), head_masks(WIDE)
    lane = lax.broadcasted_iota(jnp.int32, (1, PAIR), 1)
    sides = ((q_a, send_a, recv_a), (q_b, send_b, recv_b))
    halo = [halo_weights(mine, theirs, s_halo, d_halo, c) for c, (_, mine, theirs) in enumerate(sides)]
    merged_rows = []
    for j in range(2):
        both = [both_parts(mine, theirs, j, 0) for _, mine, theirs in sides]
        merged_rows.append([jnp.concatenate([one[w] for one in both], axis=1) for w in range(2)])
    results = []
    for place, t in enumerate(rows):
        at, row = at_tokens(place), slice(place, place + 1)
        sums = [[], []]
        for j in range(2):
            lanes = pair_lanes(j)
            queries = stacked([side_a[0, at, lanes], side_b[0, at, lanes]], masks)
            grads = stacked([side_a[1, at, lanes], side_b[1, at, lanes]], masks)
            log_total, delta = merged_rows[j]
            probs = jnp.exp2(s_own[j, place] - log_total[row])
            dscores = (probs * (d_own[j, place] - delta[row])).astype(BF16)
            for c, part in enumerate(query_parts(turned_window(own_turned, edges_turned, t, j), dscores, lane)):
                dq_ref[c, at, lanes] = part
            sums[0].append(matmul(dscores, queries, (1, 0)))
            sums[1].append(matmul(probs.astype(BF16), grads, (1, 0)))
        sums = [jnp.concatenate(parts, axis=1) for parts in sums]
        edge_parts = []
        for c in range(2):
            probs, dscores = halo[c][place]
            edge_parts.append((matmul(dscores, stacked([sides[c][0][0, at]], wide_masks), (1, 0)),
                               matmul(probs, stacked([sides[c][0][1, at]], wide_masks), (1, 0))))
        results.append([jnp.concatenate([sums[w][at_tokens(2 * i + c)] + edge_parts[c][w][at_tokens(i)]
                                         for i in range(3) for c in range(2)], axis=0) for w in range(2)])
    return results


def edge_kernel(*refs):
    operands, (_, dq_ref, dk_ref, dv_ref, out_a, out_b) = refs[:14], refs[14:]
    upper, lower = row_gradients(EDGE_ROWS, *operands, dq_ref)
    for which, (out, scale) in enumerate(((dk_ref, SCALE), (dv_ref, 1.0))):
        top, bottom = upper[which] * scale, lower[which] * scale
        out_a[which] = top[:PAIR].astype(BF16)
        out[0:2 * PAIR] = top[PAIR:]
        out_b[which] = bottom[2 * PAIR:].astype(BF16)
        out[2 * PAIR:] = bottom[:2 * PAIR]


def mid_kernel(*refs):
    operands, (_, dk_in, dv_in, dq_ref, dk_ref, dv_ref) = refs[:13], refs[13:]
    upper, lower = row_gradients(MID_ROWS, *operands, None, dq_ref)
    for which, (sums, out, scale) in enumerate(((dk_in, dk_ref, SCALE), (dv_in, dv_ref, 1.0))):
        out[0:PAIR] = sums[0:PAIR] + upper[which][:PAIR] * scale
        out[PAIR:3 * PAIR] = sums[PAIR:3 * PAIR] + (upper[which][PAIR:] + lower[which][:2 * PAIR]) * scale
        out[3 * PAIR:] = sums[3 * PAIR:] + lower[which][2 * PAIR:] * scale


ROW_SPECS = [tokens_wide] * 4 + [stats_wide] * 4 + [held_wide] * 2 + [halo_wide] * 2 + [turned_wide]
GRAD_SPECS = [tokens_wide] + [keys_wide] * 2
GRAD_SHAPES = [struct((2, CHUNK, FEAT), F32)] + [struct((ROWS * PAIR, FEAT), F32)] * 2


def edge_gradients(*operands):
    return pl.pallas_call(
        edge_kernel,
        grid=(GROUPS,),
        in_specs=ROW_SPECS + [edge_turned_wide, any_spec],
        out_specs=GRAD_SPECS + [edge_wide] * 2,
        out_shape=GRAD_SHAPES + [struct((2, PAIR, FEAT), BF16)] * 2,
        compiler_params=params(),
        cost_estimate=cost(0, 0),
        name="edge_gradients",
    )(*operands)


def mid_gradients(*operands):
    return pl.pallas_call(
        mid_kernel,
        grid=(GROUPS,),
        in_specs=ROW_SPECS + [any_spec] + [keys_wide] * 2,
        out_specs=GRAD_SPECS,
        out_shape=GRAD_SHAPES,
        compiler_params=params(),
        cost_estimate=cost(0, 0),
        name="mid_gradients",
    )(*operands)


def join_columns(side_a, side_b):
    parts = ordered(side_a, side_b)
    return jnp.concatenate([part.reshape(8, 8, FEAT) for part in parts], axis=1).astype(BF16)


def finish_kernel(dq_edge, dq_mid, dk, dv, edge_dq_a, edge_dq_b, mid_dq_a, mid_dq_b, from_a, from_b,
                  q_ref, k_ref, v_ref, buffers, sems):
    copies = []

    def send(i, t, value):
        buffers[i, t] = value
        out = (q_ref, k_ref, v_ref)[i]
        copies.append(pltpu.make_async_copy(buffers.at[i, t], out.at[pl.ds(8 * grid_row(t), 8)], sems.at[i, t]))
        copies[-1].start()

    for t in range(ROWS):
        for which, own in enumerate((dk, dv)):
            full = own[t * PAIR:(t + 1) * PAIR]
            if t == 0:
                full = full + from_a[which].astype(F32)
            if t == ROWS - 1:
                full = full + from_b[which].astype(F32)
            send(1 + which, t, join_columns(full[:CELLS], full[CELLS:]))
    for rows, dq, side_a, side_b in ((EDGE_ROWS, dq_edge, edge_dq_a, edge_dq_b), (MID_ROWS, dq_mid, mid_dq_a, mid_dq_b)):
        for place, t in enumerate(rows):
            at = at_tokens(place)
            send(0, t, join_columns(dq[0, at] + side_a[at].astype(F32), dq[1, at] + side_b[at].astype(F32)))
    for copy in copies:
        copy.wait()


def finish(*operands):
    return pl.pallas_call(
        finish_kernel,
        out_specs=[any_spec] * 3,
        out_shape=[struct((8 * ROWS, 16, FEAT), BF16)] * 3,
        scratch_shapes=[pltpu.VMEM((3, ROWS, 8, 16, FEAT), BF16), pltpu.SemaphoreType.DMA((3, ROWS))],
        compiler_params=params(),
        cost_estimate=cost(0, 0),
        name="finish",
    )(*operands)


def swap_a(x, axis):
    return lax.ppermute(x, axis, [(i, i ^ 1) for i in range(lax.axis_size(axis))])


def swap_b(x, axis, wrap):
    count = lax.axis_size(axis)
    pairs = []
    for i in range(1, count if wrap else count - 1, 2):
        pairs += [(i, (i + 1) % count), ((i + 1) % count, i)]
    return lax.ppermute(x, axis, pairs)


def over_lon(side_a, side_b):
    from_b = swap_b(side_b, "lon", True)
    return swap_a(side_a, "lon"), from_b


def over_lat(side_a, side_b):
    from_b = swap_b(side_b, "lat", False)
    return swap_a(side_a, "lat"), from_b


def on_device(query_vectors, key_vectors, value_vectors, output_grads):
    tokens = struct((2, CHUNK, FEAT), BF16)
    tiles = struct((ROWS * PAIR, FEAT), BF16)
    edge = struct((2, PAIR, FEAT), BF16)
    sides = pack(pack_queries_kernel, EDGE_ROWS, (query_vectors, output_grads), [tokens] * 2, "pack_edge", PACK_LIMIT)
    kd, vd, own_edge_a, own_edge_b = pack(pack_keys_kernel, range(ROWS), (key_vectors, value_vectors, sides[0]),
                                          [tiles] * 2 + [edge] * 2, "pack_keys", VMEM_LIMIT)
    mid_sides = pack(pack_queries_kernel, MID_ROWS, (query_vectors, output_grads, own_edge_a),
                     [tokens] * 2, "pack_mid", VMEM_LIMIT)
    halos = over_lon(*sides)
    edges = over_lat(own_edge_a, own_edge_b)
    mid_halos = over_lon(*mid_sides)

    mid_part, *mid_own, turned = mid_scores(*mid_sides, kd, vd)
    part, *own, edges_turned = edge_scores(*sides, kd, vd, *edges)
    send_a, send_b, *held = halo_scores(EDGE_ROWS, halos, kd, vd, part, edges, mid_part, "edge_halo_scores")
    stats = (send_a, send_b, *over_lon(send_a, send_b))
    halo_dq = halo_queries(EDGE_ROWS, stats, held, (turned, edges_turned), "edge_halo_queries")
    dq_parts = over_lon(*halo_dq)
    dq, dk, dv, out_a, out_b = edge_gradients(*sides, *halos, *stats, *own, *held, turned, edges_turned, halo_dq[0])
    key_parts = over_lat(out_a, out_b)

    send_a, send_b, *held = halo_scores(MID_ROWS, mid_halos, kd, vd, mid_part, (), out_a, "mid_halo_scores")
    stats = (send_a, send_b, *over_lon(send_a, send_b))
    halo_dq = halo_queries(MID_ROWS, stats, held, (turned,), "mid_halo_queries")
    mid_dq_parts = over_lon(*halo_dq)
    mid_dq, dk, dv = mid_gradients(*mid_sides, *mid_halos, *stats, *mid_own, *held, turned, halo_dq[0], dk, dv)
    return tuple(finish(dq, mid_dq, dk, dv, *dq_parts, *mid_dq_parts, *key_parts))


def solution(mesh):
    spec = P("lat", "lon", None)
    return jax.shard_map(on_device, mesh=mesh, in_specs=(spec,) * 4, out_specs=(spec,) * 3, check_vma=False)
```

```python
import functools

import jax
import jax.numpy as jnp
from jax import lax
from jax.experimental import pallas as pl
from jax.experimental.pallas import tpu as pltpu
from jax.sharding import PartitionSpec as P

ROWS = 4
CELLS = 64
CHUNK = 2 * CELLS
PAIR = 128
WIDE = 256
PAIRS = 4
GROUPS = 2
FEAT = 512
SCALE = 64 ** -0.5
LOG2E = 1.4426950408889634
MASKED = -1e30
F32 = jnp.float32
BF16 = jnp.bfloat16
VMEM_LIMIT = 20 * 1024 * 1024
PACK_LIMIT = 62 * 1024 * 1024
EDGE_ROWS = (0, 3)
MID_ROWS = (1, 2)
ORDER = EDGE_ROWS + MID_ROWS
EDGE, MID = 0, 1


def matmul(a, b, contract):
    return lax.dot_general(a, b, ((contract[:1], contract[1:]), ((), ())), preferred_element_type=F32)


def params(limit=VMEM_LIMIT):
    return pltpu.CompilerParams(vmem_limit_bytes=limit)


def cost(flops, size):
    return pl.CostEstimate(flops=int(flops), bytes_accessed=int(size), transcendentals=0)


def struct(shape, dtype):
    return jax.ShapeDtypeStruct(shape, dtype)


def grid_row(t):
    return jnp.where(lax.axis_index("lat") % 2 == 0, ROWS - 1 - t, t)


def ordered(first, second):
    swap = lax.axis_index("lon") % 2 == 1
    return jnp.where(swap, second, first), jnp.where(swap, first, second)


def split_columns(block):
    wide = block.astype(F32)
    parts = ordered(*[wide[:, c * 8:(c + 1) * 8].reshape(CELLS, FEAT) for c in range(2)])
    return [part.astype(BF16) for part in parts]


def fetch(refs, rows, buffers, sems):
    copies = [[pltpu.make_async_copy(ref.at[pl.ds(8 * grid_row(t), 8)], buffers.at[i, place], sems.at[i, place])
               for place, t in enumerate(rows)] for i, ref in enumerate(refs)]
    for place in range(len(rows)):
        for copy in copies:
            copy[place].start()
    return copies


def pack_queries_kernel(q_ref, g_ref, side_0, side_1, buffers, sems, packed, out_sems):
    copies = fetch((q_ref, g_ref), ORDER, buffers, sems)
    sends = []
    for place in range(ROWS):
        for i in range(2):
            copies[i][place].wait()
            for side, (value, out) in enumerate(zip(split_columns(buffers[i, place]), (side_0, side_1))):
                packed[side, i, place] = value
                sends.append(pltpu.make_async_copy(packed.at[side, i, place],
                                                   out.at[i, pl.ds(place * CELLS, CELLS)], out_sems.at[side, i, place]))
                sends[-1].start()
    for send in sends:
        send.wait()


def pack_queries(*operands):
    return pl.pallas_call(
        pack_queries_kernel,
        in_specs=[pl.BlockSpec(memory_space=pl.ANY)] * 2,
        out_specs=[pl.BlockSpec(memory_space=pl.ANY)] * 2,
        out_shape=[struct((2, ROWS * CELLS, FEAT), BF16)] * 2,
        scratch_shapes=[
            pltpu.VMEM((2, ROWS, 8, 16, FEAT), BF16), pltpu.SemaphoreType.DMA((2, ROWS)),
            pltpu.VMEM((2, 2, ROWS, CELLS, FEAT), BF16), pltpu.SemaphoreType.DMA((2, 2, ROWS)),
        ],
        compiler_params=params(PACK_LIMIT),
        cost_estimate=cost(0, 3 << 20),
        name="pack_queries",
    )(*operands)


def pack_keys_kernel(k_ref, v_ref, kd, vd, edge_a, edge_b, buffers, sems):
    copies = fetch((k_ref, v_ref), range(ROWS), buffers, sems)
    for t in range(ROWS):
        for i, out in enumerate((kd, vd)):
            copies[i][t].wait()
            tile = jnp.concatenate(split_columns(buffers[i, t]), axis=0)
            out[t * PAIR:(t + 1) * PAIR] = tile
            if t == 0:
                edge_a[i] = tile
            if t == ROWS - 1:
                edge_b[i] = tile


def pack_keys(*operands):
    return pl.pallas_call(
        pack_keys_kernel,
        in_specs=[pl.BlockSpec(memory_space=pl.ANY)] * 2,
        out_shape=[struct((ROWS * PAIR, FEAT), BF16)] * 2 + [struct((2, PAIR, FEAT), BF16)] * 2,
        scratch_shapes=[pltpu.VMEM((2, ROWS, 8, 16, FEAT), BF16), pltpu.SemaphoreType.DMA((2, ROWS))],
        compiler_params=params(),
        cost_estimate=cost(0, 3 << 20),
        name="pack_keys",
    )(*operands)


def head_masks(lanes):
    lane = lax.broadcasted_iota(jnp.int32, (1, lanes), 1)
    return [jnp.where((lane >= 64 * h) & (lane < 64 * (h + 1)), 1.0, 0.0).astype(F32).astype(BF16)
            for h in range(lanes // 64)]


def stacked(parts, masks):
    return jnp.concatenate([part * mask for part in parts for mask in masks], axis=0)


def key_rows(own, edges, which, t, lanes=slice(None)):
    rows = []
    for row in range(t, t + 3):
        if row == 0:
            rows.append(edges[0][which, :, lanes])
        elif row == ROWS + 1:
            rows.append(edges[1][which, :, lanes])
        else:
            rows.append(own[(row - 1) * PAIR:row * PAIR, lanes])
    return rows


def window(*where):
    return jnp.concatenate(key_rows(*where), axis=0)


def column_window(column, *where):
    return jnp.concatenate([row[column * CELLS:(column + 1) * CELLS] for row in key_rows(*where)], axis=0)


def score_block(keys, queries, t):
    scores = matmul(keys, queries, (1, 1)) * (SCALE * LOG2E)
    if t == ROWS - 1:
        lat = lax.axis_index("lat")
        outside = (lat == 0) | (lat == lax.axis_size("lat") - 1)
        cut = 2 * (keys.shape[0] // 3)
        bias = jnp.where(outside, MASKED, 0.0).astype(F32)
        scores = jnp.concatenate([scores[:cut], scores[cut:] + bias], axis=0)
    return scores


def row_stats(scores, dprobs):
    top = jnp.max(scores, axis=0, keepdims=True)
    weights = jnp.exp2(scores - top)
    total = jnp.sum(weights, axis=0, keepdims=True)
    delta = jnp.sum(weights * dprobs, axis=0, keepdims=True) / total
    return top + jnp.log(total) * LOG2E, delta


def merged(log_a, delta_a, log_b, delta_b):
    top = jnp.maximum(log_a, log_b)
    weight_a = jnp.exp2(log_a - top)
    weight_b = jnp.exp2(log_b - top)
    total = weight_a + weight_b
    return top + jnp.log(total) * LOG2E, (weight_a * delta_a + weight_b * delta_b) / total


def both_parts(mine, theirs, pair, base):
    other = 4 - base
    return merged(mine[pair, base:base + 2], mine[pair, base + 2:base + 4],
                  theirs[pair, other:other + 2], theirs[pair, other + 2:other + 4])


def turned_window(own_turned, edges_turned, t, j):
    at = slice(j * PAIR, (j + 1) * PAIR)
    rows = []
    for row in range(t, t + 3):
        if row in (0, ROWS + 1):
            rows.append(edges_turned[row // (ROWS + 1), at])
        else:
            rows.append(own_turned[at, (row - 1) * PAIR:row * PAIR])
    return jnp.concatenate(rows, axis=1)


def query_parts(keys_turned, dscores, lane):
    turned = matmul(keys_turned, dscores, (1, 0)) * SCALE
    parts = [turned[:, c * PAIR:(c + 1) * PAIR].T for c in range(2)]
    return [jnp.where(lane < 64, part[:CELLS], part[CELLS:]) for part in parts]


def at_tokens(place):
    return slice(place * CELLS, (place + 1) * CELLS)


def pair_lanes(j):
    return slice(j * PAIR, (j + 1) * PAIR)


def tokens_spec(group):
    return pl.BlockSpec((2, CHUNK, PAIR), lambda p: (0, group, p))


keys_spec = pl.BlockSpec((ROWS * PAIR, PAIR), lambda p: (0, p))
edge_spec = pl.BlockSpec((2, PAIR, PAIR), lambda p: (0, 0, p))
part_spec = pl.BlockSpec((1, 8, PAIR), lambda p: (p, 0, 0))
held_spec = pl.BlockSpec((1, 2, 3 * PAIR, WIDE), lambda p: (p, 0, 0, 0))
part_shape = struct((PAIRS, 8, PAIR), F32)
stats_shape = struct((PAIRS, 16, PAIR), F32)
held_shape = struct((PAIRS, 2, 3 * PAIR, WIDE), F32)


def tokens_wide(group):
    return pl.BlockSpec((2, CHUNK, WIDE), lambda g: (0, group, g))


def stats_wide(group):
    return pl.BlockSpec((2, 8, PAIR), lambda g: (g, group, 0))


all_tokens = pl.BlockSpec((2, 2 * CHUNK, WIDE), lambda g: (0, 0, g))
all_stats = pl.BlockSpec((2, 16, PAIR), lambda g: (g, 0, 0))
all_parts = pl.BlockSpec((2 * CHUNK, WIDE), lambda g: (0, g))
sums_wide = pl.BlockSpec((2, CHUNK, WIDE), lambda g: (0, 0, g))
keys_wide = pl.BlockSpec((ROWS * PAIR, WIDE), lambda g: (0, g))
edge_wide = pl.BlockSpec((2, PAIR, WIDE), lambda g: (0, 0, g))
turned_wide = pl.BlockSpec((WIDE, ROWS * PAIR), lambda g: (g, 0))
edge_turned_wide = pl.BlockSpec((2, WIDE, PAIR), lambda g: (0, g, 0))
held_wide = pl.BlockSpec((2, 2, 3 * PAIR, WIDE), lambda g: (g, 0, 0, 0))
halo_wide = pl.BlockSpec((1, 2, 2, 3 * CELLS, WIDE), lambda g: (g, 0, 0, 0, 0))
halo_shape = struct((GROUPS, 2, 2, 3 * CELLS, WIDE), F32)
any_spec = pl.BlockSpec(memory_space=pl.ANY)


def own_scores(rows, side_a, side_b, kd, vd, edges, part, s_out, d_out):
    masks = head_masks(PAIR)
    for place, t in enumerate(rows):
        at = at_tokens(place)
        queries = stacked([side_a[0, at], side_b[0, at]], masks)
        grads = stacked([side_a[1, at], side_b[1, at]], masks)
        scores = score_block(window(kd, edges, 0, t), queries, t)
        dprobs = matmul(window(vd, edges, 1, t), grads, (1, 1))
        s_out[0, place] = scores
        d_out[0, place] = dprobs
        for w, values in enumerate(row_stats(scores, dprobs)):
            for c in range(2):
                index = 4 * c + 2 * w + place
                part[0, index:index + 1] = values[:, pair_lanes(c)]


def mid_scores_kernel(side_0, side_1, kd, vd, part, s_out, d_out, turned):
    own_scores(MID_ROWS, side_0, side_1, kd, vd, None, part, s_out, d_out)
    turned[...] = kd[...].T


def edge_scores_kernel(side_0, side_1, kd, vd, edge_a, edge_b, part, s_out, d_out):
    own_scores(EDGE_ROWS, side_0, side_1, kd, vd, (edge_a, edge_b), part, s_out, d_out)


def mid_scores(*operands):
    return pl.pallas_call(
        mid_scores_kernel,
        grid=(PAIRS,),
        in_specs=[tokens_spec(MID)] * 2 + [keys_spec] * 2,
        out_specs=[part_spec] + [held_spec] * 2 + [pl.BlockSpec((PAIR, ROWS * PAIR), lambda p: (p, 0))],
        out_shape=[part_shape] + [held_shape] * 2 + [struct((FEAT, ROWS * PAIR), BF16)],
        compiler_params=params(),
        cost_estimate=cost(2e9, 1 << 10),
        name="mid_scores",
    )(*operands)


def edge_scores(*operands):
    return pl.pallas_call(
        edge_scores_kernel,
        grid=(PAIRS,),
        in_specs=[tokens_spec(EDGE)] * 2 + [keys_spec] * 2 + [edge_spec] * 2,
        out_specs=[part_spec] + [held_spec] * 2,
        out_shape=[part_shape] + [held_shape] * 2,
        compiler_params=params(),
        cost_estimate=cost(2e9, 1 << 10),
        name="edge_scores",
    )(*operands)


def turn_edges_kernel(edge_a, edge_b, turned):
    turned[0] = edge_a[0].T
    turned[1] = edge_b[0].T


def turn_edges(*operands):
    return pl.pallas_call(
        turn_edges_kernel,
        grid=(PAIRS,),
        in_specs=[edge_spec] * 2,
        out_specs=pl.BlockSpec((2, PAIR, PAIR), lambda p: (0, p, 0)),
        out_shape=struct((2, FEAT, PAIR), BF16),
        compiler_params=params(),
        cost_estimate=cost(1e9, 1 << 10),
        name="turn_edges",
    )(*operands)


def halo_scores_kernel(q_0, q_1, kd, vd, edge_a, edge_b, edge_part, mid_part,
                       send_0, send_1, s_edge, d_edge, s_mid, d_mid):
    masks = head_masks(WIDE)
    groups = ((EDGE_ROWS, edge_part, s_edge, d_edge), (MID_ROWS, mid_part, s_mid, d_mid))
    for group, (rows, part, s_out, d_out) in enumerate(groups):
        base = 8 * group
        for c, (q_in, send) in enumerate(((q_0, send_0), (q_1, send_1))):
            for j in range(2):
                send[j, base:base + 4] = part[j, 4 * c:4 * c + 4]
            for place, t in enumerate(rows):
                at = at_tokens(2 * group + place)
                queries = stacked([q_in[0, at]], masks)
                grads = stacked([q_in[1, at]], masks)
                scores = score_block(column_window(c, kd, (edge_a, edge_b), 0, t), queries, t)
                dprobs = matmul(column_window(c, vd, (edge_a, edge_b), 1, t), grads, (1, 1))
                s_out[0, place, c] = scores
                d_out[0, place, c] = dprobs
                for w, values in enumerate(row_stats(scores, dprobs)):
                    index = base + 4 + 2 * w + place
                    for j in range(2):
                        send[j, index:index + 1] = values[:, pair_lanes(j)]


def halo_scores(*operands):
    part = pl.BlockSpec((2, 8, PAIR), lambda g: (g, 0, 0))
    return pl.pallas_call(
        halo_scores_kernel,
        grid=(GROUPS,),
        in_specs=[all_tokens] * 2 + [keys_wide] * 2 + [edge_wide] * 2 + [part] * 2,
        out_specs=[all_stats] * 2 + [halo_wide] * 4,
        out_shape=[stats_shape] * 2 + [halo_shape] * 4,
        compiler_params=params(),
        cost_estimate=cost(2e9, 1 << 10),
        name="halo_scores",
    )(*operands)


def halo_weights(mine, theirs, s_in, d_in, c):
    both = [both_parts(mine, theirs, j, 4) for j in range(2)]
    log_total = jnp.concatenate([one[0] for one in both], axis=1)
    delta = jnp.concatenate([one[1] for one in both], axis=1)
    weights = []
    for place in range(2):
        probs = jnp.exp2(s_in[0, place, c] - log_total[place:place + 1])
        dscores = probs * (d_in[0, place, c] - delta[place:place + 1])
        weights.append((probs.astype(BF16), dscores.astype(BF16)))
    return weights


def halo_queries_kernel(send_0, send_1, recv_0, recv_1, s_edge, d_edge, s_mid, d_mid, own_turned, edges_turned,
                        out_0, out_1):
    lane = lax.broadcasted_iota(jnp.int32, (1, PAIR), 1)
    none = jnp.zeros((CELLS, PAIR), BF16)
    groups = ((EDGE_ROWS, s_edge, d_edge), (MID_ROWS, s_mid, d_mid))
    for group, (rows, s_in, d_in) in enumerate(groups):
        stats = [ref.at[:, pl.ds(8 * group, 8)] for ref in (send_0, send_1, recv_0, recv_1)]
        weights = [halo_weights(stats[c], stats[2 + c], s_in, d_in, c) for c in range(2)]
        for place, t in enumerate(rows):
            for j in range(2):
                pieces = []
                for i in range(3):
                    parts = [weights[c][place][1][at_tokens(i), pair_lanes(j)] for c in range(2)]
                    pieces += [jnp.concatenate([parts[0], none], axis=1), jnp.concatenate([none, parts[1]], axis=1)]
                keys_turned = turned_window(own_turned, edges_turned, t, j)
                grads = query_parts(keys_turned, jnp.concatenate(pieces, axis=0), lane)
                for out, grad in zip((out_0, out_1), grads):
                    out[at_tokens(2 * group + place), pair_lanes(j)] = grad.astype(BF16)


def halo_queries(*operands):
    return pl.pallas_call(
        halo_queries_kernel,
        grid=(GROUPS,),
        in_specs=[all_stats] * 4 + [halo_wide] * 4 + [turned_wide, edge_turned_wide],
        out_specs=[all_parts] * 2,
        out_shape=[struct((2 * CHUNK, FEAT), BF16)] * 2,
        compiler_params=params(),
        cost_estimate=cost(2e9, 1 << 10),
        name="halo_queries",
    )(*operands)


def row_gradients(rows, side_a, side_b, q_a, q_b, send_a, send_b, recv_a, recv_b, s_own, d_own, s_halo, d_halo,
                  own_turned, edges_turned, dq_ref):
    masks, wide_masks = head_masks(PAIR), head_masks(WIDE)
    lane = lax.broadcasted_iota(jnp.int32, (1, PAIR), 1)
    sides = ((q_a, send_a, recv_a), (q_b, send_b, recv_b))
    halo = [halo_weights(mine, theirs, s_halo, d_halo, c) for c, (_, mine, theirs) in enumerate(sides)]
    merged_rows = []
    for j in range(2):
        both = [both_parts(mine, theirs, j, 0) for _, mine, theirs in sides]
        merged_rows.append([jnp.concatenate([one[w] for one in both], axis=1) for w in range(2)])
    results = []
    for place, t in enumerate(rows):
        at, row = at_tokens(place), slice(place, place + 1)
        sums = [[], []]
        for j in range(2):
            lanes = pair_lanes(j)
            queries = stacked([side_a[0, at, lanes], side_b[0, at, lanes]], masks)
            grads = stacked([side_a[1, at, lanes], side_b[1, at, lanes]], masks)
            log_total, delta = merged_rows[j]
            probs = jnp.exp2(s_own[j, place] - log_total[row])
            dscores = (probs * (d_own[j, place] - delta[row])).astype(BF16)
            for c, part in enumerate(query_parts(turned_window(own_turned, edges_turned, t, j), dscores, lane)):
                dq_ref[c, at, lanes] = part
            sums[0].append(matmul(dscores, queries, (1, 0)))
            sums[1].append(matmul(probs.astype(BF16), grads, (1, 0)))
        sums = [jnp.concatenate(parts, axis=1) for parts in sums]
        edge_parts = []
        for c in range(2):
            probs, dscores = halo[c][place]
            edge_parts.append((matmul(dscores, stacked([sides[c][0][0, at]], wide_masks), (1, 0)),
                               matmul(probs, stacked([sides[c][0][1, at]], wide_masks), (1, 0))))
        results.append([jnp.concatenate([sums[w][at_tokens(2 * i + c)] + edge_parts[c][w][at_tokens(i)]
                                         for i in range(3) for c in range(2)], axis=0) for w in range(2)])
    return results


def edge_kernel(*refs):
    operands, (_, dq_ref, dk_ref, dv_ref, out_a, out_b) = refs[:14], refs[14:]
    upper, lower = row_gradients(EDGE_ROWS, *operands, dq_ref)
    for which, (out, scale) in enumerate(((dk_ref, SCALE), (dv_ref, 1.0))):
        top, bottom = upper[which] * scale, lower[which] * scale
        out_a[which] = top[:PAIR].astype(BF16)
        out[0:2 * PAIR] = top[PAIR:]
        out_b[which] = bottom[2 * PAIR:].astype(BF16)
        out[2 * PAIR:] = bottom[:2 * PAIR]


def mid_kernel(*refs):
    operands, (_, dk_in, dv_in, dq_ref, dk_ref, dv_ref) = refs[:13], refs[13:]
    upper, lower = row_gradients(MID_ROWS, *operands, None, dq_ref)
    for which, (sums, out, scale) in enumerate(((dk_in, dk_ref, SCALE), (dv_in, dv_ref, 1.0))):
        out[0:PAIR] = sums[0:PAIR] + upper[which][:PAIR] * scale
        out[PAIR:3 * PAIR] = sums[PAIR:3 * PAIR] + (upper[which][PAIR:] + lower[which][:2 * PAIR]) * scale
        out[3 * PAIR:] = sums[3 * PAIR:] + lower[which][2 * PAIR:] * scale


def row_specs(group):
    return ([tokens_wide(group)] * 4 + [stats_wide(group)] * 4 + [held_wide] * 2 + [halo_wide] * 2 + [turned_wide])


GRAD_SPECS = [sums_wide] + [keys_wide] * 2
GRAD_SHAPES = [struct((2, CHUNK, FEAT), F32)] + [struct((ROWS * PAIR, FEAT), F32)] * 2


def edge_gradients(*operands):
    return pl.pallas_call(
        edge_kernel,
        grid=(GROUPS,),
        in_specs=row_specs(EDGE) + [edge_turned_wide, any_spec],
        out_specs=GRAD_SPECS + [edge_wide] * 2,
        out_shape=GRAD_SHAPES + [struct((2, PAIR, FEAT), BF16)] * 2,
        compiler_params=params(),
        cost_estimate=cost(3e9, 1 << 10),
        name="edge_gradients",
    )(*operands)


def mid_gradients(*operands):
    return pl.pallas_call(
        mid_kernel,
        grid=(GROUPS,),
        in_specs=row_specs(MID) + [any_spec] + [keys_wide] * 2,
        out_specs=GRAD_SPECS,
        out_shape=GRAD_SHAPES,
        compiler_params=params(),
        cost_estimate=cost(3e9, 1 << 10),
        name="mid_gradients",
    )(*operands)


def join_columns(side_a, side_b):
    parts = ordered(side_a, side_b)
    return jnp.concatenate([part.reshape(8, 8, FEAT) for part in parts], axis=1).astype(BF16)


def finish_kernel(dq_edge, dq_mid, dk, dv, dq_0, dq_1, from_a, from_b,
                  q_ref, k_ref, v_ref, buffers, sems):
    copies = []

    def send(i, t, value):
        buffers[i, t] = value
        out = (q_ref, k_ref, v_ref)[i]
        copies.append(pltpu.make_async_copy(buffers.at[i, t], out.at[pl.ds(8 * grid_row(t), 8)], sems.at[i, t]))
        copies[-1].start()

    for t in range(ROWS):
        for which, own in enumerate((dk, dv)):
            full = own[t * PAIR:(t + 1) * PAIR]
            if t == 0:
                full = full + from_a[which].astype(F32)
            if t == ROWS - 1:
                full = full + from_b[which].astype(F32)
            send(1 + which, t, join_columns(full[:CELLS], full[CELLS:]))
    for place, t in enumerate(ORDER):
        dq = (dq_edge, dq_mid)[place // 2]
        at, there = at_tokens(place % 2), at_tokens(place)
        send(0, t, join_columns(dq[0, at] + dq_0[there].astype(F32), dq[1, at] + dq_1[there].astype(F32)))
    for copy in copies:
        copy.wait()


def finish(*operands):
    return pl.pallas_call(
        finish_kernel,
        out_specs=[any_spec] * 3,
        out_shape=[struct((8 * ROWS, 16, FEAT), BF16)] * 3,
        scratch_shapes=[pltpu.VMEM((3, ROWS, 8, 16, FEAT), BF16), pltpu.SemaphoreType.DMA((3, ROWS))],
        compiler_params=params(),
        cost_estimate=cost(0, 1 << 10),
        name="finish",
    )(*operands)


def swap_a(x, axis):
    return lax.ppermute(x, axis, [(i, i ^ 1) for i in range(lax.axis_size(axis))])


def swap_b(x, axis, wrap):
    count = lax.axis_size(axis)
    pairs = []
    for i in range(1, count if wrap else count - 1, 2):
        pairs += [(i, (i + 1) % count), ((i + 1) % count, i)]
    return lax.ppermute(x, axis, pairs)


def over_lon(side_0, side_1):
    return swap_b(side_0, "lon", True), swap_a(side_1, "lon")


def over_lat(side_a, side_b):
    return swap_a(side_a, "lat"), swap_b(side_b, "lat", False)


def on_device(query_vectors, key_vectors, value_vectors, output_grads):
    sides = pack_queries(query_vectors, output_grads)
    kd, vd, own_edge_a, own_edge_b = pack_keys(key_vectors, value_vectors)
    halos = over_lon(*sides)
    edges = over_lat(own_edge_a, own_edge_b)
    mid_part, *mid_own, turned = mid_scores(*sides, kd, vd)
    edge_part, *edge_own = edge_scores(*sides, kd, vd, *edges)
    *sends, s_edge, d_edge, s_mid, d_mid = halo_scores(*halos, kd, vd, *edges, edge_part, mid_part)
    stats = (*sends, *over_lon(*sends))
    edges_turned = turn_edges(*edges)
    halo_dq = halo_queries(*stats, s_edge, d_edge, s_mid, d_mid, turned, edges_turned)
    dq_parts = over_lon(*halo_dq)
    shared = (*sides, *halos, *stats)
    dq_edge, dk, dv, out_a, out_b = edge_gradients(*shared, *edge_own, s_edge, d_edge, turned, edges_turned, halo_dq[0])
    key_parts = over_lat(out_a, out_b)
    dq_mid, dk, dv = mid_gradients(*shared, *mid_own, s_mid, d_mid, turned, halo_dq[0], dk, dv)
    return tuple(finish(dq_edge, dq_mid, dk, dv, *dq_parts, *key_parts))


def solution(mesh):
    spec = P("lat", "lon", None)
    return jax.shard_map(on_device, mesh=mesh, in_specs=(spec,) * 4, out_specs=(spec,) * 3, check_vma=False)
```

```python
import functools

import jax
import jax.numpy as jnp
from jax import lax
from jax.experimental import pallas as pl
from jax.experimental.pallas import tpu as pltpu
from jax.sharding import PartitionSpec as P

ROWS = 4
CELLS = 64
CHUNK = 2 * CELLS
PAIR = 128
WIDE = 256
PAIRS = 4
GROUPS = 2
FEAT = 512
SCALE = 64 ** -0.5
LOG2E = 1.4426950408889634
MASKED = -1e30
F32 = jnp.float32
BF16 = jnp.bfloat16
VMEM_LIMIT = 20 * 1024 * 1024
PACK_LIMIT = 62 * 1024 * 1024
EDGE_ROWS = (0, 3)
MID_ROWS = (1, 2)
ORDER = EDGE_ROWS + MID_ROWS
EDGE, MID = 0, 1


def matmul(a, b, contract):
    return lax.dot_general(a, b, ((contract[:1], contract[1:]), ((), ())), preferred_element_type=F32)


def params(limit=VMEM_LIMIT):
    return pltpu.CompilerParams(vmem_limit_bytes=limit)


def cost(flops, size):
    return pl.CostEstimate(flops=int(flops), bytes_accessed=int(size), transcendentals=0)


def struct(shape, dtype):
    return jax.ShapeDtypeStruct(shape, dtype)


def grid_row(t):
    return jnp.where(lax.axis_index("lat") % 2 == 0, ROWS - 1 - t, t)


def ordered(first, second):
    swap = lax.axis_index("lon") % 2 == 1
    return jnp.where(swap, second, first), jnp.where(swap, first, second)


def split_columns(block):
    wide = block.astype(F32)
    parts = ordered(*[wide[:, c * 8:(c + 1) * 8].reshape(CELLS, FEAT) for c in range(2)])
    return [part.astype(BF16) for part in parts]


def fetch(refs, rows, buffers, sems):
    copies = [[pltpu.make_async_copy(ref.at[pl.ds(8 * grid_row(t), 8)], buffers.at[i, place], sems.at[i, place])
               for place, t in enumerate(rows)] for i, ref in enumerate(refs)]
    for place in range(len(rows)):
        for copy in copies:
            copy[place].start()
    return copies


def pack_queries_kernel(q_ref, g_ref, side_0, side_1, buffers, sems, packed, out_sems):
    copies = fetch((q_ref, g_ref), ORDER, buffers, sems)
    sends = []
    for place in range(ROWS):
        for i in range(2):
            copies[i][place].wait()
            for side, (value, out) in enumerate(zip(split_columns(buffers[i, place]), (side_0, side_1))):
                packed[side, i, place] = value
                sends.append(pltpu.make_async_copy(packed.at[side, i, place],
                                                   out.at[i, pl.ds(place * CELLS, CELLS)], out_sems.at[side, i, place]))
                sends[-1].start()
    for send in sends:
        send.wait()


def pack_queries(*operands):
    return pl.pallas_call(
        pack_queries_kernel,
        in_specs=[pl.BlockSpec(memory_space=pl.ANY)] * 2,
        out_specs=[pl.BlockSpec(memory_space=pl.ANY)] * 2,
        out_shape=[struct((2, ROWS * CELLS, FEAT), BF16)] * 2,
        scratch_shapes=[
            pltpu.VMEM((2, ROWS, 8, 16, FEAT), BF16), pltpu.SemaphoreType.DMA((2, ROWS)),
            pltpu.VMEM((2, 2, ROWS, CELLS, FEAT), BF16), pltpu.SemaphoreType.DMA((2, 2, ROWS)),
        ],
        compiler_params=params(PACK_LIMIT),
        cost_estimate=cost(0, 3 << 20),
        name="pack_queries",
    )(*operands)


def pack_keys_kernel(k_ref, v_ref, kd, vd, edge_a, edge_b, buffers, sems):
    copies = fetch((k_ref, v_ref), range(ROWS), buffers, sems)
    for t in range(ROWS):
        for i, out in enumerate((kd, vd)):
            copies[i][t].wait()
            tile = jnp.concatenate(split_columns(buffers[i, t]), axis=0)
            out[t * PAIR:(t + 1) * PAIR] = tile
            if t == 0:
                edge_a[i] = tile
            if t == ROWS - 1:
                edge_b[i] = tile


def pack_keys(*operands):
    return pl.pallas_call(
        pack_keys_kernel,
        in_specs=[pl.BlockSpec(memory_space=pl.ANY)] * 2,
        out_shape=[struct((ROWS * PAIR, FEAT), BF16)] * 2 + [struct((2, PAIR, FEAT), BF16)] * 2,
        scratch_shapes=[pltpu.VMEM((2, ROWS, 8, 16, FEAT), BF16), pltpu.SemaphoreType.DMA((2, ROWS))],
        compiler_params=params(),
        cost_estimate=cost(0, 3 << 20),
        name="pack_keys",
    )(*operands)


def head_masks(lanes):
    lane = lax.broadcasted_iota(jnp.int32, (1, lanes), 1)
    return [jnp.where((lane >= 64 * h) & (lane < 64 * (h + 1)), 1.0, 0.0).astype(F32).astype(BF16)
            for h in range(lanes // 64)]


def stacked(parts, masks):
    return jnp.concatenate([part * mask for part in parts for mask in masks], axis=0)


def key_rows(own, edges, which, t, lanes=slice(None)):
    rows = []
    for row in range(t, t + 3):
        if row == 0:
            rows.append(edges[0][which, :, lanes])
        elif row == ROWS + 1:
            rows.append(edges[1][which, :, lanes])
        else:
            rows.append(own[(row - 1) * PAIR:row * PAIR, lanes])
    return rows


def window(*where):
    return jnp.concatenate(key_rows(*where), axis=0)


def column_window(column, *where):
    return jnp.concatenate([row[column * CELLS:(column + 1) * CELLS] for row in key_rows(*where)], axis=0)


def score_block(keys, queries, t):
    scores = matmul(keys, queries, (1, 1)) * (SCALE * LOG2E)
    if t == ROWS - 1:
        lat = lax.axis_index("lat")
        outside = (lat == 0) | (lat == lax.axis_size("lat") - 1)
        cut = 2 * (keys.shape[0] // 3)
        bias = jnp.where(outside, MASKED, 0.0).astype(F32)
        scores = jnp.concatenate([scores[:cut], scores[cut:] + bias], axis=0)
    return scores


def row_stats(scores, dprobs):
    top = jnp.max(scores, axis=0, keepdims=True)
    weights = jnp.exp2(scores - top)
    total = jnp.sum(weights, axis=0, keepdims=True)
    delta = jnp.sum(weights * dprobs, axis=0, keepdims=True) / total
    return top + jnp.log(total) * LOG2E, delta


def merged(log_a, delta_a, log_b, delta_b):
    top = jnp.maximum(log_a, log_b)
    weight_a = jnp.exp2(log_a - top)
    weight_b = jnp.exp2(log_b - top)
    total = weight_a + weight_b
    return top + jnp.log(total) * LOG2E, (weight_a * delta_a + weight_b * delta_b) / total


def both_parts(mine, theirs, pair, base):
    other = 4 - base
    return merged(mine[pair, base:base + 2], mine[pair, base + 2:base + 4],
                  theirs[pair, other:other + 2], theirs[pair, other + 2:other + 4])


def turned_window(own_turned, edges_turned, t, j):
    at = slice(j * PAIR, (j + 1) * PAIR)
    rows = []
    for row in range(t, t + 3):
        if row in (0, ROWS + 1):
            rows.append(edges_turned[row // (ROWS + 1), at])
        else:
            rows.append(own_turned[at, (row - 1) * PAIR:row * PAIR])
    return jnp.concatenate(rows, axis=1)


def query_parts(keys_turned, dscores, lane):
    turned = matmul(keys_turned, dscores, (1, 0)) * SCALE
    parts = [turned[:, c * PAIR:(c + 1) * PAIR].T for c in range(2)]
    return [jnp.where(lane < 64, part[:CELLS], part[CELLS:]) for part in parts]


def at_tokens(place):
    return slice(place * CELLS, (place + 1) * CELLS)


def pair_lanes(j):
    return slice(j * PAIR, (j + 1) * PAIR)


def tokens_spec(group):
    return pl.BlockSpec((2, CHUNK, PAIR), lambda p: (0, group, p))


keys_spec = pl.BlockSpec((ROWS * PAIR, PAIR), lambda p: (0, p))
edge_spec = pl.BlockSpec((2, PAIR, PAIR), lambda p: (0, 0, p))
part_spec = pl.BlockSpec((1, 8, PAIR), lambda p: (p, 0, 0))
held_spec = pl.BlockSpec((1, 2, 3 * PAIR, WIDE), lambda p: (p, 0, 0, 0))
part_shape = struct((PAIRS, 8, PAIR), F32)
stats_shape = struct((PAIRS, 16, PAIR), F32)
held_shape = struct((PAIRS, 2, 3 * PAIR, WIDE), F32)


def tokens_wide(group):
    return pl.BlockSpec((2, CHUNK, WIDE), lambda g: (0, group, g))


def stats_wide(group):
    return pl.BlockSpec((2, 8, PAIR), lambda g: (g, group, 0))


all_tokens = pl.BlockSpec((2, 2 * CHUNK, WIDE), lambda g: (0, 0, g))
all_stats = pl.BlockSpec((2, 16, PAIR), lambda g: (g, 0, 0))
all_parts = pl.BlockSpec((2 * CHUNK, WIDE), lambda g: (0, g))
sums_wide = pl.BlockSpec((2, CHUNK, WIDE), lambda g: (0, 0, g))
keys_wide = pl.BlockSpec((ROWS * PAIR, WIDE), lambda g: (0, g))
edge_wide = pl.BlockSpec((2, PAIR, WIDE), lambda g: (0, 0, g))
turned_wide = pl.BlockSpec((WIDE, ROWS * PAIR), lambda g: (g, 0))
edge_turned_wide = pl.BlockSpec((2, WIDE, PAIR), lambda g: (0, g, 0))
held_wide = pl.BlockSpec((2, 2, 3 * PAIR, WIDE), lambda g: (g, 0, 0, 0))
halo_wide = pl.BlockSpec((1, 2, 2, 3 * CELLS, WIDE), lambda g: (g, 0, 0, 0, 0))
halo_shape = struct((GROUPS, 2, 2, 3 * CELLS, WIDE), F32)
any_spec = pl.BlockSpec(memory_space=pl.ANY)


def own_scores(rows, side_a, side_b, kd, vd, edges, part, s_out, d_out):
    masks = head_masks(PAIR)
    for place, t in enumerate(rows):
        at = at_tokens(place)
        queries = stacked([side_a[0, at], side_b[0, at]], masks)
        grads = stacked([side_a[1, at], side_b[1, at]], masks)
        scores = score_block(window(kd, edges, 0, t), queries, t)
        dprobs = matmul(window(vd, edges, 1, t), grads, (1, 1))
        s_out[0, place] = scores
        d_out[0, place] = dprobs
        for w, values in enumerate(row_stats(scores, dprobs)):
            for c in range(2):
                index = 4 * c + 2 * w + place
                part[0, index:index + 1] = values[:, pair_lanes(c)]


def mid_scores_kernel(side_0, side_1, kd, vd, part, s_out, d_out, turned):
    own_scores(MID_ROWS, side_0, side_1, kd, vd, None, part, s_out, d_out)
    turned[...] = kd[...].T


def edge_scores_kernel(side_0, side_1, kd, vd, edge_a, edge_b, part, s_out, d_out):
    own_scores(EDGE_ROWS, side_0, side_1, kd, vd, (edge_a, edge_b), part, s_out, d_out)


def mid_scores(*operands):
    return pl.pallas_call(
        mid_scores_kernel,
        grid=(PAIRS,),
        in_specs=[tokens_spec(MID)] * 2 + [keys_spec] * 2,
        out_specs=[part_spec] + [held_spec] * 2 + [pl.BlockSpec((PAIR, ROWS * PAIR), lambda p: (p, 0))],
        out_shape=[part_shape] + [held_shape] * 2 + [struct((FEAT, ROWS * PAIR), BF16)],
        compiler_params=params(),
        cost_estimate=cost(2e9, 1 << 10),
        name="mid_scores",
    )(*operands)


def edge_scores(*operands):
    return pl.pallas_call(
        edge_scores_kernel,
        grid=(PAIRS,),
        in_specs=[tokens_spec(EDGE)] * 2 + [keys_spec] * 2 + [edge_spec] * 2,
        out_specs=[part_spec] + [held_spec] * 2,
        out_shape=[part_shape] + [held_shape] * 2,
        compiler_params=params(),
        cost_estimate=cost(2e9, 1 << 10),
        name="edge_scores",
    )(*operands)


def turn_edges_kernel(edge_a, edge_b, turned):
    turned[0] = edge_a[0].T
    turned[1] = edge_b[0].T


def turn_edges(*operands):
    return pl.pallas_call(
        turn_edges_kernel,
        grid=(PAIRS,),
        in_specs=[edge_spec] * 2,
        out_specs=pl.BlockSpec((2, PAIR, PAIR), lambda p: (0, p, 0)),
        out_shape=struct((2, FEAT, PAIR), BF16),
        compiler_params=params(),
        cost_estimate=cost(1e9, 1 << 10),
        name="turn_edges",
    )(*operands)


def halo_scores_kernel(q_0, q_1, kd, vd, edge_a, edge_b, edge_part, mid_part,
                       send_0, send_1, s_edge, d_edge, s_mid, d_mid):
    masks = head_masks(WIDE)
    groups = ((EDGE_ROWS, edge_part, s_edge, d_edge), (MID_ROWS, mid_part, s_mid, d_mid))
    for group, (rows, part, s_out, d_out) in enumerate(groups):
        base = 8 * group
        for c, (q_in, send) in enumerate(((q_0, send_0), (q_1, send_1))):
            for j in range(2):
                send[j, base:base + 4] = part[j, 4 * c:4 * c + 4]
            for place, t in enumerate(rows):
                at = at_tokens(2 * group + place)
                queries = stacked([q_in[0, at]], masks)
                grads = stacked([q_in[1, at]], masks)
                scores = score_block(column_window(c, kd, (edge_a, edge_b), 0, t), queries, t)
                dprobs = matmul(column_window(c, vd, (edge_a, edge_b), 1, t), grads, (1, 1))
                s_out[0, place, c] = scores
                d_out[0, place, c] = dprobs
                for w, values in enumerate(row_stats(scores, dprobs)):
                    index = base + 4 + 2 * w + place
                    for j in range(2):
                        send[j, index:index + 1] = values[:, pair_lanes(j)]


def halo_scores(*operands):
    part = pl.BlockSpec((2, 8, PAIR), lambda g: (g, 0, 0))
    return pl.pallas_call(
        halo_scores_kernel,
        grid=(GROUPS,),
        in_specs=[all_tokens] * 2 + [keys_wide] * 2 + [edge_wide] * 2 + [part] * 2,
        out_specs=[all_stats] * 2 + [halo_wide] * 4,
        out_shape=[stats_shape] * 2 + [halo_shape] * 4,
        compiler_params=params(),
        cost_estimate=cost(2e9, 1 << 10),
        name="halo_scores",
    )(*operands)


def halo_weights(mine, theirs, s_in, d_in, c):
    both = [both_parts(mine, theirs, j, 4) for j in range(2)]
    log_total = jnp.concatenate([one[0] for one in both], axis=1)
    delta = jnp.concatenate([one[1] for one in both], axis=1)
    weights = []
    for place in range(2):
        probs = jnp.exp2(s_in[0, place, c] - log_total[place:place + 1])
        dscores = probs * (d_in[0, place, c] - delta[place:place + 1])
        weights.append((probs.astype(BF16), dscores.astype(BF16)))
    return weights


def halo_queries_kernel(send_0, send_1, recv_0, recv_1, s_edge, d_edge, s_mid, d_mid, own_turned, edges_turned,
                        out_0, out_1):
    lane = lax.broadcasted_iota(jnp.int32, (1, PAIR), 1)
    none = jnp.zeros((CELLS, PAIR), BF16)
    groups = ((EDGE_ROWS, s_edge, d_edge), (MID_ROWS, s_mid, d_mid))
    for group, (rows, s_in, d_in) in enumerate(groups):
        stats = [ref.at[:, pl.ds(8 * group, 8)] for ref in (send_0, send_1, recv_0, recv_1)]
        weights = [halo_weights(stats[c], stats[2 + c], s_in, d_in, c) for c in range(2)]
        for place, t in enumerate(rows):
            for j in range(2):
                pieces = []
                for i in range(3):
                    parts = [weights[c][place][1][at_tokens(i), pair_lanes(j)] for c in range(2)]
                    pieces += [jnp.concatenate([parts[0], none], axis=1), jnp.concatenate([none, parts[1]], axis=1)]
                keys_turned = turned_window(own_turned, edges_turned, t, j)
                grads = query_parts(keys_turned, jnp.concatenate(pieces, axis=0), lane)
                for out, grad in zip((out_0, out_1), grads):
                    out[at_tokens(2 * group + place), pair_lanes(j)] = grad.astype(BF16)


def halo_queries(*operands):
    return pl.pallas_call(
        halo_queries_kernel,
        grid=(GROUPS,),
        in_specs=[all_stats] * 4 + [halo_wide] * 4 + [turned_wide, edge_turned_wide],
        out_specs=[all_parts] * 2,
        out_shape=[struct((2 * CHUNK, FEAT), BF16)] * 2,
        compiler_params=params(),
        cost_estimate=cost(2e9, 1 << 10),
        name="halo_queries",
    )(*operands)


def row_gradients(rows, side_a, side_b, q_a, q_b, send_a, send_b, recv_a, recv_b, s_own, d_own, s_halo, d_halo,
                  own_turned, edges_turned, dq_ref):
    masks, wide_masks = head_masks(PAIR), head_masks(WIDE)
    lane = lax.broadcasted_iota(jnp.int32, (1, PAIR), 1)
    sides = ((q_a, send_a, recv_a), (q_b, send_b, recv_b))
    halo = [halo_weights(mine, theirs, s_halo, d_halo, c) for c, (_, mine, theirs) in enumerate(sides)]
    merged_rows = []
    for j in range(2):
        both = [both_parts(mine, theirs, j, 0) for _, mine, theirs in sides]
        merged_rows.append([jnp.concatenate([one[w] for one in both], axis=1) for w in range(2)])
    results = []
    for place, t in enumerate(rows):
        at, row = at_tokens(place), slice(place, place + 1)
        sums = [[], []]
        for j in range(2):
            lanes = pair_lanes(j)
            queries = stacked([side_a[0, at, lanes], side_b[0, at, lanes]], masks)
            grads = stacked([side_a[1, at, lanes], side_b[1, at, lanes]], masks)
            log_total, delta = merged_rows[j]
            probs = jnp.exp2(s_own[j, place] - log_total[row])
            dscores = (probs * (d_own[j, place] - delta[row])).astype(BF16)
            for c, part in enumerate(query_parts(turned_window(own_turned, edges_turned, t, j), dscores, lane)):
                dq_ref[c, at, lanes] = part
            sums[0].append(matmul(dscores, queries, (1, 0)))
            sums[1].append(matmul(probs.astype(BF16), grads, (1, 0)))
        sums = [jnp.concatenate(parts, axis=1) for parts in sums]
        edge_parts = []
        for c in range(2):
            probs, dscores = halo[c][place]
            edge_parts.append((matmul(dscores, stacked([sides[c][0][0, at]], wide_masks), (1, 0)),
                               matmul(probs, stacked([sides[c][0][1, at]], wide_masks), (1, 0))))
        results.append([jnp.concatenate([sums[w][at_tokens(2 * i + c)] + edge_parts[c][w][at_tokens(i)]
                                         for i in range(3) for c in range(2)], axis=0) for w in range(2)])
    return results


def edge_kernel(*refs):
    operands, (_, _, dq_ref, dk_ref, dv_ref, out_a, out_b) = refs[:14], refs[14:]
    upper, lower = row_gradients(EDGE_ROWS, *operands, dq_ref)
    for which, (out, scale) in enumerate(((dk_ref, SCALE), (dv_ref, 1.0))):
        top, bottom = upper[which] * scale, lower[which] * scale
        out_a[which] = top[:PAIR].astype(BF16)
        out[0:2 * PAIR] = top[PAIR:]
        out_b[which] = bottom[2 * PAIR:].astype(BF16)
        out[2 * PAIR:] = bottom[:2 * PAIR]


def mid_kernel(*refs):
    operands, (dk_in, dv_in, dq_ref, dk_ref, dv_ref) = refs[:13], refs[13:]
    upper, lower = row_gradients(MID_ROWS, *operands, None, dq_ref)
    for which, (sums, out, scale) in enumerate(((dk_in, dk_ref, SCALE), (dv_in, dv_ref, 1.0))):
        out[0:PAIR] = sums[0:PAIR] + upper[which][:PAIR] * scale
        out[PAIR:3 * PAIR] = sums[PAIR:3 * PAIR] + (upper[which][PAIR:] + lower[which][:2 * PAIR]) * scale
        out[3 * PAIR:] = sums[3 * PAIR:] + lower[which][2 * PAIR:] * scale


def row_specs(group):
    return ([tokens_wide(group)] * 4 + [stats_wide(group)] * 4 + [held_wide] * 2 + [halo_wide] * 2 + [turned_wide])


GRAD_SPECS = [sums_wide] + [keys_wide] * 2
GRAD_SHAPES = [struct((2, CHUNK, FEAT), F32)] + [struct((ROWS * PAIR, FEAT), F32)] * 2


def edge_gradients(*operands):
    return pl.pallas_call(
        edge_kernel,
        grid=(GROUPS,),
        in_specs=row_specs(EDGE) + [edge_turned_wide, any_spec, any_spec],
        out_specs=GRAD_SPECS + [edge_wide] * 2,
        out_shape=GRAD_SHAPES + [struct((2, PAIR, FEAT), BF16)] * 2,
        compiler_params=params(),
        cost_estimate=cost(3e9, 1 << 10),
        name="edge_gradients",
    )(*operands)


def mid_gradients(*operands):
    return pl.pallas_call(
        mid_kernel,
        grid=(GROUPS,),
        in_specs=row_specs(MID) + [keys_wide] * 2,
        out_specs=GRAD_SPECS,
        out_shape=GRAD_SHAPES,
        compiler_params=params(),
        cost_estimate=cost(3e9, 1 << 10),
        name="mid_gradients",
    )(*operands)


def join_columns(side_a, side_b):
    parts = ordered(side_a, side_b)
    return jnp.concatenate([part.reshape(8, 8, FEAT) for part in parts], axis=1).astype(BF16)


def finish_kernel(dq_edge, dq_mid, dk, dv, dq_0, dq_1, from_a, from_b,
                  q_ref, k_ref, v_ref, buffers, sems):
    copies = []

    def send(i, t, value):
        buffers[i, t] = value
        out = (q_ref, k_ref, v_ref)[i]
        copies.append(pltpu.make_async_copy(buffers.at[i, t], out.at[pl.ds(8 * grid_row(t), 8)], sems.at[i, t]))
        copies[-1].start()

    for t in range(ROWS):
        for which, own in enumerate((dk, dv)):
            full = own[t * PAIR:(t + 1) * PAIR]
            if t == 0:
                full = full + from_a[which].astype(F32)
            if t == ROWS - 1:
                full = full + from_b[which].astype(F32)
            send(1 + which, t, join_columns(full[:CELLS], full[CELLS:]))
    for place, t in enumerate(ORDER):
        dq = (dq_edge, dq_mid)[place // 2]
        at, there = at_tokens(place % 2), at_tokens(place)
        send(0, t, join_columns(dq[0, at] + dq_0[there].astype(F32), dq[1, at] + dq_1[there].astype(F32)))
    for copy in copies:
        copy.wait()


def finish(*operands):
    return pl.pallas_call(
        finish_kernel,
        out_specs=[any_spec] * 3,
        out_shape=[struct((8 * ROWS, 16, FEAT), BF16)] * 3,
        scratch_shapes=[pltpu.VMEM((3, ROWS, 8, 16, FEAT), BF16), pltpu.SemaphoreType.DMA((3, ROWS))],
        compiler_params=params(),
        cost_estimate=cost(0, 1 << 10),
        name="finish",
    )(*operands)


def swap_a(x, axis):
    return lax.ppermute(x, axis, [(i, i ^ 1) for i in range(lax.axis_size(axis))])


def swap_b(x, axis, wrap):
    count = lax.axis_size(axis)
    pairs = []
    for i in range(1, count if wrap else count - 1, 2):
        pairs += [(i, (i + 1) % count), ((i + 1) % count, i)]
    return lax.ppermute(x, axis, pairs)


def over_lon(side_0, side_1):
    return swap_b(side_0, "lon", True), swap_a(side_1, "lon")


def over_lat(side_a, side_b):
    return swap_a(side_a, "lat"), swap_b(side_b, "lat", False)


def on_device(query_vectors, key_vectors, value_vectors, output_grads):
    sides = pack_queries(query_vectors, output_grads)
    kd, vd, own_edge_a, own_edge_b = pack_keys(key_vectors, value_vectors)
    halos = over_lon(*sides)
    edges = over_lat(own_edge_a, own_edge_b)
    mid_part, *mid_own, turned = mid_scores(*sides, kd, vd)
    edge_part, *edge_own = edge_scores(*sides, kd, vd, *edges)
    *sends, s_edge, d_edge, s_mid, d_mid = halo_scores(*halos, kd, vd, *edges, edge_part, mid_part)
    stats = (*sends, *over_lon(*sends))
    edges_turned = turn_edges(*edges)
    halo_dq = halo_queries(*stats, s_edge, d_edge, s_mid, d_mid, turned, edges_turned)
    dq_parts = over_lon(*halo_dq)
    shared = (*sides, *halos, *stats)
    dq_edge, dk, dv, out_a, out_b = edge_gradients(*shared, *edge_own, s_edge, d_edge, turned, edges_turned, *halo_dq)
    key_parts = over_lat(out_a, out_b)
    dq_mid, dk, dv = mid_gradients(*shared, *mid_own, s_mid, d_mid, turned, dk, dv)
    return tuple(finish(dq_edge, dq_mid, dk, dv, *dq_parts, *key_parts))


def solution(mesh):
    spec = P("lat", "lon", None)
    return jax.shard_map(on_device, mesh=mesh, in_specs=(spec,) * 4, out_specs=(spec,) * 3, check_vma=False)
```

```python
import functools

import jax
import jax.numpy as jnp
from jax import lax
from jax.experimental import pallas as pl
from jax.experimental.pallas import tpu as pltpu
from jax.sharding import PartitionSpec as P

ROWS = 4
CELLS = 64
CHUNK = 2 * CELLS
PAIR = 128
WIDE = 256
PAIRS = 4
GROUPS = 2
FEAT = 512
SCALE = 64 ** -0.5
LOG2E = 1.4426950408889634
MASKED = -1e30
F32 = jnp.float32
BF16 = jnp.bfloat16
VMEM_LIMIT = 20 * 1024 * 1024
PACK_LIMIT = 62 * 1024 * 1024
any_spec = pl.BlockSpec(memory_space=pl.ANY)
EDGE_ROWS = (0, 3)
MID_ROWS = (1, 2)
ORDER = EDGE_ROWS + MID_ROWS
EDGE, MID = 0, 1


def matmul(a, b, contract):
    return lax.dot_general(a, b, ((contract[:1], contract[1:]), ((), ())), preferred_element_type=F32)


def params(limit=VMEM_LIMIT):
    return pltpu.CompilerParams(vmem_limit_bytes=limit)


def cost(flops, size):
    return pl.CostEstimate(flops=int(flops), bytes_accessed=int(size), transcendentals=0)


def struct(shape, dtype):
    return jax.ShapeDtypeStruct(shape, dtype)


def grid_row(t):
    return jnp.where(lax.axis_index("lat") % 2 == 0, ROWS - 1 - t, t)


def ordered(first, second):
    swap = lax.axis_index("lon") % 2 == 1
    return jnp.where(swap, second, first), jnp.where(swap, first, second)


def split_columns(block):
    wide = block.astype(F32)
    parts = ordered(*[wide[:, c * 8:(c + 1) * 8].reshape(CELLS, FEAT) for c in range(2)])
    return [part.astype(BF16) for part in parts]


def fetch(refs, rows, buffers, sems):
    copies = [[pltpu.make_async_copy(ref.at[pl.ds(8 * grid_row(t), 8)], buffers.at[i, place], sems.at[i, place])
               for place, t in enumerate(rows)] for i, ref in enumerate(refs)]
    for place in range(len(rows)):
        for copy in copies:
            copy[place].start()
    return copies


def key_tile(buffer):
    return jnp.concatenate(split_columns(buffer), axis=0)


def pack_queries_kernel(q_ref, g_ref, k_ref, v_ref, side_0, side_1, edge_a, edge_b,
                        buffers, sems, key_buffers, key_sems, packed, out_sems):
    key_copies = fetch((k_ref, v_ref), (ROWS - 1, 0), key_buffers, key_sems)
    copies = fetch((q_ref, g_ref), ORDER, buffers, sems)
    for i in range(2):
        for place, edge in enumerate((edge_b, edge_a)):
            key_copies[i][place].wait()
            edge[i] = key_tile(key_buffers[i, place])
    sends = []
    for place in range(ROWS):
        for i in range(2):
            copies[i][place].wait()
            for side, (value, out) in enumerate(zip(split_columns(buffers[i, place]), (side_0, side_1))):
                packed[side, i, place] = value
                sends.append(pltpu.make_async_copy(packed.at[side, i, place],
                                                   out.at[i, pl.ds(place * CELLS, CELLS)], out_sems.at[side, i, place]))
                sends[-1].start()
    for send in sends:
        send.wait()


def pack_queries(*operands):
    return pl.pallas_call(
        pack_queries_kernel,
        in_specs=[any_spec] * 4,
        out_specs=[any_spec] * 2 + [pl.BlockSpec(memory_space=pltpu.VMEM)] * 2,
        out_shape=[struct((2, ROWS * CELLS, FEAT), BF16)] * 2 + [struct((2, PAIR, FEAT), BF16)] * 2,
        scratch_shapes=[
            pltpu.VMEM((2, ROWS, 8, 16, FEAT), BF16), pltpu.SemaphoreType.DMA((2, ROWS)),
            pltpu.VMEM((2, 2, 8, 16, FEAT), BF16), pltpu.SemaphoreType.DMA((2, 2)),
            pltpu.VMEM((2, 2, ROWS, CELLS, FEAT), BF16), pltpu.SemaphoreType.DMA((2, 2, ROWS)),
        ],
        compiler_params=params(PACK_LIMIT),
        cost_estimate=cost(0, 3 << 20),
        name="pack_queries",
    )(*operands)


def pack_keys_kernel(k_ref, v_ref, kd, vd, buffers, sems):
    copies = fetch((k_ref, v_ref), range(ROWS), buffers, sems)
    for t in range(ROWS):
        for i, out in enumerate((kd, vd)):
            copies[i][t].wait()
            out[t * PAIR:(t + 1) * PAIR] = key_tile(buffers[i, t])


def pack_keys(*operands):
    return pl.pallas_call(
        pack_keys_kernel,
        in_specs=[any_spec] * 2,
        out_shape=[struct((ROWS * PAIR, FEAT), BF16)] * 2,
        scratch_shapes=[pltpu.VMEM((2, ROWS, 8, 16, FEAT), BF16), pltpu.SemaphoreType.DMA((2, ROWS))],
        compiler_params=params(),
        cost_estimate=cost(0, 3 << 20),
        name="pack_keys",
    )(*operands)


def head_masks(lanes):
    lane = lax.broadcasted_iota(jnp.int32, (1, lanes), 1)
    return [jnp.where((lane >= 64 * h) & (lane < 64 * (h + 1)), 1.0, 0.0).astype(F32).astype(BF16)
            for h in range(lanes // 64)]


def stacked(parts, masks):
    return jnp.concatenate([part * mask for part in parts for mask in masks], axis=0)


def key_rows(own, edges, which, t, lanes=slice(None)):
    rows = []
    for row in range(t, t + 3):
        if row == 0:
            rows.append(edges[0][which, :, lanes])
        elif row == ROWS + 1:
            rows.append(edges[1][which, :, lanes])
        else:
            rows.append(own[(row - 1) * PAIR:row * PAIR, lanes])
    return rows


def window(*where):
    return jnp.concatenate(key_rows(*where), axis=0)


def column_window(column, *where):
    return jnp.concatenate([row[column * CELLS:(column + 1) * CELLS] for row in key_rows(*where)], axis=0)


def score_block(keys, queries, t):
    scores = matmul(keys, queries, (1, 1)) * (SCALE * LOG2E)
    if t == ROWS - 1:
        lat = lax.axis_index("lat")
        outside = (lat == 0) | (lat == lax.axis_size("lat") - 1)
        cut = 2 * (keys.shape[0] // 3)
        bias = jnp.where(outside, MASKED, 0.0).astype(F32)
        scores = jnp.concatenate([scores[:cut], scores[cut:] + bias], axis=0)
    return scores


def row_stats(scores, dprobs):
    top = jnp.max(scores, axis=0, keepdims=True)
    weights = jnp.exp2(scores - top)
    total = jnp.sum(weights, axis=0, keepdims=True)
    delta = jnp.sum(weights * dprobs, axis=0, keepdims=True) / total
    return top + jnp.log(total) * LOG2E, delta


def merged(log_a, delta_a, log_b, delta_b):
    top = jnp.maximum(log_a, log_b)
    weight_a = jnp.exp2(log_a - top)
    weight_b = jnp.exp2(log_b - top)
    total = weight_a + weight_b
    return top + jnp.log(total) * LOG2E, (weight_a * delta_a + weight_b * delta_b) / total


def both_parts(mine, theirs, pair, base):
    return merged(mine[pair, base:base + 2], mine[pair, base + 2:base + 4],
                  theirs[pair, base:base + 2], theirs[pair, base + 2:base + 4])


def turned_window(own_turned, edges_turned, t, j):
    at = slice(j * PAIR, (j + 1) * PAIR)
    rows = []
    for row in range(t, t + 3):
        if row in (0, ROWS + 1):
            rows.append(edges_turned[row // (ROWS + 1), at])
        else:
            rows.append(own_turned[at, (row - 1) * PAIR:row * PAIR])
    return jnp.concatenate(rows, axis=1)


def query_parts(keys_turned, dscores, lane):
    turned = matmul(keys_turned, dscores, (1, 0)) * SCALE
    parts = [turned[:, c * PAIR:(c + 1) * PAIR].T for c in range(2)]
    return [jnp.where(lane < 64, part[:CELLS], part[CELLS:]) for part in parts]


def at_tokens(place):
    return slice(place * CELLS, (place + 1) * CELLS)


def pair_lanes(j):
    return slice(j * PAIR, (j + 1) * PAIR)


def tokens_spec(group):
    return pl.BlockSpec((2, CHUNK, PAIR), lambda p: (0, group, p))


keys_spec = pl.BlockSpec((ROWS * PAIR, PAIR), lambda p: (0, p))
edge_spec = pl.BlockSpec((2, PAIR, PAIR), lambda p: (0, 0, p))
stats_spec = pl.BlockSpec((1, 8, PAIR), lambda p: (p, 0, 0))
held_spec = pl.BlockSpec((1, 2, 3 * PAIR, WIDE), lambda p: (p, 0, 0, 0))
stats_shape = struct((PAIRS, 8, PAIR), F32)
held_shape = struct((PAIRS, 2, 3 * PAIR, WIDE), F32)


def tokens_wide(group):
    return pl.BlockSpec((2, CHUNK, WIDE), lambda g: (0, group, g))


all_tokens = pl.BlockSpec((2, 2 * CHUNK, WIDE), lambda g: (0, 0, g))
stats_wide = pl.BlockSpec((2, 8, PAIR), lambda g: (g, 0, 0))
all_parts = pl.BlockSpec((2 * CHUNK, WIDE), lambda g: (0, g))
sums_wide = pl.BlockSpec((2, CHUNK, WIDE), lambda g: (0, 0, g))
keys_wide = pl.BlockSpec((ROWS * PAIR, WIDE), lambda g: (0, g))
edge_wide = pl.BlockSpec((2, PAIR, WIDE), lambda g: (0, 0, g))
turned_wide = pl.BlockSpec((WIDE, ROWS * PAIR), lambda g: (g, 0))
edge_turned_wide = pl.BlockSpec((2, WIDE, PAIR), lambda g: (0, g, 0))
held_wide = pl.BlockSpec((2, 2, 3 * PAIR, WIDE), lambda g: (g, 0, 0, 0))
halo_wide = pl.BlockSpec((1, 2, 2, 3 * CELLS, WIDE), lambda g: (g, 0, 0, 0, 0))
halo_shape = struct((GROUPS, 2, 2, 3 * CELLS, WIDE), BF16)


def own_scores(rows, base, side_0, side_1, kd, vd, edges, parts, s_out, d_out):
    masks = head_masks(PAIR)
    for place, t in enumerate(rows):
        at = at_tokens(place)
        queries = stacked([side_0[0, at], side_1[0, at]], masks)
        grads = stacked([side_0[1, at], side_1[1, at]], masks)
        scores = score_block(window(kd, edges, 0, t), queries, t)
        dprobs = matmul(window(vd, edges, 1, t), grads, (1, 1))
        s_out[0, place] = scores
        d_out[0, place] = dprobs
        for w, values in enumerate(row_stats(scores, dprobs)):
            for c in range(2):
                index = base + 2 * w + place
                parts[c][0, index:index + 1] = values[:, pair_lanes(c)]


def mid_scores_kernel(side_0, side_1, kd, vd, part_0, part_1, s_out, d_out, turned):
    for part in (part_0, part_1):
        part[0, 0:4] = jnp.zeros((4, PAIR), F32)
    own_scores(MID_ROWS, 4, side_0, side_1, kd, vd, None, (part_0, part_1), s_out, d_out)
    turned[...] = kd[...].T


def edge_scores_kernel(side_0, side_1, kd, vd, edge_a, edge_b, mid_0, mid_1, part_0, part_1, s_out, d_out):
    for part, mid in ((part_0, mid_0), (part_1, mid_1)):
        part[0, 4:8] = mid[0, 4:8]
    own_scores(EDGE_ROWS, 0, side_0, side_1, kd, vd, (edge_a, edge_b), (part_0, part_1), s_out, d_out)


def mid_scores(*operands):
    return pl.pallas_call(
        mid_scores_kernel,
        grid=(PAIRS,),
        in_specs=[tokens_spec(MID)] * 2 + [keys_spec] * 2,
        out_specs=[stats_spec] * 2 + [held_spec] * 2 + [pl.BlockSpec((PAIR, ROWS * PAIR), lambda p: (p, 0))],
        out_shape=[stats_shape] * 2 + [held_shape] * 2 + [struct((FEAT, ROWS * PAIR), BF16)],
        compiler_params=params(),
        cost_estimate=cost(2e9, 1 << 10),
        name="mid_scores",
    )(*operands)


def edge_scores(*operands):
    return pl.pallas_call(
        edge_scores_kernel,
        grid=(PAIRS,),
        in_specs=[tokens_spec(EDGE)] * 2 + [keys_spec] * 2 + [edge_spec] * 2 + [stats_spec] * 2,
        out_specs=[stats_spec] * 2 + [held_spec] * 2,
        out_shape=[stats_shape] * 2 + [held_shape] * 2,
        compiler_params=params(),
        cost_estimate=cost(2e9, 1 << 10),
        name="edge_scores",
    )(*operands)


def turn_edges_kernel(edge_a, edge_b, turned):
    turned[0] = edge_a[0].T
    turned[1] = edge_b[0].T


def turn_edges(*operands):
    return pl.pallas_call(
        turn_edges_kernel,
        grid=(PAIRS,),
        in_specs=[edge_spec] * 2,
        out_specs=pl.BlockSpec((2, PAIR, PAIR), lambda p: (0, p, 0)),
        out_shape=struct((2, FEAT, PAIR), BF16),
        compiler_params=params(),
        cost_estimate=cost(1e9, 1 << 10),
        name="turn_edges",
    )(*operands)


def halo_kernel(q_0, q_1, kd, vd, edge_a, edge_b, own_0, own_1, own_turned, edges_turned,
                part_0, part_1, out_0, out_1, p_edge, ds_edge, p_mid, ds_mid, s_held, d_held):
    masks = head_masks(WIDE)
    lane = lax.broadcasted_iota(jnp.int32, (1, PAIR), 1)
    none = jnp.zeros((CELLS, PAIR), BF16)
    sides = ((q_0, own_0, part_0), (q_1, own_1, part_1))
    groups = ((EDGE_ROWS, p_edge, ds_edge), (MID_ROWS, p_mid, ds_mid))
    for group, (rows, _, _) in enumerate(groups):
        for place, t in enumerate(rows):
            at = at_tokens(2 * group + place)
            for c, (q_in, _, part) in enumerate(sides):
                queries = stacked([q_in[0, at]], masks)
                grads = stacked([q_in[1, at]], masks)
                scores = score_block(column_window(c, kd, (edge_a, edge_b), 0, t), queries, t)
                dprobs = matmul(column_window(c, vd, (edge_a, edge_b), 1, t), grads, (1, 1))
                s_held[group, place, c] = scores
                d_held[group, place, c] = dprobs
                for w, values in enumerate(row_stats(scores, dprobs)):
                    index = 4 * group + 2 * w + place
                    for j in range(2):
                        part[j, index:index + 1] = values[:, pair_lanes(j)]
    for group, (rows, p_out, ds_out) in enumerate(groups):
        rows_merged = []
        for _, own, part in sides:
            both = [both_parts(part, own, j, 4 * group) for j in range(2)]
            rows_merged.append([jnp.concatenate([one[w] for one in both], axis=1) for w in range(2)])
        for place, t in enumerate(rows):
            low = []
            for c in range(2):
                log_total, delta = rows_merged[c]
                probs = jnp.exp2(s_held[group, place, c] - log_total[place:place + 1])
                low.append((probs * (d_held[group, place, c] - delta[place:place + 1])).astype(BF16))
                p_out[0, place, c] = probs.astype(BF16)
                ds_out[0, place, c] = low[c]
            for j in range(2):
                pieces = []
                for i in range(3):
                    parts = [low[c][at_tokens(i), pair_lanes(j)] for c in range(2)]
                    pieces += [jnp.concatenate([parts[0], none], axis=1), jnp.concatenate([none, parts[1]], axis=1)]
                keys_turned = turned_window(own_turned, edges_turned, t, j)
                grads = query_parts(keys_turned, jnp.concatenate(pieces, axis=0), lane)
                for out, grad in zip((out_0, out_1), grads):
                    out[at_tokens(2 * group + place), pair_lanes(j)] = grad.astype(BF16)


def halo(*operands):
    return pl.pallas_call(
        halo_kernel,
        grid=(GROUPS,),
        in_specs=[all_tokens] * 2 + [keys_wide] * 2 + [edge_wide] * 2 + [stats_wide] * 2 + [turned_wide, edge_turned_wide],
        out_specs=[stats_wide] * 2 + [all_parts] * 2 + [halo_wide] * 4,
        out_shape=[stats_shape] * 2 + [struct((2 * CHUNK, FEAT), BF16)] * 2 + [halo_shape] * 4,
        scratch_shapes=[pltpu.VMEM((2, 2, 2, 3 * CELLS, WIDE), F32)] * 2,
        compiler_params=params(),
        cost_estimate=cost(2e9, 1 << 10),
        name="halo",
    )(*operands)


def row_gradients(rows, base, side_0, side_1, q_0, q_1, own_0, own_1, recv_0, recv_1, s_own, d_own, p_halo, ds_halo,
                  own_turned, edges_turned, dq_ref):
    masks, wide_masks = head_masks(PAIR), head_masks(WIDE)
    lane = lax.broadcasted_iota(jnp.int32, (1, PAIR), 1)
    merged_rows = []
    for j in range(2):
        both = [both_parts(own_0, recv_0, j, base), both_parts(own_1, recv_1, j, base)]
        merged_rows.append([jnp.concatenate([one[w] for one in both], axis=1) for w in range(2)])
    results = []
    for place, t in enumerate(rows):
        at, row = at_tokens(place), slice(place, place + 1)
        sums = [[], []]
        for j in range(2):
            lanes = pair_lanes(j)
            queries = stacked([side_0[0, at, lanes], side_1[0, at, lanes]], masks)
            grads = stacked([side_0[1, at, lanes], side_1[1, at, lanes]], masks)
            log_total, delta = merged_rows[j]
            probs = jnp.exp2(s_own[j, place] - log_total[row])
            dscores = (probs * (d_own[j, place] - delta[row])).astype(BF16)
            for c, part in enumerate(query_parts(turned_window(own_turned, edges_turned, t, j), dscores, lane)):
                dq_ref[c, at, lanes] = part
            sums[0].append(matmul(dscores, queries, (1, 0)))
            sums[1].append(matmul(probs.astype(BF16), grads, (1, 0)))
        sums = [jnp.concatenate(parts, axis=1) for parts in sums]
        edge_parts = []
        for c, q_in in enumerate((q_0, q_1)):
            edge_parts.append((matmul(ds_halo[0, place, c], stacked([q_in[0, at]], wide_masks), (1, 0)),
                               matmul(p_halo[0, place, c], stacked([q_in[1, at]], wide_masks), (1, 0))))
        results.append([jnp.concatenate([sums[w][at_tokens(2 * i + c)] + edge_parts[c][w][at_tokens(i)]
                                         for i in range(3) for c in range(2)], axis=0) for w in range(2)])
    return results


def edge_kernel(*refs):
    operands, (_, _, dq_ref, dk_ref, dv_ref, out_a, out_b) = refs[:14], refs[14:]
    upper, lower = row_gradients(EDGE_ROWS, 0, *operands, dq_ref)
    for which, (out, scale) in enumerate(((dk_ref, SCALE), (dv_ref, 1.0))):
        top, bottom = upper[which] * scale, lower[which] * scale
        out_a[which] = top[:PAIR].astype(BF16)
        out[0:2 * PAIR] = top[PAIR:]
        out_b[which] = bottom[2 * PAIR:].astype(BF16)
        out[2 * PAIR:] = bottom[:2 * PAIR]


def mid_kernel(*refs):
    operands, (dk_in, dv_in, dq_ref, dk_ref, dv_ref) = refs[:13], refs[13:]
    upper, lower = row_gradients(MID_ROWS, 4, *operands, None, dq_ref)
    for which, (sums, out, scale) in enumerate(((dk_in, dk_ref, SCALE), (dv_in, dv_ref, 1.0))):
        out[0:PAIR] = sums[0:PAIR] + upper[which][:PAIR] * scale
        out[PAIR:3 * PAIR] = sums[PAIR:3 * PAIR] + (upper[which][PAIR:] + lower[which][:2 * PAIR]) * scale
        out[3 * PAIR:] = sums[3 * PAIR:] + lower[which][2 * PAIR:] * scale


def row_specs(group):
    return ([tokens_wide(group)] * 4 + [stats_wide] * 4 + [held_wide] * 2 + [halo_wide] * 2 + [turned_wide])


GRAD_SPECS = [sums_wide] + [keys_wide] * 2
GRAD_SHAPES = [struct((2, CHUNK, FEAT), F32)] + [struct((ROWS * PAIR, FEAT), F32)] * 2


def edge_gradients(*operands):
    return pl.pallas_call(
        edge_kernel,
        grid=(GROUPS,),
        in_specs=row_specs(EDGE) + [edge_turned_wide, any_spec, any_spec],
        out_specs=GRAD_SPECS + [edge_wide] * 2,
        out_shape=GRAD_SHAPES + [struct((2, PAIR, FEAT), BF16)] * 2,
        compiler_params=params(),
        cost_estimate=cost(3e9, 1 << 10),
        name="edge_gradients",
    )(*operands)


def mid_gradients(*operands):
    return pl.pallas_call(
        mid_kernel,
        grid=(GROUPS,),
        in_specs=row_specs(MID) + [keys_wide] * 2,
        out_specs=GRAD_SPECS,
        out_shape=GRAD_SHAPES,
        compiler_params=params(),
        cost_estimate=cost(3e9, 1 << 10),
        name="mid_gradients",
    )(*operands)


def join_columns(side_a, side_b):
    parts = ordered(side_a, side_b)
    return jnp.concatenate([part.reshape(8, 8, FEAT) for part in parts], axis=1).astype(BF16)


def finish_kernel(dq_edge, dq_mid, dk, dv, dq_0, dq_1, from_a, from_b,
                  q_ref, k_ref, v_ref, buffers, sems):
    copies = []

    def send(i, t, value):
        buffers[i, t] = value
        out = (q_ref, k_ref, v_ref)[i]
        copies.append(pltpu.make_async_copy(buffers.at[i, t], out.at[pl.ds(8 * grid_row(t), 8)], sems.at[i, t]))
        copies[-1].start()

    for t in range(ROWS):
        for which, own in enumerate((dk, dv)):
            full = own[t * PAIR:(t + 1) * PAIR]
            if t == 0:
                full = full + from_a[which].astype(F32)
            if t == ROWS - 1:
                full = full + from_b[which].astype(F32)
            send(1 + which, t, join_columns(full[:CELLS], full[CELLS:]))
    for place, t in enumerate(ORDER):
        dq = (dq_edge, dq_mid)[place // 2]
        at, there = at_tokens(place % 2), at_tokens(place)
        send(0, t, join_columns(dq[0, at] + dq_0[there].astype(F32), dq[1, at] + dq_1[there].astype(F32)))
    for copy in copies:
        copy.wait()


def finish(*operands):
    return pl.pallas_call(
        finish_kernel,
        out_specs=[any_spec] * 3,
        out_shape=[struct((8 * ROWS, 16, FEAT), BF16)] * 3,
        scratch_shapes=[pltpu.VMEM((3, ROWS, 8, 16, FEAT), BF16), pltpu.SemaphoreType.DMA((3, ROWS))],
        compiler_params=params(),
        cost_estimate=cost(0, 1 << 10),
        name="finish",
    )(*operands)


def swap_a(x, axis):
    return lax.ppermute(x, axis, [(i, i ^ 1) for i in range(lax.axis_size(axis))])


def swap_b(x, axis, wrap):
    count = lax.axis_size(axis)
    pairs = []
    for i in range(1, count if wrap else count - 1, 2):
        pairs += [(i, (i + 1) % count), ((i + 1) % count, i)]
    return lax.ppermute(x, axis, pairs)


def over_lon(side_0, side_1):
    return swap_b(side_0, "lon", True), swap_a(side_1, "lon")


def on_device(query_vectors, key_vectors, value_vectors, output_grads):
    *sides, own_edge_a, own_edge_b = pack_queries(query_vectors, output_grads, key_vectors, value_vectors)
    kd, vd = pack_keys(key_vectors, value_vectors)
    edge_b = swap_b(own_edge_b, "lat", False)
    halos = over_lon(*sides)
    edges = (swap_a(own_edge_a, "lat"), edge_b)
    mid_0, mid_1, *mid_own, turned = mid_scores(*sides, kd, vd)
    own_0, own_1, *edge_own = edge_scores(*sides, kd, vd, *edges, mid_0, mid_1)
    edges_turned = turn_edges(*edges)
    part_0, part_1, *rest = halo(*halos, kd, vd, *edges, *over_lon(own_0, own_1), turned, edges_turned)
    halo_dq, edge_weights, mid_weights = rest[:2], rest[2:4], rest[4:]
    stats = (own_0, own_1, *over_lon(part_0, part_1))
    dq_parts = over_lon(*halo_dq)
    shared = (*sides, *halos, *stats)
    dq_edge, dk, dv, out_a, out_b = edge_gradients(*shared, *edge_own, *edge_weights, turned, edges_turned, *halo_dq)
    key_parts = (swap_a(out_a, "lat"), swap_b(out_b, "lat", False))
    dq_mid, dk, dv = mid_gradients(*shared, *mid_own, *mid_weights, turned, dk, dv)
    return tuple(finish(dq_edge, dq_mid, dk, dv, *dq_parts, *key_parts))


def solution(mesh):
    spec = P("lat", "lon", None)
    return jax.shard_map(on_device, mesh=mesh, in_specs=(spec,) * 4, out_specs=(spec,) * 3, check_vma=False)
```

```python
import functools

import jax
import jax.numpy as jnp
from jax import lax
from jax.experimental import pallas as pl
from jax.experimental.pallas import tpu as pltpu
from jax.sharding import PartitionSpec as P

ROWS = 4
CELLS = 64
CHUNK = 2 * CELLS
PAIR = 128
WIDE = 256
PAIRS = 4
GROUPS = 2
FEAT = 512
SCALE = 64 ** -0.5
LOG2E = 1.4426950408889634
MASKED = -1e30
F32 = jnp.float32
BF16 = jnp.bfloat16
VMEM_LIMIT = 20 * 1024 * 1024
PACK_LIMIT = 62 * 1024 * 1024
any_spec = pl.BlockSpec(memory_space=pl.ANY)
EDGE_ROWS = (0, 3)
MID_ROWS = (1, 2)
ORDER = EDGE_ROWS + MID_ROWS
EDGE, MID = 0, 1


def matmul(a, b, contract):
    return lax.dot_general(a, b, ((contract[:1], contract[1:]), ((), ())), preferred_element_type=F32)


def params(limit=VMEM_LIMIT):
    return pltpu.CompilerParams(vmem_limit_bytes=limit)


def cost(flops, size):
    return pl.CostEstimate(flops=int(flops), bytes_accessed=int(size), transcendentals=0)


def struct(shape, dtype):
    return jax.ShapeDtypeStruct(shape, dtype)


def grid_row(t):
    return jnp.where(lax.axis_index("lat") % 2 == 0, ROWS - 1 - t, t)


def ordered(first, second):
    swap = lax.axis_index("lon") % 2 == 0
    return jnp.where(swap, second, first), jnp.where(swap, first, second)


def split_columns(block):
    wide = block.astype(F32)
    parts = ordered(*[wide[:, c * 8:(c + 1) * 8].reshape(CELLS, FEAT) for c in range(2)])
    return [part.astype(BF16) for part in parts]


def fetch(refs, rows, buffers, sems):
    copies = [[pltpu.make_async_copy(ref.at[pl.ds(8 * grid_row(t), 8)], buffers.at[i, place], sems.at[i, place])
               for place, t in enumerate(rows)] for i, ref in enumerate(refs)]
    for place in range(len(rows)):
        for copy in copies:
            copy[place].start()
    return copies


def key_tile(buffer):
    return jnp.concatenate(split_columns(buffer), axis=0)


def pack_queries_kernel(q_ref, g_ref, k_ref, v_ref, side_0, side_1, edge_a, edge_b, buffers, sems, key_buffers, key_sems,
                        packed, out_sems, packed_keys, key_out_sems):
    key_copies = fetch((k_ref, v_ref), EDGE_ROWS, key_buffers, key_sems)
    copies = fetch((q_ref, g_ref), ORDER, buffers, sems)
    sends = []

    def send(source, out, sem):
        sends.append(pltpu.make_async_copy(source, out, sem))
        sends[-1].start()

    for place, edge in enumerate((edge_a, edge_b)):
        for i in range(2):
            key_copies[i][place].wait()
            packed_keys[place, i] = key_tile(key_buffers[i, place])
            send(packed_keys.at[place, i], edge.at[i], key_out_sems.at[place, i])
    for place in range(ROWS):
        for i in range(2):
            copies[i][place].wait()
            for side, (value, out) in enumerate(zip(split_columns(buffers[i, place]), (side_0, side_1))):
                packed[side, i, place] = value
                send(packed.at[side, i, place], out.at[i, pl.ds(place * CELLS, CELLS)], out_sems.at[side, i, place])
    for copy in sends:
        copy.wait()


def pack_queries(*operands):
    return pl.pallas_call(
        pack_queries_kernel,
        in_specs=[any_spec] * 4,
        out_specs=[any_spec] * 4,
        out_shape=[struct((2, ROWS * CELLS, FEAT), BF16)] * 2 + [struct((2, PAIR, FEAT), BF16)] * 2,
        scratch_shapes=[
            pltpu.VMEM((2, ROWS, 8, 16, FEAT), BF16), pltpu.SemaphoreType.DMA((2, ROWS)),
            pltpu.VMEM((2, 2, 8, 16, FEAT), BF16), pltpu.SemaphoreType.DMA((2, 2)),
            pltpu.VMEM((2, 2, ROWS, CELLS, FEAT), BF16), pltpu.SemaphoreType.DMA((2, 2, ROWS)),
            pltpu.VMEM((2, 2, PAIR, FEAT), BF16), pltpu.SemaphoreType.DMA((2, 2)),
        ],
        compiler_params=params(PACK_LIMIT),
        cost_estimate=cost(0, 3 << 20),
        name="pack_queries",
    )(*operands)


def pack_keys_kernel(k_ref, v_ref, kd, vd, buffers, sems):
    copies = fetch((k_ref, v_ref), range(ROWS), buffers, sems)
    for t in range(ROWS):
        for i, out in enumerate((kd, vd)):
            copies[i][t].wait()
            out[t * PAIR:(t + 1) * PAIR] = key_tile(buffers[i, t])


def pack_keys(*operands):
    return pl.pallas_call(
        pack_keys_kernel,
        in_specs=[any_spec] * 2,
        out_shape=[struct((ROWS * PAIR, FEAT), BF16)] * 2,
        scratch_shapes=[pltpu.VMEM((2, ROWS, 8, 16, FEAT), BF16), pltpu.SemaphoreType.DMA((2, ROWS))],
        compiler_params=params(),
        cost_estimate=cost(0, 3 << 20),
        name="pack_keys",
    )(*operands)


def head_masks(lanes):
    lane = lax.broadcasted_iota(jnp.int32, (1, lanes), 1)
    return [jnp.where((lane >= 64 * h) & (lane < 64 * (h + 1)), 1.0, 0.0).astype(F32).astype(BF16)
            for h in range(lanes // 64)]


def stacked(parts, masks):
    return jnp.concatenate([part * mask for part in parts for mask in masks], axis=0)


def key_rows(own, edges, which, t, lanes=slice(None)):
    rows = []
    for row in range(t, t + 3):
        if row == 0:
            rows.append(edges[0][which, :, lanes])
        elif row == ROWS + 1:
            rows.append(edges[1][which, :, lanes])
        else:
            rows.append(own[(row - 1) * PAIR:row * PAIR, lanes])
    return rows


def window(*where):
    return jnp.concatenate(key_rows(*where), axis=0)


def column_window(column, *where):
    return jnp.concatenate([row[column * CELLS:(column + 1) * CELLS] for row in key_rows(*where)], axis=0)


def score_block(keys, queries, t):
    scores = matmul(keys, queries, (1, 1)) * (SCALE * LOG2E)
    if t == ROWS - 1:
        lat = lax.axis_index("lat")
        outside = (lat == 0) | (lat == lax.axis_size("lat") - 1)
        cut = 2 * (keys.shape[0] // 3)
        bias = jnp.where(outside, MASKED, 0.0).astype(F32)
        scores = jnp.concatenate([scores[:cut], scores[cut:] + bias], axis=0)
    return scores


def row_stats(scores, dprobs):
    top = jnp.max(scores, axis=0, keepdims=True)
    weights = jnp.exp2(scores - top)
    total = jnp.sum(weights, axis=0, keepdims=True)
    delta = jnp.sum(weights * dprobs, axis=0, keepdims=True) / total
    return top + jnp.log(total) * LOG2E, delta


def merged(log_a, delta_a, log_b, delta_b):
    top = jnp.maximum(log_a, log_b)
    weight_a = jnp.exp2(log_a - top)
    weight_b = jnp.exp2(log_b - top)
    total = weight_a + weight_b
    return top + jnp.log(total) * LOG2E, (weight_a * delta_a + weight_b * delta_b) / total


def both_parts(mine, theirs, pair, base):
    other = 4 - base
    return merged(mine[pair, base:base + 2], mine[pair, base + 2:base + 4],
                  theirs[pair, other:other + 2], theirs[pair, other + 2:other + 4])


def turned_window(own_turned, edges_turned, t, j):
    at = slice(j * PAIR, (j + 1) * PAIR)
    rows = []
    for row in range(t, t + 3):
        if row in (0, ROWS + 1):
            rows.append(edges_turned[row // (ROWS + 1), at])
        else:
            rows.append(own_turned[at, (row - 1) * PAIR:row * PAIR])
    return jnp.concatenate(rows, axis=1)


def query_parts(keys_turned, dscores, lane):
    turned = matmul(keys_turned, dscores, (1, 0)) * SCALE
    parts = [turned[:, c * PAIR:(c + 1) * PAIR].T for c in range(2)]
    return [jnp.where(lane < 64, part[:CELLS], part[CELLS:]) for part in parts]


def at_tokens(place):
    return slice(place * CELLS, (place + 1) * CELLS)


def pair_lanes(j):
    return slice(j * PAIR, (j + 1) * PAIR)


def tokens_spec(group):
    return pl.BlockSpec((2, CHUNK, PAIR), lambda p: (0, group, p))


keys_spec = pl.BlockSpec((ROWS * PAIR, PAIR), lambda p: (0, p))
edge_spec = pl.BlockSpec((2, PAIR, PAIR), lambda p: (0, 0, p))
part_spec = pl.BlockSpec((1, 8, PAIR), lambda p: (p, 0, 0))
held_spec = pl.BlockSpec((1, 2, 3 * PAIR, WIDE), lambda p: (p, 0, 0, 0))
part_shape = struct((PAIRS, 8, PAIR), F32)
stats_shape = struct((PAIRS, 16, PAIR), F32)
held_shape = struct((PAIRS, 2, 3 * PAIR, WIDE), F32)


def tokens_wide(group):
    return pl.BlockSpec((2, CHUNK, WIDE), lambda g: (0, group, g))


def stats_wide(group):
    return pl.BlockSpec((2, 8, PAIR), lambda g: (g, group, 0))


all_tokens = pl.BlockSpec((2, 2 * CHUNK, WIDE), lambda g: (0, 0, g))
all_stats = pl.BlockSpec((2, 16, PAIR), lambda g: (g, 0, 0))
all_parts = pl.BlockSpec((2 * CHUNK, WIDE), lambda g: (0, g))
sums_wide = pl.BlockSpec((2, CHUNK, WIDE), lambda g: (0, 0, g))
keys_wide = pl.BlockSpec((ROWS * PAIR, WIDE), lambda g: (0, g))
edge_wide = pl.BlockSpec((2, PAIR, WIDE), lambda g: (0, 0, g))
turned_wide = pl.BlockSpec((WIDE, ROWS * PAIR), lambda g: (g, 0))
edge_turned_wide = pl.BlockSpec((2, WIDE, PAIR), lambda g: (0, g, 0))
held_wide = pl.BlockSpec((2, 2, 3 * PAIR, WIDE), lambda g: (g, 0, 0, 0))
halo_wide = pl.BlockSpec((1, 2, 3 * CELLS, WIDE), lambda g: (g, 0, 0, 0))
halo_shape = struct((GROUPS, 2, 3 * CELLS, WIDE), F32)
weight_shape = struct((GROUPS, 2, 3 * CELLS, WIDE), BF16)


def own_scores(rows, side_a, side_b, kd, vd, edges, part, s_out, d_out):
    masks = head_masks(PAIR)
    for place, t in enumerate(rows):
        at = at_tokens(place)
        queries = stacked([side_a[0, at], side_b[0, at]], masks)
        grads = stacked([side_a[1, at], side_b[1, at]], masks)
        scores = score_block(window(kd, edges, 0, t), queries, t)
        dprobs = matmul(window(vd, edges, 1, t), grads, (1, 1))
        s_out[0, place] = scores
        d_out[0, place] = dprobs
        for w, values in enumerate(row_stats(scores, dprobs)):
            for c in range(2):
                index = 4 * c + 2 * w + place
                part[0, index:index + 1] = values[:, pair_lanes(c)]


def mid_scores_kernel(side_0, side_1, kd, vd, part, s_out, d_out, turned):
    own_scores(MID_ROWS, side_0, side_1, kd, vd, None, part, s_out, d_out)
    turned[...] = kd[...].T


def edge_scores_kernel(side_0, side_1, kd, vd, edge_a, edge_b, part, s_out, d_out):
    own_scores(EDGE_ROWS, side_0, side_1, kd, vd, (edge_a, edge_b), part, s_out, d_out)


def mid_scores(*operands):
    return pl.pallas_call(
        mid_scores_kernel,
        grid=(PAIRS,),
        in_specs=[tokens_spec(MID)] * 2 + [keys_spec] * 2,
        out_specs=[part_spec] + [held_spec] * 2 + [pl.BlockSpec((PAIR, ROWS * PAIR), lambda p: (p, 0))],
        out_shape=[part_shape] + [held_shape] * 2 + [struct((FEAT, ROWS * PAIR), BF16)],
        compiler_params=params(),
        cost_estimate=cost(2e9, 1 << 10),
        name="mid_scores",
    )(*operands)


def edge_scores(*operands):
    return pl.pallas_call(
        edge_scores_kernel,
        grid=(PAIRS,),
        in_specs=[tokens_spec(EDGE)] * 2 + [keys_spec] * 2 + [edge_spec] * 2,
        out_specs=[part_spec] + [held_spec] * 2,
        out_shape=[part_shape] + [held_shape] * 2,
        compiler_params=params(),
        cost_estimate=cost(2e9, 1 << 10),
        name="edge_scores",
    )(*operands)


def turn_edges_kernel(edge_a, edge_b, turned):
    turned[0] = edge_a[0].T
    turned[1] = edge_b[0].T


def turn_edges(*operands):
    return pl.pallas_call(
        turn_edges_kernel,
        grid=(PAIRS,),
        in_specs=[edge_spec] * 2,
        out_specs=pl.BlockSpec((2, PAIR, PAIR), lambda p: (0, p, 0)),
        out_shape=struct((2, FEAT, PAIR), BF16),
        compiler_params=params(),
        cost_estimate=cost(1e9, 1 << 10),
        name="turn_edges",
    )(*operands)


def halo_scores_kernel(c, q_in, kd, vd, edge_a, edge_b, edge_part, mid_part, send, s_edge, d_edge, s_mid, d_mid):
    masks = head_masks(WIDE)
    groups = ((EDGE_ROWS, edge_part, s_edge, d_edge), (MID_ROWS, mid_part, s_mid, d_mid))
    for group, (rows, part, s_out, d_out) in enumerate(groups):
        base = 8 * group
        for j in range(2):
            send[j, base:base + 4] = part[j, 4 * c:4 * c + 4]
        for place, t in enumerate(rows):
            at = at_tokens(2 * group + place)
            queries = stacked([q_in[0, at]], masks)
            grads = stacked([q_in[1, at]], masks)
            scores = score_block(column_window(c, kd, (edge_a, edge_b), 0, t), queries, t)
            dprobs = matmul(column_window(c, vd, (edge_a, edge_b), 1, t), grads, (1, 1))
            s_out[0, place] = scores
            d_out[0, place] = dprobs
            for w, values in enumerate(row_stats(scores, dprobs)):
                index = base + 4 + 2 * w + place
                for j in range(2):
                    send[j, index:index + 1] = values[:, pair_lanes(j)]


def halo_scores(c, *operands):
    part = pl.BlockSpec((2, 8, PAIR), lambda g: (g, 0, 0))
    return pl.pallas_call(
        functools.partial(halo_scores_kernel, c),
        grid=(GROUPS,),
        in_specs=[all_tokens] + [keys_wide] * 2 + [edge_wide] * 2 + [part] * 2,
        out_specs=[all_stats] + [halo_wide] * 4,
        out_shape=[stats_shape] + [halo_shape] * 4,
        compiler_params=params(),
        cost_estimate=cost(2e9, 1 << 10),
        name="halo_scores_" + "ab"[c],
    )(*operands)


def halo_queries_kernel(c, send, recv, s_edge, d_edge, s_mid, d_mid, own_turned, edges_turned,
                        out, p_edge, ds_edge, p_mid, ds_mid):
    lane = lax.broadcasted_iota(jnp.int32, (1, PAIR), 1)
    none = jnp.zeros((CELLS, PAIR), BF16)
    groups = ((EDGE_ROWS, s_edge, d_edge, p_edge, ds_edge), (MID_ROWS, s_mid, d_mid, p_mid, ds_mid))
    for group, (rows, s_in, d_in, p_out, ds_out) in enumerate(groups):
        mine, theirs = [ref.at[:, pl.ds(8 * group, 8)] for ref in (send, recv)]
        both = [both_parts(mine, theirs, j, 4) for j in range(2)]
        log_total, delta = [jnp.concatenate([one[w] for one in both], axis=1) for w in range(2)]
        for place, t in enumerate(rows):
            probs = jnp.exp2(s_in[0, place] - log_total[place:place + 1])
            dscores = (probs * (d_in[0, place] - delta[place:place + 1])).astype(BF16)
            p_out[0, place] = probs.astype(BF16)
            ds_out[0, place] = dscores
            for j in range(2):
                pieces = []
                for i in range(3):
                    part = dscores[at_tokens(i), pair_lanes(j)]
                    pieces += [none, part] if c else [part, none]
                turned = matmul(turned_window(own_turned, edges_turned, t, j), jnp.concatenate(pieces, axis=0), (1, 0))
                grad = turned.T * SCALE
                out[at_tokens(2 * group + place), pair_lanes(j)] = jnp.where(lane < 64, grad[:CELLS], grad[CELLS:]).astype(BF16)


def halo_queries(c, *operands):
    return pl.pallas_call(
        functools.partial(halo_queries_kernel, c),
        grid=(GROUPS,),
        in_specs=[all_stats] * 2 + [halo_wide] * 4 + [turned_wide, edge_turned_wide],
        out_specs=[all_parts] + [halo_wide] * 4,
        out_shape=[struct((2 * CHUNK, FEAT), BF16)] + [weight_shape] * 4,
        compiler_params=params(),
        cost_estimate=cost(2e9, 1 << 10),
        name="halo_queries_" + "ab"[c],
    )(*operands)


def row_gradients(rows, side_0, side_1, q_0, q_1, send_0, send_1, recv_0, recv_1, s_own, d_own, p_0, ds_0, p_1, ds_1,
                  own_turned, edges_turned, dq_ref):
    masks, wide_masks = head_masks(PAIR), head_masks(WIDE)
    lane = lax.broadcasted_iota(jnp.int32, (1, PAIR), 1)
    merged_rows = []
    for j in range(2):
        both = [both_parts(send_0, recv_0, j, 0), both_parts(send_1, recv_1, j, 0)]
        merged_rows.append([jnp.concatenate([one[w] for one in both], axis=1) for w in range(2)])
    results = []
    for place, t in enumerate(rows):
        at, row = at_tokens(place), slice(place, place + 1)
        sums = [[], []]
        for j in range(2):
            lanes = pair_lanes(j)
            queries = stacked([side_0[0, at, lanes], side_1[0, at, lanes]], masks)
            grads = stacked([side_0[1, at, lanes], side_1[1, at, lanes]], masks)
            log_total, delta = merged_rows[j]
            probs = jnp.exp2(s_own[j, place] - log_total[row])
            dscores = (probs * (d_own[j, place] - delta[row])).astype(BF16)
            for c, part in enumerate(query_parts(turned_window(own_turned, edges_turned, t, j), dscores, lane)):
                dq_ref[c, at, lanes] = part
            sums[0].append(matmul(dscores, queries, (1, 0)))
            sums[1].append(matmul(probs.astype(BF16), grads, (1, 0)))
        sums = [jnp.concatenate(parts, axis=1) for parts in sums]
        edge_parts = []
        for q_in, p_halo, ds_halo in ((q_0, p_0, ds_0), (q_1, p_1, ds_1)):
            edge_parts.append((matmul(ds_halo[0, place], stacked([q_in[0, at]], wide_masks), (1, 0)),
                               matmul(p_halo[0, place], stacked([q_in[1, at]], wide_masks), (1, 0))))
        results.append([jnp.concatenate([sums[w][at_tokens(2 * i + c)] + edge_parts[c][w][at_tokens(i)]
                                         for i in range(3) for c in range(2)], axis=0) for w in range(2)])
    return results


def edge_kernel(*refs):
    operands, (_, _, dq_ref, dk_ref, dv_ref, out_a, out_b) = refs[:16], refs[16:]
    upper, lower = row_gradients(EDGE_ROWS, *operands, dq_ref)
    for which, (out, scale) in enumerate(((dk_ref, SCALE), (dv_ref, 1.0))):
        top, bottom = upper[which] * scale, lower[which] * scale
        out_a[which] = top[:PAIR].astype(BF16)
        out[0:2 * PAIR] = top[PAIR:]
        out_b[which] = bottom[2 * PAIR:].astype(BF16)
        out[2 * PAIR:] = bottom[:2 * PAIR]


def mid_kernel(*refs):
    operands, (dk_in, dv_in, dq_ref, dk_ref, dv_ref) = refs[:15], refs[15:]
    upper, lower = row_gradients(MID_ROWS, *operands, None, dq_ref)
    for which, (sums, out, scale) in enumerate(((dk_in, dk_ref, SCALE), (dv_in, dv_ref, 1.0))):
        out[0:PAIR] = sums[0:PAIR] + upper[which][:PAIR] * scale
        out[PAIR:3 * PAIR] = sums[PAIR:3 * PAIR] + (upper[which][PAIR:] + lower[which][:2 * PAIR]) * scale
        out[3 * PAIR:] = sums[3 * PAIR:] + lower[which][2 * PAIR:] * scale


def row_specs(group):
    return ([tokens_wide(group)] * 4 + [stats_wide(group)] * 4 + [held_wide] * 2 + [halo_wide] * 4 + [turned_wide])


GRAD_SPECS = [sums_wide] + [keys_wide] * 2
GRAD_SHAPES = [struct((2, CHUNK, FEAT), F32)] + [struct((ROWS * PAIR, FEAT), F32)] * 2


def edge_gradients(*operands):
    return pl.pallas_call(
        edge_kernel,
        grid=(GROUPS,),
        in_specs=row_specs(EDGE) + [edge_turned_wide, any_spec, any_spec],
        out_specs=GRAD_SPECS + [edge_wide] * 2,
        out_shape=GRAD_SHAPES + [struct((2, PAIR, FEAT), BF16)] * 2,
        compiler_params=params(),
        cost_estimate=cost(3e9, 1 << 10),
        name="edge_gradients",
    )(*operands)


def mid_gradients(*operands):
    return pl.pallas_call(
        mid_kernel,
        grid=(GROUPS,),
        in_specs=row_specs(MID) + [keys_wide] * 2,
        out_specs=GRAD_SPECS,
        out_shape=GRAD_SHAPES,
        compiler_params=params(),
        cost_estimate=cost(3e9, 1 << 10),
        name="mid_gradients",
    )(*operands)


def join_columns(side_a, side_b):
    parts = ordered(side_a, side_b)
    return jnp.concatenate([part.reshape(8, 8, FEAT) for part in parts], axis=1).astype(BF16)


def finish_kernel(dq_edge, dq_mid, dk, dv, dq_0, dq_1, from_a, from_b,
                  q_ref, k_ref, v_ref, buffers, sems):
    copies = []

    def send(i, t, value):
        buffers[i, t] = value
        out = (q_ref, k_ref, v_ref)[i]
        copies.append(pltpu.make_async_copy(buffers.at[i, t], out.at[pl.ds(8 * grid_row(t), 8)], sems.at[i, t]))
        copies[-1].start()

    for t in range(ROWS):
        for which, own in enumerate((dk, dv)):
            full = own[t * PAIR:(t + 1) * PAIR]
            if t == 0:
                full = full + from_a[which].astype(F32)
            if t == ROWS - 1:
                full = full + from_b[which].astype(F32)
            send(1 + which, t, join_columns(full[:CELLS], full[CELLS:]))
    for place, t in enumerate(ORDER):
        dq = (dq_edge, dq_mid)[place // 2]
        at, there = at_tokens(place % 2), at_tokens(place)
        send(0, t, join_columns(dq[0, at] + dq_0[there].astype(F32), dq[1, at] + dq_1[there].astype(F32)))
    for copy in copies:
        copy.wait()


def finish(*operands):
    return pl.pallas_call(
        finish_kernel,
        out_specs=[any_spec] * 3,
        out_shape=[struct((8 * ROWS, 16, FEAT), BF16)] * 3,
        scratch_shapes=[pltpu.VMEM((3, ROWS, 8, 16, FEAT), BF16), pltpu.SemaphoreType.DMA((3, ROWS))],
        compiler_params=params(),
        cost_estimate=cost(0, 1 << 10),
        name="finish",
    )(*operands)


def swap_a(x, axis):
    return lax.ppermute(x, axis, [(i, i ^ 1) for i in range(lax.axis_size(axis))])


def swap_b(x, axis, wrap):
    count = lax.axis_size(axis)
    pairs = []
    for i in range(1, count if wrap else count - 1, 2):
        pairs += [(i, (i + 1) % count), ((i + 1) % count, i)]
    return lax.ppermute(x, axis, pairs)


def swap_lon(c, x):
    return swap_b(x, "lon", True) if c else swap_a(x, "lon")


def on_device(query_vectors, key_vectors, value_vectors, output_grads):
    *sides, own_edge_a, own_edge_b = pack_queries(query_vectors, output_grads, key_vectors, value_vectors)
    kd, vd = pack_keys(key_vectors, value_vectors)
    edge_b = swap_b(own_edge_b, "lat", False)
    halos = [swap_lon(c, side) for c, side in enumerate(sides)]
    edges = (swap_a(own_edge_a, "lat"), edge_b)
    mid_part, *mid_own, turned = mid_scores(*sides, kd, vd)
    edge_part, *edge_own = edge_scores(*sides, kd, vd, *edges)
    edges_turned = turn_edges(*edges)
    sends, recvs, halo_dq, dq_parts, weights = [], [], [], [], []
    for c in range(2):
        send, *held = halo_scores(c, halos[c], kd, vd, *edges, edge_part, mid_part)
        recv = swap_lon(c, send)
        grad, *weight = halo_queries(c, send, recv, *held, turned, edges_turned)
        sends.append(send)
        recvs.append(recv)
        halo_dq.append(grad)
        dq_parts.append(swap_lon(c, grad))
        weights.append(weight)
    shared = (*sides, *halos, *sends, *recvs)
    dq_edge, dk, dv, out_a, out_b = edge_gradients(*shared, *edge_own, *weights[0][:2], *weights[1][:2], turned, edges_turned,
                                                   *halo_dq)
    key_parts = (swap_a(out_a, "lat"), swap_b(out_b, "lat", False))
    dq_mid, dk, dv = mid_gradients(*shared, *mid_own, *weights[0][2:], *weights[1][2:], turned, dk, dv)
    return tuple(finish(dq_edge, dq_mid, dk, dv, *dq_parts, *key_parts))


def solution(mesh):
    spec = P("lat", "lon", None)
    return jax.shard_map(on_device, mesh=mesh, in_specs=(spec,) * 4, out_specs=(spec,) * 3, check_vma=False)
```

```python
import functools

import jax
import jax.numpy as jnp
from jax import lax
from jax.experimental import pallas as pl
from jax.experimental.pallas import tpu as pltpu
from jax.sharding import PartitionSpec as P

ROWS = 4
CELLS = 64
CHUNK = 2 * CELLS
PAIR = 128
WIDE = 256
PAIRS = 4
GROUPS = 2
FEAT = 512
SCALE = 64 ** -0.5
LOG2E = 1.4426950408889634
MASKED = -1e30
F32 = jnp.float32
BF16 = jnp.bfloat16
VMEM_LIMIT = 20 * 1024 * 1024
PACK_LIMIT = 62 * 1024 * 1024
any_spec = pl.BlockSpec(memory_space=pl.ANY)
EDGE_ROWS = (0, 3)
MID_ROWS = (1, 2)
ORDER = EDGE_ROWS + MID_ROWS
EDGE, MID = 0, 1


def matmul(a, b, contract):
    return lax.dot_general(a, b, ((contract[:1], contract[1:]), ((), ())), preferred_element_type=F32)


def params(limit=VMEM_LIMIT):
    return pltpu.CompilerParams(vmem_limit_bytes=limit)


def cost(flops, size):
    return pl.CostEstimate(flops=int(flops), bytes_accessed=int(size), transcendentals=0)


def struct(shape, dtype):
    return jax.ShapeDtypeStruct(shape, dtype)


def grid_row(t):
    return jnp.where(lax.axis_index("lat") % 2 == 0, ROWS - 1 - t, t)


def ordered(first, second):
    swap = lax.axis_index("lon") % 2 == 0
    return jnp.where(swap, second, first), jnp.where(swap, first, second)


def split_columns(block):
    wide = block.astype(F32)
    parts = ordered(*[wide[:, c * 8:(c + 1) * 8].reshape(CELLS, FEAT) for c in range(2)])
    return [part.astype(BF16) for part in parts]


def fetch(refs, rows, buffers, sems):
    copies = [[pltpu.make_async_copy(ref.at[pl.ds(8 * grid_row(t), 8)], buffers.at[i, place], sems.at[i, place])
               for place, t in enumerate(rows)] for i, ref in enumerate(refs)]
    for place in range(len(rows)):
        for copy in copies:
            copy[place].start()
    return copies


def key_tile(buffer):
    return jnp.concatenate(split_columns(buffer), axis=0)


def pack_queries_kernel(q_ref, g_ref, k_ref, v_ref, side_0, side_1, edge_a, edge_b, buffers, sems, key_buffers, key_sems,
                        packed, out_sems, packed_keys, key_out_sems):
    key_copies = fetch((k_ref, v_ref), EDGE_ROWS, key_buffers, key_sems)
    copies = fetch((q_ref, g_ref), ORDER, buffers, sems)
    sends = []

    def send(source, out, sem):
        sends.append(pltpu.make_async_copy(source, out, sem))
        sends[-1].start()

    for place, edge in enumerate((edge_a, edge_b)):
        for i in range(2):
            key_copies[i][place].wait()
            packed_keys[place, i] = key_tile(key_buffers[i, place])
            send(packed_keys.at[place, i], edge.at[i], key_out_sems.at[place, i])
    for place in range(ROWS):
        for i in range(2):
            copies[i][place].wait()
            for side, (value, out) in enumerate(zip(split_columns(buffers[i, place]), (side_0, side_1))):
                packed[side, i, place] = value
                send(packed.at[side, i, place], out.at[i, pl.ds(place * CELLS, CELLS)], out_sems.at[side, i, place])
    for copy in sends:
        copy.wait()


def pack_queries(*operands):
    return pl.pallas_call(
        pack_queries_kernel,
        in_specs=[any_spec] * 4,
        out_specs=[any_spec] * 4,
        out_shape=[struct((2, ROWS * CELLS, FEAT), BF16)] * 2 + [struct((2, PAIR, FEAT), BF16)] * 2,
        scratch_shapes=[
            pltpu.VMEM((2, ROWS, 8, 16, FEAT), BF16), pltpu.SemaphoreType.DMA((2, ROWS)),
            pltpu.VMEM((2, 2, 8, 16, FEAT), BF16), pltpu.SemaphoreType.DMA((2, 2)),
            pltpu.VMEM((2, 2, ROWS, CELLS, FEAT), BF16), pltpu.SemaphoreType.DMA((2, 2, ROWS)),
            pltpu.VMEM((2, 2, PAIR, FEAT), BF16), pltpu.SemaphoreType.DMA((2, 2)),
        ],
        compiler_params=params(PACK_LIMIT),
        cost_estimate=cost(0, 3 << 20),
        name="pack_queries",
    )(*operands)


def pack_keys_kernel(k_ref, v_ref, kd, vd, buffers, sems):
    copies = fetch((k_ref, v_ref), range(ROWS), buffers, sems)
    for t in range(ROWS):
        for i, out in enumerate((kd, vd)):
            copies[i][t].wait()
            out[t * PAIR:(t + 1) * PAIR] = key_tile(buffers[i, t])


def pack_keys(*operands):
    return pl.pallas_call(
        pack_keys_kernel,
        in_specs=[any_spec] * 2,
        out_shape=[struct((ROWS * PAIR, FEAT), BF16)] * 2,
        scratch_shapes=[pltpu.VMEM((2, ROWS, 8, 16, FEAT), BF16), pltpu.SemaphoreType.DMA((2, ROWS))],
        compiler_params=params(),
        cost_estimate=cost(0, 3 << 20),
        name="pack_keys",
    )(*operands)


def head_masks(lanes):
    lane = lax.broadcasted_iota(jnp.int32, (1, lanes), 1)
    return [jnp.where((lane >= 64 * h) & (lane < 64 * (h + 1)), 1.0, 0.0).astype(F32).astype(BF16)
            for h in range(lanes // 64)]


def stacked(parts, masks):
    return jnp.concatenate([part * mask for part in parts for mask in masks], axis=0)


def key_rows(own, edges, which, t, lanes=slice(None)):
    rows = []
    for row in range(t, t + 3):
        if row == 0:
            rows.append(edges[0][which, :, lanes])
        elif row == ROWS + 1:
            rows.append(edges[1][which, :, lanes])
        else:
            rows.append(own[(row - 1) * PAIR:row * PAIR, lanes])
    return rows


def window(*where):
    return jnp.concatenate(key_rows(*where), axis=0)


def column_window(column, *where):
    return jnp.concatenate([row[column * CELLS:(column + 1) * CELLS] for row in key_rows(*where)], axis=0)


def score_block(keys, queries, t):
    scores = matmul(keys, queries, (1, 1)) * (SCALE * LOG2E)
    if t == ROWS - 1:
        lat = lax.axis_index("lat")
        outside = (lat == 0) | (lat == lax.axis_size("lat") - 1)
        cut = 2 * (keys.shape[0] // 3)
        bias = jnp.where(outside, MASKED, 0.0).astype(F32)
        scores = jnp.concatenate([scores[:cut], scores[cut:] + bias], axis=0)
    return scores


def row_stats(scores, dprobs):
    top = jnp.max(scores, axis=0, keepdims=True)
    weights = jnp.exp2(scores - top)
    total = jnp.sum(weights, axis=0, keepdims=True)
    delta = jnp.sum(weights * dprobs, axis=0, keepdims=True) / total
    return top + jnp.log(total) * LOG2E, delta


def merged(log_a, delta_a, log_b, delta_b):
    top = jnp.maximum(log_a, log_b)
    weight_a = jnp.exp2(log_a - top)
    weight_b = jnp.exp2(log_b - top)
    total = weight_a + weight_b
    return top + jnp.log(total) * LOG2E, (weight_a * delta_a + weight_b * delta_b) / total


def both_parts(mine, theirs, pair, base):
    other = 4 - base
    return merged(mine[pair, base:base + 2], mine[pair, base + 2:base + 4],
                  theirs[pair, other:other + 2], theirs[pair, other + 2:other + 4])


def turned_window(own_turned, edges_turned, t, j):
    at = slice(j * PAIR, (j + 1) * PAIR)
    rows = []
    for row in range(t, t + 3):
        if row in (0, ROWS + 1):
            rows.append(edges_turned[row // (ROWS + 1), at])
        else:
            rows.append(own_turned[at, (row - 1) * PAIR:row * PAIR])
    return jnp.concatenate(rows, axis=1)


def query_parts(keys_turned, dscores, lane):
    turned = matmul(keys_turned, dscores, (1, 0)) * SCALE
    parts = [turned[:, c * PAIR:(c + 1) * PAIR].T for c in range(2)]
    return [jnp.where(lane < 64, part[:CELLS], part[CELLS:]) for part in parts]


def at_tokens(place):
    return slice(place * CELLS, (place + 1) * CELLS)


def pair_lanes(j):
    return slice(j * PAIR, (j + 1) * PAIR)


def tokens_spec(group):
    return pl.BlockSpec((2, CHUNK, PAIR), lambda p: (0, group, p))


keys_spec = pl.BlockSpec((ROWS * PAIR, PAIR), lambda p: (0, p))
edge_spec = pl.BlockSpec((2, PAIR, PAIR), lambda p: (0, 0, p))
part_spec = pl.BlockSpec((1, 8, PAIR), lambda p: (p, 0, 0))
held_spec = pl.BlockSpec((1, 2, 3 * PAIR, WIDE), lambda p: (p, 0, 0, 0))
part_shape = struct((PAIRS, 8, PAIR), F32)
stats_shape = struct((PAIRS, 16, PAIR), F32)
held_shape = struct((PAIRS, 2, 3 * PAIR, WIDE), F32)


def tokens_wide(group):
    return pl.BlockSpec((2, CHUNK, WIDE), lambda g: (0, group, g))


def stats_wide(group):
    return pl.BlockSpec((2, 8, PAIR), lambda g: (g, group, 0))


all_tokens = pl.BlockSpec((2, 2 * CHUNK, WIDE), lambda g: (0, 0, g))
all_stats = pl.BlockSpec((2, 16, PAIR), lambda g: (g, 0, 0))
all_parts = pl.BlockSpec((2 * CHUNK, WIDE), lambda g: (0, g))
sums_wide = pl.BlockSpec((2, CHUNK, WIDE), lambda g: (0, 0, g))
keys_wide = pl.BlockSpec((ROWS * PAIR, WIDE), lambda g: (0, g))
edge_wide = pl.BlockSpec((2, PAIR, WIDE), lambda g: (0, 0, g))
turned_wide = pl.BlockSpec((WIDE, ROWS * PAIR), lambda g: (g, 0))
edge_turned_wide = pl.BlockSpec((2, WIDE, PAIR), lambda g: (0, g, 0))
held_wide = pl.BlockSpec((2, 2, 3 * PAIR, WIDE), lambda g: (g, 0, 0, 0))
halo_wide = pl.BlockSpec((1, 2, 3 * CELLS, WIDE), lambda g: (g, 0, 0, 0))
halo_shape = struct((GROUPS, 2, 3 * CELLS, WIDE), F32)
weight_shape = struct((GROUPS, 2, 3 * CELLS, WIDE), BF16)


def own_scores(rows, side_a, side_b, kd, vd, edges, part, s_out, d_out):
    masks = head_masks(PAIR)
    for place, t in enumerate(rows):
        at = at_tokens(place)
        queries = stacked([side_a[0, at], side_b[0, at]], masks)
        grads = stacked([side_a[1, at], side_b[1, at]], masks)
        scores = score_block(window(kd, edges, 0, t), queries, t)
        dprobs = matmul(window(vd, edges, 1, t), grads, (1, 1))
        s_out[0, place] = scores
        d_out[0, place] = dprobs
        for w, values in enumerate(row_stats(scores, dprobs)):
            for c in range(2):
                index = 4 * c + 2 * w + place
                part[0, index:index + 1] = values[:, pair_lanes(c)]


def mid_scores_kernel(side_0, side_1, kd, vd, part, s_out, d_out, turned):
    own_scores(MID_ROWS, side_0, side_1, kd, vd, None, part, s_out, d_out)
    turned[...] = kd[...].T


def edge_scores_kernel(side_0, side_1, kd, vd, edge_a, edge_b, part, s_out, d_out):
    own_scores(EDGE_ROWS, side_0, side_1, kd, vd, (edge_a, edge_b), part, s_out, d_out)


def mid_scores(*operands):
    return pl.pallas_call(
        mid_scores_kernel,
        grid=(PAIRS,),
        in_specs=[tokens_spec(MID)] * 2 + [keys_spec] * 2,
        out_specs=[part_spec] + [held_spec] * 2 + [pl.BlockSpec((PAIR, ROWS * PAIR), lambda p: (p, 0))],
        out_shape=[part_shape] + [held_shape] * 2 + [struct((FEAT, ROWS * PAIR), BF16)],
        compiler_params=params(),
        cost_estimate=cost(6e9, 1 << 10),
        name="mid_scores",
    )(*operands)


def edge_scores(*operands):
    return pl.pallas_call(
        edge_scores_kernel,
        grid=(PAIRS,),
        in_specs=[tokens_spec(EDGE)] * 2 + [keys_spec] * 2 + [edge_spec] * 2,
        out_specs=[part_spec] + [held_spec] * 2,
        out_shape=[part_shape] + [held_shape] * 2,
        compiler_params=params(),
        cost_estimate=cost(2e9, 1 << 10),
        name="edge_scores",
    )(*operands)


def turn_edges_kernel(edge_a, edge_b, turned):
    turned[0] = edge_a[0].T
    turned[1] = edge_b[0].T


def turn_edges(*operands):
    return pl.pallas_call(
        turn_edges_kernel,
        grid=(PAIRS,),
        in_specs=[edge_spec] * 2,
        out_specs=pl.BlockSpec((2, PAIR, PAIR), lambda p: (0, p, 0)),
        out_shape=struct((2, FEAT, PAIR), BF16),
        compiler_params=params(),
        cost_estimate=cost(1e9, 1 << 10),
        name="turn_edges",
    )(*operands)


def halo_scores_kernel(c, q_in, kd, vd, edge_a, edge_b, edge_part, mid_part, *refs):
    send, s_edge, d_edge, s_mid, d_mid = refs[-5:]
    masks = head_masks(WIDE)
    groups = ((EDGE_ROWS, edge_part, s_edge, d_edge), (MID_ROWS, mid_part, s_mid, d_mid))
    for group, (rows, part, s_out, d_out) in enumerate(groups):
        base = 8 * group
        for j in range(2):
            send[j, base:base + 4] = part[j, 4 * c:4 * c + 4]
        for place, t in enumerate(rows):
            at = at_tokens(2 * group + place)
            queries = stacked([q_in[0, at]], masks)
            grads = stacked([q_in[1, at]], masks)
            scores = score_block(column_window(c, kd, (edge_a, edge_b), 0, t), queries, t)
            dprobs = matmul(column_window(c, vd, (edge_a, edge_b), 1, t), grads, (1, 1))
            s_out[0, place] = scores
            d_out[0, place] = dprobs
            for w, values in enumerate(row_stats(scores, dprobs)):
                index = base + 4 + 2 * w + place
                for j in range(2):
                    send[j, index:index + 1] = values[:, pair_lanes(j)]


def halo_scores(c, *operands):
    part = pl.BlockSpec((2, 8, PAIR), lambda g: (g, 0, 0))
    return pl.pallas_call(
        functools.partial(halo_scores_kernel, c),
        grid=(GROUPS,),
        in_specs=[all_tokens] + [keys_wide] * 2 + [edge_wide] * 2 + [part] * 2 + [any_spec] * (len(operands) - 7),
        out_specs=[all_stats] + [halo_wide] * 4,
        out_shape=[stats_shape] + [halo_shape] * 4,
        compiler_params=params(),
        cost_estimate=cost(1e9, 1 << 10),
        name="halo_scores_" + "ab"[c],
    )(*operands)


def halo_queries_kernel(c, send, recv, s_edge, d_edge, s_mid, d_mid, own_turned, edges_turned,
                        out, p_edge, ds_edge, p_mid, ds_mid):
    lane = lax.broadcasted_iota(jnp.int32, (1, PAIR), 1)
    none = jnp.zeros((CELLS, PAIR), BF16)
    groups = ((EDGE_ROWS, s_edge, d_edge, p_edge, ds_edge), (MID_ROWS, s_mid, d_mid, p_mid, ds_mid))
    for group, (rows, s_in, d_in, p_out, ds_out) in enumerate(groups):
        mine, theirs = [ref.at[:, pl.ds(8 * group, 8)] for ref in (send, recv)]
        both = [both_parts(mine, theirs, j, 4) for j in range(2)]
        log_total, delta = [jnp.concatenate([one[w] for one in both], axis=1) for w in range(2)]
        for place, t in enumerate(rows):
            probs = jnp.exp2(s_in[0, place] - log_total[place:place + 1])
            dscores = (probs * (d_in[0, place] - delta[place:place + 1])).astype(BF16)
            p_out[0, place] = probs.astype(BF16)
            ds_out[0, place] = dscores
            for j in range(2):
                pieces = []
                for i in range(3):
                    part = dscores[at_tokens(i), pair_lanes(j)]
                    pieces += [none, part] if c else [part, none]
                turned = matmul(turned_window(own_turned, edges_turned, t, j), jnp.concatenate(pieces, axis=0), (1, 0))
                grad = turned.T * SCALE
                out[at_tokens(2 * group + place), pair_lanes(j)] = jnp.where(lane < 64, grad[:CELLS], grad[CELLS:]).astype(BF16)


def halo_queries(c, *operands):
    return pl.pallas_call(
        functools.partial(halo_queries_kernel, c),
        grid=(GROUPS,),
        in_specs=[all_stats] * 2 + [halo_wide] * 4 + [turned_wide, edge_turned_wide],
        out_specs=[all_parts] + [halo_wide] * 4,
        out_shape=[struct((2 * CHUNK, FEAT), BF16)] + [weight_shape] * 4,
        compiler_params=params(),
        cost_estimate=cost(2e9, 1 << 10),
        name="halo_queries_" + "ab"[c],
    )(*operands)


def row_gradients(rows, side_0, side_1, q_0, q_1, send_0, send_1, recv_0, recv_1, s_own, d_own, p_0, ds_0, p_1, ds_1,
                  own_turned, edges_turned, dq_ref):
    masks, wide_masks = head_masks(PAIR), head_masks(WIDE)
    lane = lax.broadcasted_iota(jnp.int32, (1, PAIR), 1)
    merged_rows = []
    for j in range(2):
        both = [both_parts(send_0, recv_0, j, 0), both_parts(send_1, recv_1, j, 0)]
        merged_rows.append([jnp.concatenate([one[w] for one in both], axis=1) for w in range(2)])
    results = []
    for place, t in enumerate(rows):
        at, row = at_tokens(place), slice(place, place + 1)
        sums = [[], []]
        for j in range(2):
            lanes = pair_lanes(j)
            queries = stacked([side_0[0, at, lanes], side_1[0, at, lanes]], masks)
            grads = stacked([side_0[1, at, lanes], side_1[1, at, lanes]], masks)
            log_total, delta = merged_rows[j]
            probs = jnp.exp2(s_own[j, place] - log_total[row])
            dscores = (probs * (d_own[j, place] - delta[row])).astype(BF16)
            for c, part in enumerate(query_parts(turned_window(own_turned, edges_turned, t, j), dscores, lane)):
                dq_ref[c, at, lanes] = part
            sums[0].append(matmul(dscores, queries, (1, 0)))
            sums[1].append(matmul(probs.astype(BF16), grads, (1, 0)))
        sums = [jnp.concatenate(parts, axis=1) for parts in sums]
        edge_parts = []
        for q_in, p_halo, ds_halo in ((q_0, p_0, ds_0), (q_1, p_1, ds_1)):
            edge_parts.append((matmul(ds_halo[0, place], stacked([q_in[0, at]], wide_masks), (1, 0)),
                               matmul(p_halo[0, place], stacked([q_in[1, at]], wide_masks), (1, 0))))
        results.append([jnp.concatenate([sums[w][at_tokens(2 * i + c)] + edge_parts[c][w][at_tokens(i)]
                                         for i in range(3) for c in range(2)], axis=0) for w in range(2)])
    return results


def edge_kernel(*refs):
    operands, (_, _, dq_ref, dk_ref, dv_ref, out_a, out_b) = refs[:16], refs[16:]
    upper, lower = row_gradients(EDGE_ROWS, *operands, dq_ref)
    for which, (out, scale) in enumerate(((dk_ref, SCALE), (dv_ref, 1.0))):
        top, bottom = upper[which] * scale, lower[which] * scale
        out_a[which] = top[:PAIR].astype(BF16)
        out[0:2 * PAIR] = top[PAIR:]
        out_b[which] = bottom[2 * PAIR:].astype(BF16)
        out[2 * PAIR:] = bottom[:2 * PAIR]


def mid_kernel(*refs):
    operands, (dk_in, dv_in, dq_ref, dk_ref, dv_ref) = refs[:15], refs[15:]
    upper, lower = row_gradients(MID_ROWS, *operands, None, dq_ref)
    for which, (sums, out, scale) in enumerate(((dk_in, dk_ref, SCALE), (dv_in, dv_ref, 1.0))):
        out[0:PAIR] = sums[0:PAIR] + upper[which][:PAIR] * scale
        out[PAIR:3 * PAIR] = sums[PAIR:3 * PAIR] + (upper[which][PAIR:] + lower[which][:2 * PAIR]) * scale
        out[3 * PAIR:] = sums[3 * PAIR:] + lower[which][2 * PAIR:] * scale


def row_specs(group):
    return ([tokens_wide(group)] * 4 + [stats_wide(group)] * 4 + [held_wide] * 2 + [halo_wide] * 4 + [turned_wide])


GRAD_SPECS = [sums_wide] + [keys_wide] * 2
GRAD_SHAPES = [struct((2, CHUNK, FEAT), F32)] + [struct((ROWS * PAIR, FEAT), F32)] * 2


def edge_gradients(*operands):
    return pl.pallas_call(
        edge_kernel,
        grid=(GROUPS,),
        in_specs=row_specs(EDGE) + [edge_turned_wide, any_spec, any_spec],
        out_specs=GRAD_SPECS + [edge_wide] * 2,
        out_shape=GRAD_SHAPES + [struct((2, PAIR, FEAT), BF16)] * 2,
        compiler_params=params(),
        cost_estimate=cost(3e9, 1 << 10),
        name="edge_gradients",
    )(*operands)


def mid_gradients(*operands):
    return pl.pallas_call(
        mid_kernel,
        grid=(GROUPS,),
        in_specs=row_specs(MID) + [keys_wide] * 2,
        out_specs=GRAD_SPECS,
        out_shape=GRAD_SHAPES,
        compiler_params=params(),
        cost_estimate=cost(3e9, 1 << 10),
        name="mid_gradients",
    )(*operands)


def join_columns(side_a, side_b):
    parts = ordered(side_a, side_b)
    return jnp.concatenate([part.reshape(8, 8, FEAT) for part in parts], axis=1).astype(BF16)


def finish_kernel(dq_edge, dq_mid, dk, dv, dq_0, dq_1, from_a, from_b,
                  q_ref, k_ref, v_ref, buffers, sems):
    copies = []

    def send(i, t, value):
        buffers[i, t] = value
        out = (q_ref, k_ref, v_ref)[i]
        copies.append(pltpu.make_async_copy(buffers.at[i, t], out.at[pl.ds(8 * grid_row(t), 8)], sems.at[i, t]))
        copies[-1].start()

    for t in range(ROWS):
        for which, own in enumerate((dk, dv)):
            full = own[t * PAIR:(t + 1) * PAIR]
            if t == 0:
                full = full + from_a[which].astype(F32)
            if t == ROWS - 1:
                full = full + from_b[which].astype(F32)
            send(1 + which, t, join_columns(full[:CELLS], full[CELLS:]))
    for place, t in enumerate(ORDER):
        dq = (dq_edge, dq_mid)[place // 2]
        at, there = at_tokens(place % 2), at_tokens(place)
        send(0, t, join_columns(dq[0, at] + dq_0[there].astype(F32), dq[1, at] + dq_1[there].astype(F32)))
    for copy in copies:
        copy.wait()


def finish(*operands):
    return pl.pallas_call(
        finish_kernel,
        out_specs=[any_spec] * 3,
        out_shape=[struct((8 * ROWS, 16, FEAT), BF16)] * 3,
        scratch_shapes=[pltpu.VMEM((3, ROWS, 8, 16, FEAT), BF16), pltpu.SemaphoreType.DMA((3, ROWS))],
        compiler_params=params(),
        cost_estimate=cost(0, 1 << 10),
        name="finish",
    )(*operands)


def swap_a(x, axis):
    return lax.ppermute(x, axis, [(i, i ^ 1) for i in range(lax.axis_size(axis))])


def swap_b(x, axis, wrap):
    count = lax.axis_size(axis)
    pairs = []
    for i in range(1, count if wrap else count - 1, 2):
        pairs += [(i, (i + 1) % count), ((i + 1) % count, i)]
    return lax.ppermute(x, axis, pairs)


def swap_lon(c, x):
    return swap_b(x, "lon", True) if c else swap_a(x, "lon")


def on_device(query_vectors, key_vectors, value_vectors, output_grads):
    *sides, own_edge_a, own_edge_b = pack_queries(query_vectors, output_grads, key_vectors, value_vectors)
    kd, vd = pack_keys(key_vectors, value_vectors)
    edge_b = swap_b(own_edge_b, "lat", False)
    halos = [swap_lon(c, side) for c, side in enumerate(sides)]
    edges = (swap_a(own_edge_a, "lat"), edge_b)
    mid_part, *mid_own, turned = mid_scores(*sides, kd, vd)
    edge_part, *edge_own = edge_scores(*sides, kd, vd, *edges)
    edges_turned = turn_edges(*edges)
    sends, recvs, halo_dq, dq_parts, weights = [{} for _ in range(5)]
    for c in (1, 0):
        before = halo_dq.values()
        sends[c], *held = halo_scores(c, halos[c], kd, vd, *edges, edge_part, mid_part, *before)
        recvs[c] = swap_lon(c, sends[c])
        halo_dq[c], *weights[c] = halo_queries(c, sends[c], recvs[c], *held, turned, edges_turned)
        dq_parts[c] = swap_lon(c, halo_dq[c])
    sends, recvs, halo_dq, dq_parts = [[one[0], one[1]] for one in (sends, recvs, halo_dq, dq_parts)]
    shared = (*sides, *halos, *sends, *recvs)
    dq_edge, dk, dv, out_a, out_b = edge_gradients(*shared, *edge_own, *weights[0][:2], *weights[1][:2], turned, edges_turned,
                                                   *halo_dq)
    key_parts = (swap_a(out_a, "lat"), swap_b(out_b, "lat", False))
    dq_mid, dk, dv = mid_gradients(*shared, *mid_own, *weights[0][2:], *weights[1][2:], turned, dk, dv)
    return tuple(finish(dq_edge, dq_mid, dk, dv, *dq_parts, *key_parts))


def solution(mesh):
    spec = P("lat", "lon", None)
    return jax.shard_map(on_device, mesh=mesh, in_specs=(spec,) * 4, out_specs=(spec,) * 3, check_vma=False)
```

```python
import functools

import jax
import jax.numpy as jnp
from jax import lax
from jax.experimental import pallas as pl
from jax.experimental.pallas import tpu as pltpu
from jax.sharding import PartitionSpec as P

ROWS = 4
CELLS = 64
CHUNK = 2 * CELLS
PAIR = 128
WIDE = 256
PAIRS = 4
GROUPS = 2
FEAT = 512
SCALE = 64 ** -0.5
LOG2E = 1.4426950408889634
MASKED = -1e30
F32 = jnp.float32
BF16 = jnp.bfloat16
VMEM_LIMIT = 20 * 1024 * 1024
PACK_LIMIT = 62 * 1024 * 1024
any_spec = pl.BlockSpec(memory_space=pl.ANY)
EDGE_ROWS = (0, 3)
MID_ROWS = (1, 2)
ORDER = EDGE_ROWS + MID_ROWS
EDGE, MID = 0, 1


def matmul(a, b, contract):
    return lax.dot_general(a, b, ((contract[:1], contract[1:]), ((), ())), preferred_element_type=F32)


def params(limit=VMEM_LIMIT):
    return pltpu.CompilerParams(vmem_limit_bytes=limit)


def cost(flops, size):
    return pl.CostEstimate(flops=int(flops), bytes_accessed=int(size), transcendentals=0)


def struct(shape, dtype):
    return jax.ShapeDtypeStruct(shape, dtype)


def grid_row(t):
    return jnp.where(lax.axis_index("lat") % 2 == 0, ROWS - 1 - t, t)


def ordered(first, second):
    swap = lax.axis_index("lon") % 2 == 0
    return jnp.where(swap, second, first), jnp.where(swap, first, second)


def split_columns(block):
    wide = block.astype(F32)
    parts = ordered(*[wide[:, c * 8:(c + 1) * 8].reshape(CELLS, FEAT) for c in range(2)])
    return [part.astype(BF16) for part in parts]


def fetch(refs, rows, buffers, sems):
    copies = [[pltpu.make_async_copy(ref.at[pl.ds(8 * grid_row(t), 8)], buffers.at[i, place], sems.at[i, place])
               for place, t in enumerate(rows)] for i, ref in enumerate(refs)]
    for place in range(len(rows)):
        for copy in copies:
            copy[place].start()
    return copies


def key_tile(buffer):
    return jnp.concatenate(split_columns(buffer), axis=0)


def pack_queries_kernel(q_ref, g_ref, k_ref, v_ref, side_0, side_1, edge_a, edge_b, buffers, sems, key_buffers, key_sems,
                        packed, out_sems, packed_keys, key_out_sems):
    key_copies = fetch((k_ref, v_ref), EDGE_ROWS, key_buffers, key_sems)
    copies = fetch((q_ref, g_ref), ORDER, buffers, sems)
    sends = []

    def send(source, out, sem):
        sends.append(pltpu.make_async_copy(source, out, sem))
        sends[-1].start()

    for place, edge in enumerate((edge_a, edge_b)):
        for i in range(2):
            key_copies[i][place].wait()
            packed_keys[place, i] = key_tile(key_buffers[i, place])
            send(packed_keys.at[place, i], edge.at[i], key_out_sems.at[place, i])
    for place in range(ROWS):
        for i in range(2):
            copies[i][place].wait()
            for side, (value, out) in enumerate(zip(split_columns(buffers[i, place]), (side_0, side_1))):
                packed[side, i, place] = value
                send(packed.at[side, i, place], out.at[i, pl.ds(place * CELLS, CELLS)], out_sems.at[side, i, place])
    for copy in sends:
        copy.wait()


def pack_queries(*operands):
    return pl.pallas_call(
        pack_queries_kernel,
        in_specs=[any_spec] * 4,
        out_specs=[any_spec] * 4,
        out_shape=[struct((2, ROWS * CELLS, FEAT), BF16)] * 2 + [struct((2, PAIR, FEAT), BF16)] * 2,
        scratch_shapes=[
            pltpu.VMEM((2, ROWS, 8, 16, FEAT), BF16), pltpu.SemaphoreType.DMA((2, ROWS)),
            pltpu.VMEM((2, 2, 8, 16, FEAT), BF16), pltpu.SemaphoreType.DMA((2, 2)),
            pltpu.VMEM((2, 2, ROWS, CELLS, FEAT), BF16), pltpu.SemaphoreType.DMA((2, 2, ROWS)),
            pltpu.VMEM((2, 2, PAIR, FEAT), BF16), pltpu.SemaphoreType.DMA((2, 2)),
        ],
        compiler_params=params(PACK_LIMIT),
        cost_estimate=cost(0, 3 << 20),
        name="pack_queries",
    )(*operands)


def pack_keys_kernel(k_ref, v_ref, kd, vd, buffers, sems):
    copies = fetch((k_ref, v_ref), range(ROWS), buffers, sems)
    for t in range(ROWS):
        for i, out in enumerate((kd, vd)):
            copies[i][t].wait()
            out[t * PAIR:(t + 1) * PAIR] = key_tile(buffers[i, t])


def pack_keys(*operands):
    return pl.pallas_call(
        pack_keys_kernel,
        in_specs=[any_spec] * 2,
        out_shape=[struct((ROWS * PAIR, FEAT), BF16)] * 2,
        scratch_shapes=[pltpu.VMEM((2, ROWS, 8, 16, FEAT), BF16), pltpu.SemaphoreType.DMA((2, ROWS))],
        compiler_params=params(),
        cost_estimate=cost(0, 3 << 20),
        name="pack_keys",
    )(*operands)


def head_masks(lanes):
    lane = lax.broadcasted_iota(jnp.int32, (1, lanes), 1)
    return [jnp.where((lane >= 64 * h) & (lane < 64 * (h + 1)), 1.0, 0.0).astype(F32).astype(BF16)
            for h in range(lanes // 64)]


def stacked(parts, masks):
    return jnp.concatenate([part * mask for part in parts for mask in masks], axis=0)


def key_rows(own, edges, which, t, lanes=slice(None)):
    rows = []
    for row in range(t, t + 3):
        if row == 0:
            rows.append(edges[0][which, :, lanes])
        elif row == ROWS + 1:
            rows.append(edges[1][which, :, lanes])
        else:
            rows.append(own[(row - 1) * PAIR:row * PAIR, lanes])
    return rows


def window(*where):
    return jnp.concatenate(key_rows(*where), axis=0)


def column_window(column, *where):
    return jnp.concatenate([row[column * CELLS:(column + 1) * CELLS] for row in key_rows(*where)], axis=0)


def score_block(keys, queries, t):
    scores = matmul(keys, queries, (1, 1)) * (SCALE * LOG2E)
    if t == ROWS - 1:
        lat = lax.axis_index("lat")
        outside = (lat == 0) | (lat == lax.axis_size("lat") - 1)
        cut = 2 * (keys.shape[0] // 3)
        bias = jnp.where(outside, MASKED, 0.0).astype(F32)
        scores = jnp.concatenate([scores[:cut], scores[cut:] + bias], axis=0)
    return scores


def row_stats(scores, dprobs):
    top = jnp.max(scores, axis=0, keepdims=True)
    weights = jnp.exp2(scores - top)
    total = jnp.sum(weights, axis=0, keepdims=True)
    delta = jnp.sum(weights * dprobs, axis=0, keepdims=True) / total
    return top + jnp.log(total) * LOG2E, delta


def merged(log_a, delta_a, log_b, delta_b):
    top = jnp.maximum(log_a, log_b)
    weight_a = jnp.exp2(log_a - top)
    weight_b = jnp.exp2(log_b - top)
    total = weight_a + weight_b
    return top + jnp.log(total) * LOG2E, (weight_a * delta_a + weight_b * delta_b) / total


def both_parts(mine, theirs, pair, base):
    other = 4 - base
    return merged(mine[pair, base:base + 2], mine[pair, base + 2:base + 4],
                  theirs[pair, other:other + 2], theirs[pair, other + 2:other + 4])


def turned_window(own_turned, edges_turned, t, j):
    at = slice(j * PAIR, (j + 1) * PAIR)
    rows = []
    for row in range(t, t + 3):
        if row in (0, ROWS + 1):
            rows.append(edges_turned[row // (ROWS + 1), at])
        else:
            rows.append(own_turned[at, (row - 1) * PAIR:row * PAIR])
    return jnp.concatenate(rows, axis=1)


def query_parts(keys_turned, dscores, lane):
    turned = matmul(keys_turned, dscores, (1, 0)) * SCALE
    parts = [turned[:, c * PAIR:(c + 1) * PAIR].T for c in range(2)]
    return [jnp.where(lane < 64, part[:CELLS], part[CELLS:]) for part in parts]


def at_tokens(place):
    return slice(place * CELLS, (place + 1) * CELLS)


def pair_lanes(j):
    return slice(j * PAIR, (j + 1) * PAIR)


def tokens_spec(group):
    return pl.BlockSpec((2, CHUNK, PAIR), lambda p: (0, group, p))


keys_spec = pl.BlockSpec((ROWS * PAIR, PAIR), lambda p: (0, p))
edge_spec = pl.BlockSpec((2, PAIR, PAIR), lambda p: (0, 0, p))
part_spec = pl.BlockSpec((1, 8, PAIR), lambda p: (p, 0, 0))
held_spec = pl.BlockSpec((1, 2, 3 * PAIR, WIDE), lambda p: (p, 0, 0, 0))
part_shape = struct((PAIRS, 8, PAIR), F32)
stats_shape = struct((PAIRS, 16, PAIR), F32)
held_shape = struct((PAIRS, 2, 3 * PAIR, WIDE), F32)


def tokens_wide(group):
    return pl.BlockSpec((2, CHUNK, WIDE), lambda g: (0, group, g))


def stats_wide(group):
    return pl.BlockSpec((2, 8, PAIR), lambda g: (g, group, 0))


all_tokens = pl.BlockSpec((2, 2 * CHUNK, WIDE), lambda g: (0, 0, g))
all_stats = pl.BlockSpec((2, 16, PAIR), lambda g: (g, 0, 0))
all_parts = pl.BlockSpec((2 * CHUNK, WIDE), lambda g: (0, g))
sums_wide = pl.BlockSpec((2, CHUNK, WIDE), lambda g: (0, 0, g))
keys_wide = pl.BlockSpec((ROWS * PAIR, WIDE), lambda g: (0, g))
edge_wide = pl.BlockSpec((2, PAIR, WIDE), lambda g: (0, 0, g))
turned_wide = pl.BlockSpec((WIDE, ROWS * PAIR), lambda g: (g, 0))
edge_turned_wide = pl.BlockSpec((2, WIDE, PAIR), lambda g: (0, g, 0))
held_wide = pl.BlockSpec((2, 2, 3 * PAIR, WIDE), lambda g: (g, 0, 0, 0))
halo_wide = pl.BlockSpec((1, 2, 3 * CELLS, WIDE), lambda g: (g, 0, 0, 0))
halo_shape = struct((GROUPS, 2, 3 * CELLS, WIDE), F32)
weight_shape = struct((GROUPS, 2, 3 * CELLS, WIDE), BF16)


def own_scores(rows, side_a, side_b, kd, vd, edges, part, s_out, d_out):
    masks = head_masks(PAIR)
    for place, t in enumerate(rows):
        at = at_tokens(place)
        queries = stacked([side_a[0, at], side_b[0, at]], masks)
        grads = stacked([side_a[1, at], side_b[1, at]], masks)
        scores = score_block(window(kd, edges, 0, t), queries, t)
        dprobs = matmul(window(vd, edges, 1, t), grads, (1, 1))
        s_out[0, place] = scores
        d_out[0, place] = dprobs
        for w, values in enumerate(row_stats(scores, dprobs)):
            for c in range(2):
                index = 4 * c + 2 * w + place
                part[0, index:index + 1] = values[:, pair_lanes(c)]


def mid_scores_kernel(side_0, side_1, kd, vd, part, s_out, d_out, turned):
    own_scores(MID_ROWS, side_0, side_1, kd, vd, None, part, s_out, d_out)
    turned[...] = kd[...].T


def edge_scores_kernel(side_0, side_1, kd, vd, edge_a, edge_b, part, s_out, d_out):
    own_scores(EDGE_ROWS, side_0, side_1, kd, vd, (edge_a, edge_b), part, s_out, d_out)


def mid_scores(*operands):
    return pl.pallas_call(
        mid_scores_kernel,
        grid=(PAIRS,),
        in_specs=[tokens_spec(MID)] * 2 + [keys_spec] * 2,
        out_specs=[part_spec] + [held_spec] * 2 + [pl.BlockSpec((PAIR, ROWS * PAIR), lambda p: (p, 0))],
        out_shape=[part_shape] + [held_shape] * 2 + [struct((FEAT, ROWS * PAIR), BF16)],
        compiler_params=params(),
        cost_estimate=cost(2e9, 1 << 10),
        name="mid_scores",
    )(*operands)


def edge_scores(*operands):
    return pl.pallas_call(
        edge_scores_kernel,
        grid=(PAIRS,),
        in_specs=[tokens_spec(EDGE)] * 2 + [keys_spec] * 2 + [edge_spec] * 2,
        out_specs=[part_spec] + [held_spec] * 2,
        out_shape=[part_shape] + [held_shape] * 2,
        compiler_params=params(),
        cost_estimate=cost(2e9, 1 << 10),
        name="edge_scores",
    )(*operands)


def turn_edges_kernel(edge_a, edge_b, turned):
    turned[0] = edge_a[0].T
    turned[1] = edge_b[0].T


def turn_edges(*operands):
    return pl.pallas_call(
        turn_edges_kernel,
        grid=(PAIRS,),
        in_specs=[edge_spec] * 2,
        out_specs=pl.BlockSpec((2, PAIR, PAIR), lambda p: (0, p, 0)),
        out_shape=struct((2, FEAT, PAIR), BF16),
        compiler_params=params(),
        cost_estimate=cost(1e9, 1 << 10),
        name="turn_edges",
    )(*operands)


def halo_scores_kernel(c, q_in, kd, vd, edge_a, edge_b, edge_part, mid_part, send, s_edge, d_edge, s_mid, d_mid):
    masks = head_masks(WIDE)
    groups = ((EDGE_ROWS, edge_part, s_edge, d_edge), (MID_ROWS, mid_part, s_mid, d_mid))
    for group, (rows, part, s_out, d_out) in enumerate(groups):
        base = 8 * group
        for j in range(2):
            send[j, base:base + 4] = part[j, 4 * c:4 * c + 4]
        for place, t in enumerate(rows):
            at = at_tokens(2 * group + place)
            queries = stacked([q_in[0, at]], masks)
            grads = stacked([q_in[1, at]], masks)
            scores = score_block(column_window(c, kd, (edge_a, edge_b), 0, t), queries, t)
            dprobs = matmul(column_window(c, vd, (edge_a, edge_b), 1, t), grads, (1, 1))
            s_out[0, place] = scores
            d_out[0, place] = dprobs
            for w, values in enumerate(row_stats(scores, dprobs)):
                index = base + 4 + 2 * w + place
                for j in range(2):
                    send[j, index:index + 1] = values[:, pair_lanes(j)]


def halo_scores(c, *operands):
    part = pl.BlockSpec((2, 8, PAIR), lambda g: (g, 0, 0))
    return pl.pallas_call(
        functools.partial(halo_scores_kernel, c),
        grid=(GROUPS,),
        in_specs=[all_tokens] + [keys_wide] * 2 + [edge_wide] * 2 + [part] * 2,
        out_specs=[all_stats] + [halo_wide] * 4,
        out_shape=[stats_shape] + [halo_shape] * 4,
        compiler_params=params(),
        cost_estimate=cost(2e9, 1 << 10),
        name="halo_scores_" + "ab"[c],
    )(*operands)


def halo_queries_kernel(c, send, recv, s_edge, d_edge, s_mid, d_mid, own_turned, edges_turned,
                        out, p_edge, ds_edge, p_mid, ds_mid):
    lane = lax.broadcasted_iota(jnp.int32, (1, PAIR), 1)
    none = jnp.zeros((CELLS, PAIR), BF16)
    groups = ((EDGE_ROWS, s_edge, d_edge, p_edge, ds_edge), (MID_ROWS, s_mid, d_mid, p_mid, ds_mid))
    for group, (rows, s_in, d_in, p_out, ds_out) in enumerate(groups):
        mine, theirs = [ref.at[:, pl.ds(8 * group, 8)] for ref in (send, recv)]
        both = [both_parts(mine, theirs, j, 4) for j in range(2)]
        log_total, delta = [jnp.concatenate([one[w] for one in both], axis=1) for w in range(2)]
        for place, t in enumerate(rows):
            probs = jnp.exp2(s_in[0, place] - log_total[place:place + 1])
            dscores = (probs * (d_in[0, place] - delta[place:place + 1])).astype(BF16)
            p_out[0, place] = probs.astype(BF16)
            ds_out[0, place] = dscores
            for j in range(2):
                pieces = []
                for i in range(3):
                    part = dscores[at_tokens(i), pair_lanes(j)]
                    pieces += [none, part] if c else [part, none]
                turned = matmul(turned_window(own_turned, edges_turned, t, j), jnp.concatenate(pieces, axis=0), (1, 0))
                grad = turned.T * SCALE
                out[at_tokens(2 * group + place), pair_lanes(j)] = jnp.where(lane < 64, grad[:CELLS], grad[CELLS:]).astype(BF16)


def halo_queries(c, *operands):
    return pl.pallas_call(
        functools.partial(halo_queries_kernel, c),
        grid=(GROUPS,),
        in_specs=[all_stats] * 2 + [halo_wide] * 4 + [turned_wide, edge_turned_wide],
        out_specs=[all_parts] + [halo_wide] * 4,
        out_shape=[struct((2 * CHUNK, FEAT), BF16)] + [weight_shape] * 4,
        compiler_params=params(),
        cost_estimate=cost(0, 1 << 10),
        name="halo_queries_" + "ab"[c],
    )(*operands)


def row_gradients(rows, side_0, side_1, q_0, q_1, send_0, send_1, recv_0, recv_1, s_own, d_own, p_0, ds_0, p_1, ds_1,
                  own_turned, edges_turned, dq_ref):
    masks, wide_masks = head_masks(PAIR), head_masks(WIDE)
    lane = lax.broadcasted_iota(jnp.int32, (1, PAIR), 1)
    merged_rows = []
    for j in range(2):
        both = [both_parts(send_0, recv_0, j, 0), both_parts(send_1, recv_1, j, 0)]
        merged_rows.append([jnp.concatenate([one[w] for one in both], axis=1) for w in range(2)])
    results = []
    for place, t in enumerate(rows):
        at, row = at_tokens(place), slice(place, place + 1)
        sums = [[], []]
        for j in range(2):
            lanes = pair_lanes(j)
            queries = stacked([side_0[0, at, lanes], side_1[0, at, lanes]], masks)
            grads = stacked([side_0[1, at, lanes], side_1[1, at, lanes]], masks)
            log_total, delta = merged_rows[j]
            probs = jnp.exp2(s_own[j, place] - log_total[row])
            dscores = (probs * (d_own[j, place] - delta[row])).astype(BF16)
            for c, part in enumerate(query_parts(turned_window(own_turned, edges_turned, t, j), dscores, lane)):
                dq_ref[c, at, lanes] = part
            sums[0].append(matmul(dscores, queries, (1, 0)))
            sums[1].append(matmul(probs.astype(BF16), grads, (1, 0)))
        sums = [jnp.concatenate(parts, axis=1) for parts in sums]
        edge_parts = []
        for q_in, p_halo, ds_halo in ((q_0, p_0, ds_0), (q_1, p_1, ds_1)):
            edge_parts.append((matmul(ds_halo[0, place], stacked([q_in[0, at]], wide_masks), (1, 0)),
                               matmul(p_halo[0, place], stacked([q_in[1, at]], wide_masks), (1, 0))))
        results.append([jnp.concatenate([sums[w][at_tokens(2 * i + c)] + edge_parts[c][w][at_tokens(i)]
                                         for i in range(3) for c in range(2)], axis=0) for w in range(2)])
    return results


def edge_kernel(*refs):
    operands, (_, _, dq_ref, dk_ref, dv_ref, out_a, out_b) = refs[:16], refs[16:]
    upper, lower = row_gradients(EDGE_ROWS, *operands, dq_ref)
    for which, (out, scale) in enumerate(((dk_ref, SCALE), (dv_ref, 1.0))):
        top, bottom = upper[which] * scale, lower[which] * scale
        out_a[which] = top[:PAIR].astype(BF16)
        out[0:2 * PAIR] = top[PAIR:]
        out_b[which] = bottom[2 * PAIR:].astype(BF16)
        out[2 * PAIR:] = bottom[:2 * PAIR]


def mid_kernel(*refs):
    operands, (dk_in, dv_in, dq_ref, dk_ref, dv_ref) = refs[:15], refs[15:]
    upper, lower = row_gradients(MID_ROWS, *operands, None, dq_ref)
    for which, (sums, out, scale) in enumerate(((dk_in, dk_ref, SCALE), (dv_in, dv_ref, 1.0))):
        out[0:PAIR] = sums[0:PAIR] + upper[which][:PAIR] * scale
        out[PAIR:3 * PAIR] = sums[PAIR:3 * PAIR] + (upper[which][PAIR:] + lower[which][:2 * PAIR]) * scale
        out[3 * PAIR:] = sums[3 * PAIR:] + lower[which][2 * PAIR:] * scale


def row_specs(group):
    return ([tokens_wide(group)] * 4 + [stats_wide(group)] * 4 + [held_wide] * 2 + [halo_wide] * 4 + [turned_wide])


GRAD_SPECS = [sums_wide] + [keys_wide] * 2
GRAD_SHAPES = [struct((2, CHUNK, FEAT), F32)] + [struct((ROWS * PAIR, FEAT), F32)] * 2


def edge_gradients(*operands):
    return pl.pallas_call(
        edge_kernel,
        grid=(GROUPS,),
        in_specs=row_specs(EDGE) + [edge_turned_wide, any_spec, any_spec],
        out_specs=GRAD_SPECS + [edge_wide] * 2,
        out_shape=GRAD_SHAPES + [struct((2, PAIR, FEAT), BF16)] * 2,
        compiler_params=params(),
        cost_estimate=cost(3e9, 1 << 10),
        name="edge_gradients",
    )(*operands)


def mid_gradients(*operands):
    return pl.pallas_call(
        mid_kernel,
        grid=(GROUPS,),
        in_specs=row_specs(MID) + [keys_wide] * 2,
        out_specs=GRAD_SPECS,
        out_shape=GRAD_SHAPES,
        compiler_params=params(),
        cost_estimate=cost(3e9, 1 << 10),
        name="mid_gradients",
    )(*operands)


def join_columns(side_a, side_b):
    parts = ordered(side_a, side_b)
    return jnp.concatenate([part.reshape(8, 8, FEAT) for part in parts], axis=1).astype(BF16)


def finish_kernel(dq_edge, dq_mid, dk, dv, dq_0, dq_1, from_a, from_b,
                  q_ref, k_ref, v_ref, buffers, sems):
    copies = []

    def send(i, t, value):
        buffers[i, t] = value
        out = (q_ref, k_ref, v_ref)[i]
        copies.append(pltpu.make_async_copy(buffers.at[i, t], out.at[pl.ds(8 * grid_row(t), 8)], sems.at[i, t]))
        copies[-1].start()

    for t in range(ROWS):
        for which, own in enumerate((dk, dv)):
            full = own[t * PAIR:(t + 1) * PAIR]
            if t == 0:
                full = full + from_a[which].astype(F32)
            if t == ROWS - 1:
                full = full + from_b[which].astype(F32)
            send(1 + which, t, join_columns(full[:CELLS], full[CELLS:]))
    for place, t in enumerate(ORDER):
        dq = (dq_edge, dq_mid)[place // 2]
        at, there = at_tokens(place % 2), at_tokens(place)
        send(0, t, join_columns(dq[0, at] + dq_0[there].astype(F32), dq[1, at] + dq_1[there].astype(F32)))
    for copy in copies:
        copy.wait()


def finish(*operands):
    return pl.pallas_call(
        finish_kernel,
        out_specs=[any_spec] * 3,
        out_shape=[struct((8 * ROWS, 16, FEAT), BF16)] * 3,
        scratch_shapes=[pltpu.VMEM((3, ROWS, 8, 16, FEAT), BF16), pltpu.SemaphoreType.DMA((3, ROWS))],
        compiler_params=params(),
        cost_estimate=cost(0, 1 << 10),
        name="finish",
    )(*operands)


def swap_a(x, axis):
    return lax.ppermute(x, axis, [(i, i ^ 1) for i in range(lax.axis_size(axis))])


def swap_b(x, axis, wrap):
    count = lax.axis_size(axis)
    pairs = []
    for i in range(1, count if wrap else count - 1, 2):
        pairs += [(i, (i + 1) % count), ((i + 1) % count, i)]
    return lax.ppermute(x, axis, pairs)


def swap_lon(c, x):
    return swap_b(x, "lon", True) if c else swap_a(x, "lon")


def on_device(query_vectors, key_vectors, value_vectors, output_grads):
    *sides, own_edge_a, own_edge_b = pack_queries(query_vectors, output_grads, key_vectors, value_vectors)
    kd, vd = pack_keys(key_vectors, value_vectors)
    edge_b = swap_b(own_edge_b, "lat", False)
    halos = [swap_lon(c, side) for c, side in enumerate(sides)]
    edges = (swap_a(own_edge_a, "lat"), edge_b)
    mid_part, *mid_own, turned = mid_scores(*sides, kd, vd)
    edge_part, *edge_own = edge_scores(*sides, kd, vd, *edges)
    edges_turned = turn_edges(*edges)
    sends, recvs, halo_dq, dq_parts, weights = [], [], [], [], []
    for c in range(2):
        send, *held = halo_scores(c, halos[c], kd, vd, *edges, edge_part, mid_part)
        recv = swap_lon(c, send)
        grad, *weight = halo_queries(c, send, recv, *held, turned, edges_turned)
        sends.append(send)
        recvs.append(recv)
        halo_dq.append(grad)
        dq_parts.append(swap_lon(c, grad))
        weights.append(weight)
    shared = (*sides, *halos, *sends, *recvs)
    dq_edge, dk, dv, out_a, out_b = edge_gradients(*shared, *edge_own, *weights[0][:2], *weights[1][:2], turned, edges_turned,
                                                   *halo_dq)
    key_parts = (swap_a(out_a, "lat"), swap_b(out_b, "lat", False))
    dq_mid, dk, dv = mid_gradients(*shared, *mid_own, *weights[0][2:], *weights[1][2:], turned, dk, dv)
    return tuple(finish(dq_edge, dq_mid, dk, dv, *dq_parts, *key_parts))


def solution(mesh):
    spec = P("lat", "lon", None)
    return jax.shard_map(on_device, mesh=mesh, in_specs=(spec,) * 4, out_specs=(spec,) * 3, check_vma=False)
```

```python
import functools

import jax
import jax.numpy as jnp
from jax import lax
from jax.experimental import pallas as pl
from jax.experimental.pallas import tpu as pltpu
from jax.sharding import PartitionSpec as P

ROWS = 4
CELLS = 64
CHUNK = 2 * CELLS
PAIR = 128
WIDE = 256
PAIRS = 4
GROUPS = 2
FEAT = 512
SCALE = 64 ** -0.5
LOG2E = 1.4426950408889634
MASKED = -1e30
F32 = jnp.float32
BF16 = jnp.bfloat16
VMEM_LIMIT = 20 * 1024 * 1024
PACK_LIMIT = 62 * 1024 * 1024
any_spec = pl.BlockSpec(memory_space=pl.ANY)
EDGE_ROWS = (0, 3)
MID_ROWS = (1, 2)
ORDER = EDGE_ROWS + MID_ROWS
EDGE, MID = 0, 1


def matmul(a, b, contract):
    return lax.dot_general(a, b, ((contract[:1], contract[1:]), ((), ())), preferred_element_type=F32)


def params(limit=VMEM_LIMIT):
    return pltpu.CompilerParams(vmem_limit_bytes=limit)


def cost(flops, size):
    return pl.CostEstimate(flops=int(flops), bytes_accessed=int(size), transcendentals=0)


def struct(shape, dtype):
    return jax.ShapeDtypeStruct(shape, dtype)


def grid_row(t):
    return jnp.where(lax.axis_index("lat") % 2 == 0, ROWS - 1 - t, t)


def ordered(first, second):
    swap = lax.axis_index("lon") % 2 == 0
    return jnp.where(swap, second, first), jnp.where(swap, first, second)


def split_columns(block):
    wide = block.astype(F32)
    parts = ordered(*[wide[:, c * 8:(c + 1) * 8].reshape(CELLS, FEAT) for c in range(2)])
    return [part.astype(BF16) for part in parts]


def fetch(refs, rows, buffers, sems):
    copies = [[pltpu.make_async_copy(ref.at[pl.ds(8 * grid_row(t), 8)], buffers.at[i, place], sems.at[i, place])
               for place, t in enumerate(rows)] for i, ref in enumerate(refs)]
    for place in range(len(rows)):
        for copy in copies:
            copy[place].start()
    return copies


def key_tile(buffer):
    return jnp.concatenate(split_columns(buffer), axis=0)


def pack_queries_kernel(q_ref, g_ref, k_ref, v_ref, side_0, side_1, edge_a, edge_b, buffers, sems, key_buffers, key_sems,
                        packed, out_sems, packed_keys, key_out_sems):
    key_copies = fetch((k_ref, v_ref), EDGE_ROWS, key_buffers, key_sems)
    copies = fetch((q_ref, g_ref), ORDER, buffers, sems)
    sends = []

    def send(source, out, sem):
        sends.append(pltpu.make_async_copy(source, out, sem))
        sends[-1].start()

    for place, edge in enumerate((edge_a, edge_b)):
        for i in range(2):
            key_copies[i][place].wait()
            packed_keys[place, i] = key_tile(key_buffers[i, place])
            send(packed_keys.at[place, i], edge.at[i], key_out_sems.at[place, i])
    for place in range(ROWS):
        for i in range(2):
            copies[i][place].wait()
            for side, (value, out) in enumerate(zip(split_columns(buffers[i, place]), (side_0, side_1))):
                packed[side, i, place] = value
                send(packed.at[side, i, place], out.at[i, pl.ds(place * CELLS, CELLS)], out_sems.at[side, i, place])
    for copy in sends:
        copy.wait()


def pack_queries(*operands):
    return pl.pallas_call(
        pack_queries_kernel,
        in_specs=[any_spec] * 4,
        out_specs=[any_spec] * 4,
        out_shape=[struct((2, ROWS * CELLS, FEAT), BF16)] * 2 + [struct((2, PAIR, FEAT), BF16)] * 2,
        scratch_shapes=[
            pltpu.VMEM((2, ROWS, 8, 16, FEAT), BF16), pltpu.SemaphoreType.DMA((2, ROWS)),
            pltpu.VMEM((2, 2, 8, 16, FEAT), BF16), pltpu.SemaphoreType.DMA((2, 2)),
            pltpu.VMEM((2, 2, ROWS, CELLS, FEAT), BF16), pltpu.SemaphoreType.DMA((2, 2, ROWS)),
            pltpu.VMEM((2, 2, PAIR, FEAT), BF16), pltpu.SemaphoreType.DMA((2, 2)),
        ],
        compiler_params=params(PACK_LIMIT),
        cost_estimate=cost(0, 3 << 20),
        name="pack_queries",
    )(*operands)


def pack_keys_kernel(k_ref, v_ref, kd, vd, buffers, sems):
    copies = fetch((k_ref, v_ref), range(ROWS), buffers, sems)
    for t in range(ROWS):
        for i, out in enumerate((kd, vd)):
            copies[i][t].wait()
            out[t * PAIR:(t + 1) * PAIR] = key_tile(buffers[i, t])


def pack_keys(*operands):
    return pl.pallas_call(
        pack_keys_kernel,
        in_specs=[any_spec] * 2,
        out_shape=[struct((ROWS * PAIR, FEAT), BF16)] * 2,
        scratch_shapes=[pltpu.VMEM((2, ROWS, 8, 16, FEAT), BF16), pltpu.SemaphoreType.DMA((2, ROWS))],
        compiler_params=params(),
        cost_estimate=cost(0, 3 << 20),
        name="pack_keys",
    )(*operands)


def head_masks(lanes):
    lane = lax.broadcasted_iota(jnp.int32, (1, lanes), 1)
    return [jnp.where((lane >= 64 * h) & (lane < 64 * (h + 1)), 1.0, 0.0).astype(F32).astype(BF16)
            for h in range(lanes // 64)]


def stacked(parts, masks):
    return jnp.concatenate([part * mask for part in parts for mask in masks], axis=0)


def key_rows(own, edges, which, t, lanes=slice(None)):
    rows = []
    for row in range(t, t + 3):
        if row == 0:
            rows.append(edges[0][which, :, lanes])
        elif row == ROWS + 1:
            rows.append(edges[1][which, :, lanes])
        else:
            rows.append(own[(row - 1) * PAIR:row * PAIR, lanes])
    return rows


def window(*where):
    return jnp.concatenate(key_rows(*where), axis=0)


def column_window(column, *where):
    return jnp.concatenate([row[column * CELLS:(column + 1) * CELLS] for row in key_rows(*where)], axis=0)


def score_block(keys, queries, t):
    scores = matmul(keys, queries, (1, 1)) * (SCALE * LOG2E)
    if t == ROWS - 1:
        lat = lax.axis_index("lat")
        outside = (lat == 0) | (lat == lax.axis_size("lat") - 1)
        cut = 2 * (keys.shape[0] // 3)
        bias = jnp.where(outside, MASKED, 0.0).astype(F32)
        scores = jnp.concatenate([scores[:cut], scores[cut:] + bias], axis=0)
    return scores


def row_stats(scores, dprobs):
    top = jnp.max(scores, axis=0, keepdims=True)
    weights = jnp.exp2(scores - top)
    total = jnp.sum(weights, axis=0, keepdims=True)
    delta = jnp.sum(weights * dprobs, axis=0, keepdims=True) / total
    return top + jnp.log(total) * LOG2E, delta


def merged(log_a, delta_a, log_b, delta_b):
    top = jnp.maximum(log_a, log_b)
    weight_a = jnp.exp2(log_a - top)
    weight_b = jnp.exp2(log_b - top)
    total = weight_a + weight_b
    return top + jnp.log(total) * LOG2E, (weight_a * delta_a + weight_b * delta_b) / total


def both_parts(mine, theirs, pair, base):
    other = 4 - base
    return merged(mine[pair, base:base + 2], mine[pair, base + 2:base + 4],
                  theirs[pair, other:other + 2], theirs[pair, other + 2:other + 4])


def turned_window(own_turned, edges_turned, t, j):
    at = slice(j * PAIR, (j + 1) * PAIR)
    rows = []
    for row in range(t, t + 3):
        if row in (0, ROWS + 1):
            rows.append(edges_turned[row // (ROWS + 1), at])
        else:
            rows.append(own_turned[at, (row - 1) * PAIR:row * PAIR])
    return jnp.concatenate(rows, axis=1)


def query_parts(keys_turned, dscores, lane):
    turned = matmul(keys_turned, dscores, (1, 0)) * SCALE
    parts = [turned[:, c * PAIR:(c + 1) * PAIR].T for c in range(2)]
    return [jnp.where(lane < 64, part[:CELLS], part[CELLS:]) for part in parts]


def at_tokens(place):
    return slice(place * CELLS, (place + 1) * CELLS)


def pair_lanes(j):
    return slice(j * PAIR, (j + 1) * PAIR)


def tokens_spec(group):
    return pl.BlockSpec((2, CHUNK, PAIR), lambda p: (0, group, p))


keys_spec = pl.BlockSpec((ROWS * PAIR, PAIR), lambda p: (0, p))
edge_spec = pl.BlockSpec((2, PAIR, PAIR), lambda p: (0, 0, p))
part_spec = pl.BlockSpec((1, 8, PAIR), lambda p: (p, 0, 0))
held_spec = pl.BlockSpec((1, 2, 3 * PAIR, WIDE), lambda p: (p, 0, 0, 0))
part_shape = struct((PAIRS, 8, PAIR), F32)
stats_shape = struct((PAIRS, 16, PAIR), F32)
held_shape = struct((PAIRS, 2, 3 * PAIR, WIDE), F32)


def tokens_wide(group):
    return pl.BlockSpec((2, CHUNK, WIDE), lambda g: (0, group, g))


def stats_wide(group):
    return pl.BlockSpec((2, 8, PAIR), lambda g: (g, group, 0))


all_tokens = pl.BlockSpec((2, 2 * CHUNK, WIDE), lambda g: (0, 0, g))
all_stats = pl.BlockSpec((2, 16, PAIR), lambda g: (g, 0, 0))
all_parts = pl.BlockSpec((2 * CHUNK, WIDE), lambda g: (0, g))
sums_wide = pl.BlockSpec((2, CHUNK, WIDE), lambda g: (0, 0, g))
keys_wide = pl.BlockSpec((ROWS * PAIR, WIDE), lambda g: (0, g))
edge_wide = pl.BlockSpec((2, PAIR, WIDE), lambda g: (0, 0, g))
turned_wide = pl.BlockSpec((WIDE, ROWS * PAIR), lambda g: (g, 0))
edge_turned_wide = pl.BlockSpec((2, WIDE, PAIR), lambda g: (0, g, 0))
held_wide = pl.BlockSpec((2, 2, 3 * PAIR, WIDE), lambda g: (g, 0, 0, 0))
halo_wide = pl.BlockSpec((1, 2, 3 * CELLS, WIDE), lambda g: (g, 0, 0, 0))
halo_shape = struct((GROUPS, 2, 3 * CELLS, WIDE), F32)
weight_shape = struct((GROUPS, 2, 3 * CELLS, WIDE), BF16)


def own_scores(rows, side_a, side_b, kd, vd, edges, part, s_out, d_out):
    masks = head_masks(PAIR)
    for place, t in enumerate(rows):
        at = at_tokens(place)
        queries = stacked([side_a[0, at], side_b[0, at]], masks)
        grads = stacked([side_a[1, at], side_b[1, at]], masks)
        scores = score_block(window(kd, edges, 0, t), queries, t)
        dprobs = matmul(window(vd, edges, 1, t), grads, (1, 1))
        s_out[0, place] = scores
        d_out[0, place] = dprobs
        for w, values in enumerate(row_stats(scores, dprobs)):
            for c in range(2):
                index = 4 * c + 2 * w + place
                part[0, index:index + 1] = values[:, pair_lanes(c)]


def mid_scores_kernel(side_0, side_1, kd, vd, part, s_out, d_out, turned):
    own_scores(MID_ROWS, side_0, side_1, kd, vd, None, part, s_out, d_out)
    turned[...] = kd[...].T


def edge_scores_kernel(side_0, side_1, kd, vd, edge_a, edge_b, part, s_out, d_out):
    own_scores(EDGE_ROWS, side_0, side_1, kd, vd, (edge_a, edge_b), part, s_out, d_out)


def mid_scores(*operands):
    return pl.pallas_call(
        mid_scores_kernel,
        grid=(PAIRS,),
        in_specs=[tokens_spec(MID)] * 2 + [keys_spec] * 2,
        out_specs=[part_spec] + [held_spec] * 2 + [pl.BlockSpec((PAIR, ROWS * PAIR), lambda p: (p, 0))],
        out_shape=[part_shape] + [held_shape] * 2 + [struct((FEAT, ROWS * PAIR), BF16)],
        compiler_params=params(),
        cost_estimate=cost(2e9, 1 << 10),
        name="mid_scores",
    )(*operands)


def edge_scores(*operands):
    return pl.pallas_call(
        edge_scores_kernel,
        grid=(PAIRS,),
        in_specs=[tokens_spec(EDGE)] * 2 + [keys_spec] * 2 + [edge_spec] * 2,
        out_specs=[part_spec] + [held_spec] * 2,
        out_shape=[part_shape] + [held_shape] * 2,
        compiler_params=params(),
        cost_estimate=cost(2e9, 1 << 10),
        name="edge_scores",
    )(*operands)


def turn_edges_kernel(edge_a, edge_b, turned):
    turned[0] = edge_a[0].T
    turned[1] = edge_b[0].T


def turn_edges(*operands):
    return pl.pallas_call(
        turn_edges_kernel,
        grid=(PAIRS,),
        in_specs=[edge_spec] * 2,
        out_specs=pl.BlockSpec((2, PAIR, PAIR), lambda p: (0, p, 0)),
        out_shape=struct((2, FEAT, PAIR), BF16),
        compiler_params=params(),
        cost_estimate=cost(1e9, 1 << 10),
        name="turn_edges",
    )(*operands)


def halo_scores_kernel(c, q_in, kd, vd, edge_a, edge_b, edge_part, mid_part, send, s_edge, d_edge, s_mid, d_mid):
    masks = head_masks(WIDE)
    groups = ((EDGE_ROWS, edge_part, s_edge, d_edge), (MID_ROWS, mid_part, s_mid, d_mid))
    for group, (rows, part, s_out, d_out) in enumerate(groups):
        base = 8 * group
        for j in range(2):
            send[j, base:base + 4] = part[j, 4 * c:4 * c + 4]
        for place, t in enumerate(rows):
            at = at_tokens(2 * group + place)
            queries = stacked([q_in[0, at]], masks)
            grads = stacked([q_in[1, at]], masks)
            scores = score_block(column_window(c, kd, (edge_a, edge_b), 0, t), queries, t)
            dprobs = matmul(column_window(c, vd, (edge_a, edge_b), 1, t), grads, (1, 1))
            s_out[0, place] = scores
            d_out[0, place] = dprobs
            for w, values in enumerate(row_stats(scores, dprobs)):
                index = base + 4 + 2 * w + place
                for j in range(2):
                    send[j, index:index + 1] = values[:, pair_lanes(j)]


def halo_scores(c, *operands):
    part = pl.BlockSpec((2, 8, PAIR), lambda g: (g, 0, 0))
    return pl.pallas_call(
        functools.partial(halo_scores_kernel, c),
        grid=(GROUPS,),
        in_specs=[all_tokens] + [keys_wide] * 2 + [edge_wide] * 2 + [part] * 2,
        out_specs=[all_stats] + [halo_wide] * 4,
        out_shape=[stats_shape] + [halo_shape] * 4,
        compiler_params=params(),
        cost_estimate=cost(2e9, 1 << 10),
        name="halo_scores_" + "ab"[c],
    )(*operands)


def halo_queries_kernel(c, send, recv, s_edge, d_edge, s_mid, d_mid, own_turned, edges_turned,
                        out, p_edge, ds_edge, p_mid, ds_mid):
    lane = lax.broadcasted_iota(jnp.int32, (1, PAIR), 1)
    none = jnp.zeros((CELLS, PAIR), BF16)
    groups = ((EDGE_ROWS, s_edge, d_edge, p_edge, ds_edge), (MID_ROWS, s_mid, d_mid, p_mid, ds_mid))
    for group, (rows, s_in, d_in, p_out, ds_out) in enumerate(groups):
        mine, theirs = [ref.at[:, pl.ds(8 * group, 8)] for ref in (send, recv)]
        both = [both_parts(mine, theirs, j, 4) for j in range(2)]
        log_total, delta = [jnp.concatenate([one[w] for one in both], axis=1) for w in range(2)]
        for place, t in enumerate(rows):
            probs = jnp.exp2(s_in[0, place] - log_total[place:place + 1])
            dscores = (probs * (d_in[0, place] - delta[place:place + 1])).astype(BF16)
            p_out[0, place] = probs.astype(BF16)
            ds_out[0, place] = dscores
            for j in range(2):
                pieces = []
                for i in range(3):
                    part = dscores[at_tokens(i), pair_lanes(j)]
                    pieces += [none, part] if c else [part, none]
                turned = matmul(turned_window(own_turned, edges_turned, t, j), jnp.concatenate(pieces, axis=0), (1, 0))
                grad = turned.T * SCALE
                out[at_tokens(2 * group + place), pair_lanes(j)] = jnp.where(lane < 64, grad[:CELLS], grad[CELLS:]).astype(BF16)


def halo_queries(c, *operands):
    return pl.pallas_call(
        functools.partial(halo_queries_kernel, c),
        grid=(GROUPS,),
        in_specs=[all_stats] * 2 + [halo_wide] * 4 + [turned_wide, edge_turned_wide],
        out_specs=[all_parts] + [halo_wide] * 4,
        out_shape=[struct((2 * CHUNK, FEAT), BF16)] + [weight_shape] * 4,
        compiler_params=params(),
        cost_estimate=cost(0, 1 << 10),
        name="halo_queries_" + "ab"[c],
    )(*operands)


def row_gradients(rows, side_0, side_1, q_0, q_1, send_0, send_1, recv_0, recv_1, s_own, d_own, p_0, ds_0, p_1, ds_1,
                  own_turned, edges_turned, dq_ref):
    masks, wide_masks = head_masks(PAIR), head_masks(WIDE)
    lane = lax.broadcasted_iota(jnp.int32, (1, PAIR), 1)
    merged_rows = []
    for j in range(2):
        both = [both_parts(send_0, recv_0, j, 0), both_parts(send_1, recv_1, j, 0)]
        merged_rows.append([jnp.concatenate([one[w] for one in both], axis=1) for w in range(2)])
    results = []
    for place, t in enumerate(rows):
        at, row = at_tokens(place), slice(place, place + 1)
        sums = [[], []]
        for j in range(2):
            lanes = pair_lanes(j)
            queries = stacked([side_0[0, at, lanes], side_1[0, at, lanes]], masks)
            grads = stacked([side_0[1, at, lanes], side_1[1, at, lanes]], masks)
            log_total, delta = merged_rows[j]
            probs = jnp.exp2(s_own[j, place] - log_total[row])
            dscores = (probs * (d_own[j, place] - delta[row])).astype(BF16)
            for c, part in enumerate(query_parts(turned_window(own_turned, edges_turned, t, j), dscores, lane)):
                dq_ref[c, at, lanes] = part
            sums[0].append(matmul(dscores, queries, (1, 0)))
            sums[1].append(matmul(probs.astype(BF16), grads, (1, 0)))
        sums = [jnp.concatenate(parts, axis=1) for parts in sums]
        edge_parts = []
        for q_in, p_halo, ds_halo in ((q_0, p_0, ds_0), (q_1, p_1, ds_1)):
            edge_parts.append((matmul(ds_halo[0, place], stacked([q_in[0, at]], wide_masks), (1, 0)),
                               matmul(p_halo[0, place], stacked([q_in[1, at]], wide_masks), (1, 0))))
        results.append([jnp.concatenate([sums[w][at_tokens(2 * i + c)] + edge_parts[c][w][at_tokens(i)]
                                         for i in range(3) for c in range(2)], axis=0) for w in range(2)])
    return results


def edge_kernel(*refs):
    operands, (_, _, dq_ref, dk_ref, dv_ref, out_a, out_b) = refs[:16], refs[16:]
    upper, lower = row_gradients(EDGE_ROWS, *operands, dq_ref)
    for which, (out, scale) in enumerate(((dk_ref, SCALE), (dv_ref, 1.0))):
        top, bottom = upper[which] * scale, lower[which] * scale
        out_a[which] = top[:PAIR].astype(BF16)
        out[0:2 * PAIR] = top[PAIR:]
        out_b[which] = bottom[2 * PAIR:].astype(BF16)
        out[2 * PAIR:] = bottom[:2 * PAIR]


def mid_kernel(*refs):
    operands, (dk_in, dv_in, dq_ref, dk_ref, dv_ref) = refs[:15], refs[15:]
    upper, lower = row_gradients(MID_ROWS, *operands, None, dq_ref)
    for which, (sums, out, scale) in enumerate(((dk_in, dk_ref, SCALE), (dv_in, dv_ref, 1.0))):
        out[0:PAIR] = sums[0:PAIR] + upper[which][:PAIR] * scale
        out[PAIR:3 * PAIR] = sums[PAIR:3 * PAIR] + (upper[which][PAIR:] + lower[which][:2 * PAIR]) * scale
        out[3 * PAIR:] = sums[3 * PAIR:] + lower[which][2 * PAIR:] * scale


def row_specs(group):
    return ([tokens_wide(group)] * 4 + [stats_wide(group)] * 4 + [held_wide] * 2 + [halo_wide] * 4 + [turned_wide])


GRAD_SPECS = [sums_wide] + [keys_wide] * 2
GRAD_SHAPES = [struct((2, CHUNK, FEAT), F32)] + [struct((ROWS * PAIR, FEAT), F32)] * 2


def edge_gradients(*operands):
    return pl.pallas_call(
        edge_kernel,
        grid=(GROUPS,),
        in_specs=row_specs(EDGE) + [edge_turned_wide, any_spec, any_spec],
        out_specs=GRAD_SPECS + [edge_wide] * 2,
        out_shape=GRAD_SHAPES + [struct((2, PAIR, FEAT), BF16)] * 2,
        compiler_params=params(),
        cost_estimate=cost(3e9, 1 << 10),
        name="edge_gradients",
    )(*operands)


def mid_gradients(*operands):
    return pl.pallas_call(
        mid_kernel,
        grid=(GROUPS,),
        in_specs=row_specs(MID) + [keys_wide] * 2,
        out_specs=GRAD_SPECS,
        out_shape=GRAD_SHAPES,
        compiler_params=params(),
        cost_estimate=cost(3e9, 1 << 10),
        name="mid_gradients",
    )(*operands)


def join_columns(side_a, side_b):
    parts = ordered(side_a, side_b)
    return jnp.concatenate([part.reshape(8, 8, FEAT) for part in parts], axis=1).astype(BF16)


def sender(refs, buffers, sems):
    copies = []

    def send(i, t, value):
        buffers[i, t] = value
        copies.append(pltpu.make_async_copy(buffers.at[i, t], refs[i].at[pl.ds(8 * grid_row(t), 8)], sems.at[i, t]))
        copies[-1].start()

    return copies, send


def inner_kernel(dq_edge, dq_mid, dk, dv, dq_0, dq_1, q_ref, k_ref, v_ref, buffers, sems):
    copies, send = sender((q_ref, k_ref, v_ref), buffers, sems)
    for t in MID_ROWS:
        for which, own in enumerate((dk, dv)):
            full = own[t * PAIR:(t + 1) * PAIR]
            send(1 + which, t, join_columns(full[:CELLS], full[CELLS:]))
    for place, t in enumerate(ORDER):
        dq = (dq_edge, dq_mid)[place // 2]
        at, there = at_tokens(place % 2), at_tokens(place)
        send(0, t, join_columns(dq[0, at] + dq_0[there].astype(F32), dq[1, at] + dq_1[there].astype(F32)))
    for copy in copies:
        copy.wait()


def outer_kernel(dk, dv, from_a, from_b, _k, _v, k_ref, v_ref, buffers, sems):
    copies, send = sender((k_ref, v_ref), buffers, sems)
    for t, part in zip(EDGE_ROWS, (from_a, from_b)):
        for which, own in enumerate((dk, dv)):
            full = own[t * PAIR:(t + 1) * PAIR] + part[which].astype(F32)
            send(which, t, join_columns(full[:CELLS], full[CELLS:]))
    for copy in copies:
        copy.wait()


def finish(dq_edge, dq_mid, dk, dv, dq_0, dq_1, from_a, from_b):
    out = struct((8 * ROWS, 16, FEAT), BF16)
    q_out, k_inner, v_inner = pl.pallas_call(
        inner_kernel,
        out_specs=[any_spec] * 3,
        out_shape=[out] * 3,
        scratch_shapes=[pltpu.VMEM((3, ROWS, 8, 16, FEAT), BF16), pltpu.SemaphoreType.DMA((3, ROWS))],
        compiler_params=params(),
        cost_estimate=cost(0, 1 << 10),
        name="finish_inner",
    )(dq_edge, dq_mid, dk, dv, dq_0, dq_1)
    whole = pl.BlockSpec(memory_space=pltpu.VMEM)
    k_out, v_out = pl.pallas_call(
        outer_kernel,
        in_specs=[whole] * 4 + [any_spec] * 2,
        out_specs=[any_spec] * 2,
        out_shape=[out] * 2,
        input_output_aliases={4: 0, 5: 1},
        scratch_shapes=[pltpu.VMEM((2, ROWS, 8, 16, FEAT), BF16), pltpu.SemaphoreType.DMA((2, ROWS))],
        compiler_params=params(),
        cost_estimate=cost(0, 1 << 10),
        name="finish_outer",
    )(dk, dv, from_a, from_b, k_inner, v_inner)
    return q_out, k_out, v_out


def swap_a(x, axis):
    return lax.ppermute(x, axis, [(i, i ^ 1) for i in range(lax.axis_size(axis))])


def swap_b(x, axis, wrap):
    count = lax.axis_size(axis)
    pairs = []
    for i in range(1, count if wrap else count - 1, 2):
        pairs += [(i, (i + 1) % count), ((i + 1) % count, i)]
    return lax.ppermute(x, axis, pairs)


def swap_lon(c, x):
    return swap_b(x, "lon", True) if c else swap_a(x, "lon")


def on_device(query_vectors, key_vectors, value_vectors, output_grads):
    *sides, own_edge_a, own_edge_b = pack_queries(query_vectors, output_grads, key_vectors, value_vectors)
    kd, vd = pack_keys(key_vectors, value_vectors)
    edge_b = swap_b(own_edge_b, "lat", False)
    halos = [swap_lon(c, side) for c, side in enumerate(sides)]
    edges = (swap_a(own_edge_a, "lat"), edge_b)
    mid_part, *mid_own, turned = mid_scores(*sides, kd, vd)
    edge_part, *edge_own = edge_scores(*sides, kd, vd, *edges)
    edges_turned = turn_edges(*edges)
    sends, recvs, halo_dq, dq_parts, weights = [], [], [], [], []
    for c in range(2):
        send, *held = halo_scores(c, halos[c], kd, vd, *edges, edge_part, mid_part)
        recv = swap_lon(c, send)
        grad, *weight = halo_queries(c, send, recv, *held, turned, edges_turned)
        sends.append(send)
        recvs.append(recv)
        halo_dq.append(grad)
        dq_parts.append(swap_lon(c, grad))
        weights.append(weight)
    shared = (*sides, *halos, *sends, *recvs)
    dq_edge, dk, dv, out_a, out_b = edge_gradients(*shared, *edge_own, *weights[0][:2], *weights[1][:2], turned, edges_turned,
                                                   *halo_dq)
    key_parts = (swap_a(out_a, "lat"), swap_b(out_b, "lat", False))
    dq_mid, dk, dv = mid_gradients(*shared, *mid_own, *weights[0][2:], *weights[1][2:], turned, dk, dv)
    return tuple(finish(dq_edge, dq_mid, dk, dv, *dq_parts, *key_parts))


def solution(mesh):
    spec = P("lat", "lon", None)
    return jax.shard_map(on_device, mesh=mesh, in_specs=(spec,) * 4, out_specs=(spec,) * 3, check_vma=False)
```

```python
import functools

import jax
import jax.numpy as jnp
from jax import lax
from jax.experimental import pallas as pl
from jax.experimental.pallas import tpu as pltpu
from jax.sharding import PartitionSpec as P

ROWS = 4
CELLS = 64
CHUNK = 2 * CELLS
PAIR = 128
WIDE = 256
PAIRS = 4
GROUPS = 2
FEAT = 512
SCALE = 64 ** -0.5
LOG2E = 1.4426950408889634
MASKED = -1e30
F32 = jnp.float32
BF16 = jnp.bfloat16
VMEM_LIMIT = 20 * 1024 * 1024
PACK_LIMIT = 62 * 1024 * 1024
any_spec = pl.BlockSpec(memory_space=pl.ANY)
EDGE_ROWS = (0, 3)
MID_ROWS = (1, 2)
ORDER = EDGE_ROWS + MID_ROWS
EDGE, MID = 0, 1


def matmul(a, b, contract):
    return lax.dot_general(a, b, ((contract[:1], contract[1:]), ((), ())), preferred_element_type=F32)


def params(limit=VMEM_LIMIT):
    return pltpu.CompilerParams(vmem_limit_bytes=limit)


def cost(flops, size):
    return pl.CostEstimate(flops=int(flops), bytes_accessed=int(size), transcendentals=0)


def struct(shape, dtype):
    return jax.ShapeDtypeStruct(shape, dtype)


def grid_row(t):
    return jnp.where(lax.axis_index("lat") % 2 == 0, ROWS - 1 - t, t)


def ordered(first, second):
    swap = lax.axis_index("lon") % 2 == 0
    return jnp.where(swap, second, first), jnp.where(swap, first, second)


def split_columns(block):
    wide = block.astype(F32)
    parts = ordered(*[wide[:, c * 8:(c + 1) * 8].reshape(CELLS, FEAT) for c in range(2)])
    return [part.astype(BF16) for part in parts]


def fetch(refs, rows, buffers, sems):
    copies = [[pltpu.make_async_copy(ref.at[pl.ds(8 * grid_row(t), 8)], buffers.at[i, place], sems.at[i, place])
               for place, t in enumerate(rows)] for i, ref in enumerate(refs)]
    for place in range(len(rows)):
        for copy in copies:
            copy[place].start()
    return copies


def key_tile(buffer):
    return jnp.concatenate(split_columns(buffer), axis=0)


def pack_queries_kernel(q_ref, g_ref, k_ref, v_ref, side_0, side_1, edge_a, edge_b, buffers, sems, key_buffers, key_sems,
                        packed, out_sems, packed_keys, key_out_sems):
    key_copies = fetch((k_ref, v_ref), EDGE_ROWS, key_buffers, key_sems)
    copies = fetch((q_ref, g_ref), ORDER, buffers, sems)
    sends = []

    def send(source, out, sem):
        sends.append(pltpu.make_async_copy(source, out, sem))
        sends[-1].start()

    for place, edge in enumerate((edge_a, edge_b)):
        for i in range(2):
            key_copies[i][place].wait()
            packed_keys[place, i] = key_tile(key_buffers[i, place])
            send(packed_keys.at[place, i], edge.at[i], key_out_sems.at[place, i])
    for place in range(ROWS):
        for i in range(2):
            copies[i][place].wait()
            for side, (value, out) in enumerate(zip(split_columns(buffers[i, place]), (side_0, side_1))):
                packed[side, i, place] = value
                send(packed.at[side, i, place], out.at[i, pl.ds(place * CELLS, CELLS)], out_sems.at[side, i, place])
    for copy in sends:
        copy.wait()


def pack_queries(*operands):
    return pl.pallas_call(
        pack_queries_kernel,
        in_specs=[any_spec] * 4,
        out_specs=[any_spec] * 4,
        out_shape=[struct((2, ROWS * CELLS, FEAT), BF16)] * 2 + [struct((2, PAIR, FEAT), BF16)] * 2,
        scratch_shapes=[
            pltpu.VMEM((2, ROWS, 8, 16, FEAT), BF16), pltpu.SemaphoreType.DMA((2, ROWS)),
            pltpu.VMEM((2, 2, 8, 16, FEAT), BF16), pltpu.SemaphoreType.DMA((2, 2)),
            pltpu.VMEM((2, 2, ROWS, CELLS, FEAT), BF16), pltpu.SemaphoreType.DMA((2, 2, ROWS)),
            pltpu.VMEM((2, 2, PAIR, FEAT), BF16), pltpu.SemaphoreType.DMA((2, 2)),
        ],
        compiler_params=params(PACK_LIMIT),
        cost_estimate=cost(0, 3 << 20),
        name="pack_queries",
    )(*operands)


def pack_keys_kernel(k_ref, v_ref, kd, vd, buffers, sems):
    copies = fetch((k_ref, v_ref), range(ROWS), buffers, sems)
    for t in range(ROWS):
        for i, out in enumerate((kd, vd)):
            copies[i][t].wait()
            out[t * PAIR:(t + 1) * PAIR] = key_tile(buffers[i, t])


def pack_keys(*operands):
    return pl.pallas_call(
        pack_keys_kernel,
        in_specs=[any_spec] * 2,
        out_shape=[struct((ROWS * PAIR, FEAT), BF16)] * 2,
        scratch_shapes=[pltpu.VMEM((2, ROWS, 8, 16, FEAT), BF16), pltpu.SemaphoreType.DMA((2, ROWS))],
        compiler_params=params(),
        cost_estimate=cost(0, 3 << 20),
        name="pack_keys",
    )(*operands)


def head_masks(lanes):
    lane = lax.broadcasted_iota(jnp.int32, (1, lanes), 1)
    return [jnp.where((lane >= 64 * h) & (lane < 64 * (h + 1)), 1.0, 0.0).astype(F32).astype(BF16)
            for h in range(lanes // 64)]


def stacked(parts, masks):
    return jnp.concatenate([part * mask for part in parts for mask in masks], axis=0)


def key_rows(own, edges, which, t, lanes=slice(None)):
    rows = []
    for row in range(t, t + 3):
        if row == 0:
            rows.append(edges[0][which, :, lanes])
        elif row == ROWS + 1:
            rows.append(edges[1][which, :, lanes])
        else:
            rows.append(own[(row - 1) * PAIR:row * PAIR, lanes])
    return rows


def window(*where):
    return jnp.concatenate(key_rows(*where), axis=0)


def column_window(column, *where):
    return jnp.concatenate([row[column * CELLS:(column + 1) * CELLS] for row in key_rows(*where)], axis=0)


def score_block(keys, queries, t):
    scores = matmul(keys, queries, (1, 1)) * (SCALE * LOG2E)
    if t == ROWS - 1:
        lat = lax.axis_index("lat")
        outside = (lat == 0) | (lat == lax.axis_size("lat") - 1)
        cut = 2 * (keys.shape[0] // 3)
        bias = jnp.where(outside, MASKED, 0.0).astype(F32)
        scores = jnp.concatenate([scores[:cut], scores[cut:] + bias], axis=0)
    return scores


def row_stats(scores, dprobs):
    top = jnp.max(scores, axis=0, keepdims=True)
    weights = jnp.exp2(scores - top)
    total = jnp.sum(weights, axis=0, keepdims=True)
    delta = jnp.sum(weights * dprobs, axis=0, keepdims=True) / total
    return top + jnp.log(total) * LOG2E, delta


def merged(log_a, delta_a, log_b, delta_b):
    top = jnp.maximum(log_a, log_b)
    weight_a = jnp.exp2(log_a - top)
    weight_b = jnp.exp2(log_b - top)
    total = weight_a + weight_b
    return top + jnp.log(total) * LOG2E, (weight_a * delta_a + weight_b * delta_b) / total


def both_parts(mine, theirs, pair, base):
    other = 4 - base
    return merged(mine[pair, base:base + 2], mine[pair, base + 2:base + 4],
                  theirs[pair, other:other + 2], theirs[pair, other + 2:other + 4])


def turned_window(own_turned, edges_turned, t, j):
    at = slice(j * PAIR, (j + 1) * PAIR)
    rows = []
    for row in range(t, t + 3):
        if row in (0, ROWS + 1):
            rows.append(edges_turned[row // (ROWS + 1), at])
        else:
            rows.append(own_turned[at, (row - 1) * PAIR:row * PAIR])
    return jnp.concatenate(rows, axis=1)


def query_parts(keys_turned, dscores, lane):
    turned = matmul(keys_turned, dscores, (1, 0)) * SCALE
    parts = [turned[:, c * PAIR:(c + 1) * PAIR].T for c in range(2)]
    return [jnp.where(lane < 64, part[:CELLS], part[CELLS:]) for part in parts]


def at_tokens(place):
    return slice(place * CELLS, (place + 1) * CELLS)


def pair_lanes(j):
    return slice(j * PAIR, (j + 1) * PAIR)


def tokens_spec(group):
    return pl.BlockSpec((2, CHUNK, PAIR), lambda p: (0, group, p))


keys_spec = pl.BlockSpec((ROWS * PAIR, PAIR), lambda p: (0, p))
edge_spec = pl.BlockSpec((2, PAIR, PAIR), lambda p: (0, 0, p))
part_spec = pl.BlockSpec((1, 8, PAIR), lambda p: (p, 0, 0))
held_spec = pl.BlockSpec((1, 2, 3 * PAIR, WIDE), lambda p: (p, 0, 0, 0))
part_shape = struct((PAIRS, 8, PAIR), F32)
stats_shape = struct((PAIRS, 16, PAIR), F32)
held_shape = struct((PAIRS, 2, 3 * PAIR, WIDE), F32)


def tokens_wide(group):
    return pl.BlockSpec((2, CHUNK, WIDE), lambda g: (0, group, g))


def stats_wide(group):
    return pl.BlockSpec((2, 8, PAIR), lambda g: (g, group, 0))


all_tokens = pl.BlockSpec((2, 2 * CHUNK, WIDE), lambda g: (0, 0, g))
all_stats = pl.BlockSpec((2, 16, PAIR), lambda g: (g, 0, 0))
all_parts = pl.BlockSpec((2 * CHUNK, WIDE), lambda g: (0, g))
sums_wide = pl.BlockSpec((2, CHUNK, WIDE), lambda g: (0, 0, g))
keys_wide = pl.BlockSpec((ROWS * PAIR, WIDE), lambda g: (0, g))
edge_wide = pl.BlockSpec((2, PAIR, WIDE), lambda g: (0, 0, g))
turned_wide = pl.BlockSpec((WIDE, ROWS * PAIR), lambda g: (g, 0))
edge_turned_wide = pl.BlockSpec((2, WIDE, PAIR), lambda g: (0, g, 0))
held_wide = pl.BlockSpec((2, 2, 3 * PAIR, WIDE), lambda g: (g, 0, 0, 0))
halo_wide = pl.BlockSpec((1, 2, 3 * CELLS, WIDE), lambda g: (g, 0, 0, 0))
halo_shape = struct((GROUPS, 2, 3 * CELLS, WIDE), F32)
weight_shape = struct((GROUPS, 2, 3 * CELLS, WIDE), BF16)


def own_scores(rows, side_a, side_b, kd, vd, edges, part, s_out, d_out):
    masks = head_masks(PAIR)
    for place, t in enumerate(rows):
        at = at_tokens(place)
        queries = stacked([side_a[0, at], side_b[0, at]], masks)
        grads = stacked([side_a[1, at], side_b[1, at]], masks)
        scores = score_block(window(kd, edges, 0, t), queries, t)
        dprobs = matmul(window(vd, edges, 1, t), grads, (1, 1))
        s_out[0, place] = scores
        d_out[0, place] = dprobs
        for w, values in enumerate(row_stats(scores, dprobs)):
            for c in range(2):
                index = 4 * c + 2 * w + place
                part[0, index:index + 1] = values[:, pair_lanes(c)]


def mid_scores_kernel(side_0, side_1, kd, vd, part, s_out, d_out, turned):
    own_scores(MID_ROWS, side_0, side_1, kd, vd, None, part, s_out, d_out)
    turned[...] = kd[...].T


def edge_scores_kernel(side_0, side_1, kd, vd, edge_a, edge_b, part, s_out, d_out):
    own_scores(EDGE_ROWS, side_0, side_1, kd, vd, (edge_a, edge_b), part, s_out, d_out)


def mid_scores(*operands):
    return pl.pallas_call(
        mid_scores_kernel,
        grid=(PAIRS,),
        in_specs=[tokens_spec(MID)] * 2 + [keys_spec] * 2,
        out_specs=[part_spec] + [held_spec] * 2 + [pl.BlockSpec((PAIR, ROWS * PAIR), lambda p: (p, 0))],
        out_shape=[part_shape] + [held_shape] * 2 + [struct((FEAT, ROWS * PAIR), BF16)],
        compiler_params=params(),
        cost_estimate=cost(2e9, 1 << 10),
        name="mid_scores",
    )(*operands)


def edge_scores(*operands):
    return pl.pallas_call(
        edge_scores_kernel,
        grid=(PAIRS,),
        in_specs=[tokens_spec(EDGE)] * 2 + [keys_spec] * 2 + [edge_spec] * 2,
        out_specs=[part_spec] + [held_spec] * 2,
        out_shape=[part_shape] + [held_shape] * 2,
        compiler_params=params(),
        cost_estimate=cost(2e9, 1 << 10),
        name="edge_scores",
    )(*operands)


def turn_edges_kernel(edge_a, edge_b, turned):
    turned[0] = edge_a[0].T
    turned[1] = edge_b[0].T


def turn_edges(*operands):
    return pl.pallas_call(
        turn_edges_kernel,
        grid=(PAIRS,),
        in_specs=[edge_spec] * 2,
        out_specs=pl.BlockSpec((2, PAIR, PAIR), lambda p: (0, p, 0)),
        out_shape=struct((2, FEAT, PAIR), BF16),
        compiler_params=params(),
        cost_estimate=cost(1e9, 1 << 10),
        name="turn_edges",
    )(*operands)


def halo_scores_kernel(c, q_in, kd, vd, edge_a, edge_b, edge_part, mid_part, send, s_edge, d_edge, s_mid, d_mid):
    masks = head_masks(WIDE)
    groups = ((EDGE_ROWS, edge_part, s_edge, d_edge), (MID_ROWS, mid_part, s_mid, d_mid))
    for group, (rows, part, s_out, d_out) in enumerate(groups):
        base = 8 * group
        for j in range(2):
            send[j, base:base + 4] = part[j, 4 * c:4 * c + 4]
        for place, t in enumerate(rows):
            at = at_tokens(2 * group + place)
            queries = stacked([q_in[0, at]], masks)
            grads = stacked([q_in[1, at]], masks)
            scores = score_block(column_window(c, kd, (edge_a, edge_b), 0, t), queries, t)
            dprobs = matmul(column_window(c, vd, (edge_a, edge_b), 1, t), grads, (1, 1))
            s_out[0, place] = scores
            d_out[0, place] = dprobs
            for w, values in enumerate(row_stats(scores, dprobs)):
                index = base + 4 + 2 * w + place
                for j in range(2):
                    send[j, index:index + 1] = values[:, pair_lanes(j)]


def halo_scores(c, *operands):
    part = pl.BlockSpec((2, 8, PAIR), lambda g: (g, 0, 0))
    return pl.pallas_call(
        functools.partial(halo_scores_kernel, c),
        grid=(GROUPS,),
        in_specs=[all_tokens] + [keys_wide] * 2 + [edge_wide] * 2 + [part] * 2,
        out_specs=[all_stats] + [halo_wide] * 4,
        out_shape=[stats_shape] + [halo_shape] * 4,
        compiler_params=params(),
        cost_estimate=cost(2e9, 1 << 10),
        name="halo_scores_" + "ab"[c],
    )(*operands)


def halo_queries_kernel(c, send, recv, s_edge, d_edge, s_mid, d_mid, own_turned, edges_turned,
                        out, p_edge, ds_edge, p_mid, ds_mid):
    lane = lax.broadcasted_iota(jnp.int32, (1, PAIR), 1)
    none = jnp.zeros((CELLS, PAIR), BF16)
    groups = ((EDGE_ROWS, s_edge, d_edge, p_edge, ds_edge), (MID_ROWS, s_mid, d_mid, p_mid, ds_mid))
    for group, (rows, s_in, d_in, p_out, ds_out) in enumerate(groups):
        mine, theirs = [ref.at[:, pl.ds(8 * group, 8)] for ref in (send, recv)]
        both = [both_parts(mine, theirs, j, 4) for j in range(2)]
        log_total, delta = [jnp.concatenate([one[w] for one in both], axis=1) for w in range(2)]
        for place, t in enumerate(rows):
            probs = jnp.exp2(s_in[0, place] - log_total[place:place + 1])
            dscores = (probs * (d_in[0, place] - delta[place:place + 1])).astype(BF16)
            p_out[0, place] = probs.astype(BF16)
            ds_out[0, place] = dscores
            for j in range(2):
                pieces = []
                for i in range(3):
                    part = dscores[at_tokens(i), pair_lanes(j)]
                    pieces += [none, part] if c else [part, none]
                turned = matmul(turned_window(own_turned, edges_turned, t, j), jnp.concatenate(pieces, axis=0), (1, 0))
                grad = turned.T * SCALE
                out[at_tokens(2 * group + place), pair_lanes(j)] = jnp.where(lane < 64, grad[:CELLS], grad[CELLS:]).astype(BF16)


def halo_queries(c, *operands):
    return pl.pallas_call(
        functools.partial(halo_queries_kernel, c),
        grid=(GROUPS,),
        in_specs=[all_stats] * 2 + [halo_wide] * 4 + [turned_wide, edge_turned_wide],
        out_specs=[all_parts] + [halo_wide] * 4,
        out_shape=[struct((2 * CHUNK, FEAT), BF16)] + [weight_shape] * 4,
        compiler_params=params(),
        cost_estimate=cost(0, 1 << 10),
        name="halo_queries_" + "ab"[c],
    )(*operands)


def row_gradients(rows, side_0, side_1, q_0, q_1, send_0, send_1, recv_0, recv_1, s_own, d_own, p_0, ds_0, p_1, ds_1,
                  own_turned, edges_turned, dq_ref):
    masks, wide_masks = head_masks(PAIR), head_masks(WIDE)
    lane = lax.broadcasted_iota(jnp.int32, (1, PAIR), 1)
    merged_rows = []
    for j in range(2):
        both = [both_parts(send_0, recv_0, j, 0), both_parts(send_1, recv_1, j, 0)]
        merged_rows.append([jnp.concatenate([one[w] for one in both], axis=1) for w in range(2)])
    results = []
    for place, t in enumerate(rows):
        at, row = at_tokens(place), slice(place, place + 1)
        sums = [[], []]
        for j in range(2):
            lanes = pair_lanes(j)
            queries = stacked([side_0[0, at, lanes], side_1[0, at, lanes]], masks)
            grads = stacked([side_0[1, at, lanes], side_1[1, at, lanes]], masks)
            log_total, delta = merged_rows[j]
            probs = jnp.exp2(s_own[j, place] - log_total[row])
            dscores = (probs * (d_own[j, place] - delta[row])).astype(BF16)
            for c, part in enumerate(query_parts(turned_window(own_turned, edges_turned, t, j), dscores, lane)):
                dq_ref[c, at, lanes] = part
            sums[0].append(matmul(dscores, queries, (1, 0)))
            sums[1].append(matmul(probs.astype(BF16), grads, (1, 0)))
        sums = [jnp.concatenate(parts, axis=1) for parts in sums]
        edge_parts = []
        for q_in, p_halo, ds_halo in ((q_0, p_0, ds_0), (q_1, p_1, ds_1)):
            edge_parts.append((matmul(ds_halo[0, place], stacked([q_in[0, at]], wide_masks), (1, 0)),
                               matmul(p_halo[0, place], stacked([q_in[1, at]], wide_masks), (1, 0))))
        results.append([jnp.concatenate([sums[w][at_tokens(2 * i + c)] + edge_parts[c][w][at_tokens(i)]
                                         for i in range(3) for c in range(2)], axis=0) for w in range(2)])
    return results


def edge_kernel(*refs):
    operands, (_, dq_ref, dk_ref, dv_ref, out_a, out_b) = refs[:16], refs[16:]
    upper, lower = row_gradients(EDGE_ROWS, *operands, dq_ref)
    for which, (out, scale) in enumerate(((dk_ref, SCALE), (dv_ref, 1.0))):
        top, bottom = upper[which] * scale, lower[which] * scale
        out_a[which] = top[:PAIR].astype(BF16)
        out[0:2 * PAIR] = top[PAIR:]
        out_b[which] = bottom[2 * PAIR:].astype(BF16)
        out[2 * PAIR:] = bottom[:2 * PAIR]


def mid_kernel(*refs):
    operands, (dk_in, dv_in, dq_ref, dk_ref, dv_ref) = refs[:15], refs[15:]
    upper, lower = row_gradients(MID_ROWS, *operands, None, dq_ref)
    for which, (sums, out, scale) in enumerate(((dk_in, dk_ref, SCALE), (dv_in, dv_ref, 1.0))):
        out[0:PAIR] = sums[0:PAIR] + upper[which][:PAIR] * scale
        out[PAIR:3 * PAIR] = sums[PAIR:3 * PAIR] + (upper[which][PAIR:] + lower[which][:2 * PAIR]) * scale
        out[3 * PAIR:] = sums[3 * PAIR:] + lower[which][2 * PAIR:] * scale


def row_specs(group):
    return ([tokens_wide(group)] * 4 + [stats_wide(group)] * 4 + [held_wide] * 2 + [halo_wide] * 4 + [turned_wide])


GRAD_SPECS = [sums_wide] + [keys_wide] * 2
GRAD_SHAPES = [struct((2, CHUNK, FEAT), F32)] + [struct((ROWS * PAIR, FEAT), F32)] * 2


def edge_gradients(*operands):
    return pl.pallas_call(
        edge_kernel,
        grid=(GROUPS,),
        in_specs=row_specs(EDGE) + [edge_turned_wide, any_spec],
        out_specs=GRAD_SPECS + [edge_wide] * 2,
        out_shape=GRAD_SHAPES + [struct((2, PAIR, FEAT), BF16)] * 2,
        compiler_params=params(),
        cost_estimate=cost(3e9, 1 << 10),
        name="edge_gradients",
    )(*operands)


def mid_gradients(*operands):
    return pl.pallas_call(
        mid_kernel,
        grid=(GROUPS,),
        in_specs=row_specs(MID) + [keys_wide] * 2,
        out_specs=GRAD_SPECS,
        out_shape=GRAD_SHAPES,
        compiler_params=params(),
        cost_estimate=cost(3e9, 1 << 10),
        name="mid_gradients",
    )(*operands)


def join_columns(side_a, side_b):
    parts = ordered(side_a, side_b)
    return jnp.concatenate([part.reshape(8, 8, FEAT) for part in parts], axis=1).astype(BF16)


def sender(refs, buffers, sems):
    copies = []

    def send(i, t, value):
        buffers[i, t] = value
        copies.append(pltpu.make_async_copy(buffers.at[i, t], refs[i].at[pl.ds(8 * grid_row(t), 8)], sems.at[i, t]))
        copies[-1].start()

    return copies, send


def keys_kernel(dk, dv, from_a, from_b, k_ref, v_ref, buffers, sems):
    copies, send = sender((k_ref, v_ref), buffers, sems)
    for t in MID_ROWS + EDGE_ROWS:
        for which, own in enumerate((dk, dv)):
            full = own[t * PAIR:(t + 1) * PAIR]
            if t in EDGE_ROWS:
                full = full + (from_b if t else from_a)[which].astype(F32)
            send(which, t, join_columns(full[:CELLS], full[CELLS:]))
    for copy in copies:
        copy.wait()


def queries_kernel(dq_edge, dq_mid, dq_0, dq_1, q_ref, buffers, sems):
    copies, send = sender((q_ref,), buffers, sems)
    for place, t in enumerate(ORDER):
        dq = (dq_edge, dq_mid)[place // 2]
        at, there = at_tokens(place % 2), at_tokens(place)
        send(0, t, join_columns(dq[0, at] + dq_0[there].astype(F32), dq[1, at] + dq_1[there].astype(F32)))
    for copy in copies:
        copy.wait()


def finish(kernel, count, operands, name):
    return pl.pallas_call(
        kernel,
        out_specs=[any_spec] * count,
        out_shape=[struct((8 * ROWS, 16, FEAT), BF16)] * count,
        scratch_shapes=[pltpu.VMEM((count, ROWS, 8, 16, FEAT), BF16), pltpu.SemaphoreType.DMA((count, ROWS))],
        compiler_params=params(),
        cost_estimate=cost(0, 1 << 10),
        name=name,
    )(*operands)


def swap_a(x, axis):
    return lax.ppermute(x, axis, [(i, i ^ 1) for i in range(lax.axis_size(axis))])


def swap_b(x, axis, wrap):
    count = lax.axis_size(axis)
    pairs = []
    for i in range(1, count if wrap else count - 1, 2):
        pairs += [(i, (i + 1) % count), ((i + 1) % count, i)]
    return lax.ppermute(x, axis, pairs)


def swap_lon(c, x):
    return swap_b(x, "lon", True) if c else swap_a(x, "lon")


def on_device(query_vectors, key_vectors, value_vectors, output_grads):
    *sides, own_edge_a, own_edge_b = pack_queries(query_vectors, output_grads, key_vectors, value_vectors)
    kd, vd = pack_keys(key_vectors, value_vectors)
    edge_b = swap_b(own_edge_b, "lat", False)
    halos = [swap_lon(c, side) for c, side in enumerate(sides)]
    edges = (swap_a(own_edge_a, "lat"), edge_b)
    mid_part, *mid_own, turned = mid_scores(*sides, kd, vd)
    edge_part, *edge_own = edge_scores(*sides, kd, vd, *edges)
    edges_turned = turn_edges(*edges)
    sends, recvs, halo_dq, dq_parts, weights = [], [], [], [], []
    for c in range(2):
        send, *held = halo_scores(c, halos[c], kd, vd, *edges, edge_part, mid_part)
        recv = swap_lon(c, send)
        grad, *weight = halo_queries(c, send, recv, *held, turned, edges_turned)
        sends.append(send)
        recvs.append(recv)
        halo_dq.append(grad)
        dq_parts.append(swap_lon(c, grad))
        weights.append(weight)
    shared = (*sides, *halos, *sends, *recvs)
    dq_edge, dk, dv, out_a, out_b = edge_gradients(*shared, *edge_own, *weights[0][:2], *weights[1][:2], turned, edges_turned,
                                                   halo_dq[1])
    key_parts = (swap_a(out_a, "lat"), swap_b(out_b, "lat", False))
    dq_mid, dk, dv = mid_gradients(*shared, *mid_own, *weights[0][2:], *weights[1][2:], turned, dk, dv)
    k_out, v_out = finish(keys_kernel, 2, (dk, dv, *key_parts), "finish_keys")
    q_out, = finish(queries_kernel, 1, (dq_edge, dq_mid, *dq_parts), "finish_queries")
    return q_out, k_out, v_out


def solution(mesh):
    spec = P("lat", "lon", None)
    return jax.shard_map(on_device, mesh=mesh, in_specs=(spec,) * 4, out_specs=(spec,) * 3, check_vma=False)
```

```python
import functools

import jax
import jax.numpy as jnp
from jax import lax
from jax.experimental import pallas as pl
from jax.experimental.pallas import tpu as pltpu
from jax.sharding import PartitionSpec as P

ROWS = 4
CELLS = 64
CHUNK = 2 * CELLS
PAIR = 128
WIDE = 256
PAIRS = 4
GROUPS = 2
FEAT = 512
SCALE = 64 ** -0.5
LOG2E = 1.4426950408889634
MASKED = -1e30
F32 = jnp.float32
BF16 = jnp.bfloat16
VMEM_LIMIT = 20 * 1024 * 1024
PACK_LIMIT = 62 * 1024 * 1024
any_spec = pl.BlockSpec(memory_space=pl.ANY)
EDGE_ROWS = (0, 3)
MID_ROWS = (1, 2)
ORDER = EDGE_ROWS + MID_ROWS
EDGE, MID = 0, 1


def matmul(a, b, contract):
    return lax.dot_general(a, b, ((contract[:1], contract[1:]), ((), ())), preferred_element_type=F32)


def params(limit=VMEM_LIMIT):
    return pltpu.CompilerParams(vmem_limit_bytes=limit)


def cost(flops, size):
    return pl.CostEstimate(flops=int(flops), bytes_accessed=int(size), transcendentals=0)


def struct(shape, dtype):
    return jax.ShapeDtypeStruct(shape, dtype)


def grid_row(t):
    return jnp.where(lax.axis_index("lat") % 2 == 0, ROWS - 1 - t, t)


def ordered(first, second):
    swap = lax.axis_index("lon") % 2 == 0
    return jnp.where(swap, second, first), jnp.where(swap, first, second)


def split_columns(block):
    wide = block.astype(F32)
    parts = ordered(*[wide[:, c * 8:(c + 1) * 8].reshape(CELLS, FEAT) for c in range(2)])
    return [part.astype(BF16) for part in parts]


def fetch(refs, rows, buffers, sems):
    copies = [[pltpu.make_async_copy(ref.at[pl.ds(8 * grid_row(t), 8)], buffers.at[i, place], sems.at[i, place])
               for place, t in enumerate(rows)] for i, ref in enumerate(refs)]
    for place in range(len(rows)):
        for copy in copies:
            copy[place].start()
    return copies


def key_tile(buffer):
    return jnp.concatenate(split_columns(buffer), axis=0)


def pack_queries_kernel(q_ref, g_ref, k_ref, v_ref, side_0, side_1, edge_a, edge_b, buffers, sems, key_buffers, key_sems,
                        packed, out_sems, packed_keys, key_out_sems):
    key_copies = fetch((k_ref, v_ref), EDGE_ROWS, key_buffers, key_sems)
    copies = fetch((q_ref, g_ref), ORDER, buffers, sems)
    sends = []

    def send(source, out, sem):
        sends.append(pltpu.make_async_copy(source, out, sem))
        sends[-1].start()

    for place, edge in enumerate((edge_a, edge_b)):
        for i in range(2):
            key_copies[i][place].wait()
            packed_keys[place, i] = key_tile(key_buffers[i, place])
            send(packed_keys.at[place, i], edge.at[i], key_out_sems.at[place, i])
    for place in range(ROWS):
        for i in range(2):
            copies[i][place].wait()
            for side, (value, out) in enumerate(zip(split_columns(buffers[i, place]), (side_0, side_1))):
                packed[side, i, place] = value
                send(packed.at[side, i, place], out.at[i, pl.ds(place * CELLS, CELLS)], out_sems.at[side, i, place])
    for copy in sends:
        copy.wait()


def pack_queries(*operands):
    return pl.pallas_call(
        pack_queries_kernel,
        in_specs=[any_spec] * 4,
        out_specs=[any_spec] * 4,
        out_shape=[struct((2, ROWS * CELLS, FEAT), BF16)] * 2 + [struct((2, PAIR, FEAT), BF16)] * 2,
        scratch_shapes=[
            pltpu.VMEM((2, ROWS, 8, 16, FEAT), BF16), pltpu.SemaphoreType.DMA((2, ROWS)),
            pltpu.VMEM((2, 2, 8, 16, FEAT), BF16), pltpu.SemaphoreType.DMA((2, 2)),
            pltpu.VMEM((2, 2, ROWS, CELLS, FEAT), BF16), pltpu.SemaphoreType.DMA((2, 2, ROWS)),
            pltpu.VMEM((2, 2, PAIR, FEAT), BF16), pltpu.SemaphoreType.DMA((2, 2)),
        ],
        compiler_params=params(PACK_LIMIT),
        cost_estimate=cost(0, 3 << 20),
        name="pack_queries",
    )(*operands)


def pack_keys_kernel(k_ref, v_ref, kd, vd, buffers, sems):
    copies = fetch((k_ref, v_ref), range(ROWS), buffers, sems)
    for t in range(ROWS):
        for i, out in enumerate((kd, vd)):
            copies[i][t].wait()
            out[t * PAIR:(t + 1) * PAIR] = key_tile(buffers[i, t])


def pack_keys(*operands):
    return pl.pallas_call(
        pack_keys_kernel,
        in_specs=[any_spec] * 2,
        out_shape=[struct((ROWS * PAIR, FEAT), BF16)] * 2,
        scratch_shapes=[pltpu.VMEM((2, ROWS, 8, 16, FEAT), BF16), pltpu.SemaphoreType.DMA((2, ROWS))],
        compiler_params=params(),
        cost_estimate=cost(0, 3 << 20),
        name="pack_keys",
    )(*operands)


def head_masks(lanes):
    lane = lax.broadcasted_iota(jnp.int32, (1, lanes), 1)
    return [jnp.where((lane >= 64 * h) & (lane < 64 * (h + 1)), 1.0, 0.0).astype(F32).astype(BF16)
            for h in range(lanes // 64)]


def stacked(parts, masks):
    return jnp.concatenate([part * mask for part in parts for mask in masks], axis=0)


def key_rows(own, edges, which, t, lanes=slice(None)):
    rows = []
    for row in range(t, t + 3):
        if row == 0:
            rows.append(edges[0][which, :, lanes])
        elif row == ROWS + 1:
            rows.append(edges[1][which, :, lanes])
        else:
            rows.append(own[(row - 1) * PAIR:row * PAIR, lanes])
    return rows


def window(*where):
    return jnp.concatenate(key_rows(*where), axis=0)


def column_window(column, *where):
    return jnp.concatenate([row[column * CELLS:(column + 1) * CELLS] for row in key_rows(*where)], axis=0)


def score_block(keys, queries, t):
    scores = matmul(keys, queries, (1, 1)) * (SCALE * LOG2E)
    if t == ROWS - 1:
        lat = lax.axis_index("lat")
        outside = (lat == 0) | (lat == lax.axis_size("lat") - 1)
        cut = 2 * (keys.shape[0] // 3)
        bias = jnp.where(outside, MASKED, 0.0).astype(F32)
        scores = jnp.concatenate([scores[:cut], scores[cut:] + bias], axis=0)
    return scores


def row_stats(scores, dprobs):
    top = jnp.max(scores, axis=0, keepdims=True)
    weights = jnp.exp2(scores - top)
    total = jnp.sum(weights, axis=0, keepdims=True)
    delta = jnp.sum(weights * dprobs, axis=0, keepdims=True) / total
    return top + jnp.log(total) * LOG2E, delta


def merged(log_a, delta_a, log_b, delta_b):
    top = jnp.maximum(log_a, log_b)
    weight_a = jnp.exp2(log_a - top)
    weight_b = jnp.exp2(log_b - top)
    total = weight_a + weight_b
    return top + jnp.log(total) * LOG2E, (weight_a * delta_a + weight_b * delta_b) / total


def both_parts(mine, theirs, pair, base):
    other = 4 - base
    return merged(mine[pair, base:base + 2], mine[pair, base + 2:base + 4],
                  theirs[pair, other:other + 2], theirs[pair, other + 2:other + 4])


def turned_window(own_turned, edges_turned, t, j):
    at = slice(j * PAIR, (j + 1) * PAIR)
    rows = []
    for row in range(t, t + 3):
        if row in (0, ROWS + 1):
            rows.append(edges_turned[row // (ROWS + 1), at])
        else:
            rows.append(own_turned[at, (row - 1) * PAIR:row * PAIR])
    return jnp.concatenate(rows, axis=1)


def query_parts(keys_turned, dscores, lane):
    turned = matmul(keys_turned, dscores, (1, 0)) * SCALE
    parts = [turned[:, c * PAIR:(c + 1) * PAIR].T for c in range(2)]
    return [jnp.where(lane < 64, part[:CELLS], part[CELLS:]) for part in parts]


def at_tokens(place):
    return slice(place * CELLS, (place + 1) * CELLS)


def pair_lanes(j):
    return slice(j * PAIR, (j + 1) * PAIR)


def tokens_spec(group):
    return pl.BlockSpec((2, CHUNK, PAIR), lambda p: (0, group, p))


keys_spec = pl.BlockSpec((ROWS * PAIR, PAIR), lambda p: (0, p))
edge_spec = pl.BlockSpec((2, PAIR, PAIR), lambda p: (0, 0, p))
part_spec = pl.BlockSpec((1, 8, PAIR), lambda p: (p, 0, 0))
held_spec = pl.BlockSpec((1, 2, 3 * PAIR, WIDE), lambda p: (p, 0, 0, 0))
part_shape = struct((PAIRS, 8, PAIR), F32)
stats_shape = struct((PAIRS, 16, PAIR), F32)
held_shape = struct((PAIRS, 2, 3 * PAIR, WIDE), F32)


def tokens_wide(group):
    return pl.BlockSpec((2, CHUNK, WIDE), lambda g: (0, group, g))


def stats_wide(group):
    return pl.BlockSpec((2, 8, PAIR), lambda g: (g, group, 0))


all_tokens = pl.BlockSpec((2, 2 * CHUNK, WIDE), lambda g: (0, 0, g))
all_stats = pl.BlockSpec((2, 16, PAIR), lambda g: (g, 0, 0))
all_parts = pl.BlockSpec((2 * CHUNK, WIDE), lambda g: (0, g))
sums_wide = pl.BlockSpec((2, CHUNK, WIDE), lambda g: (0, 0, g))
keys_wide = pl.BlockSpec((ROWS * PAIR, WIDE), lambda g: (0, g))
edge_wide = pl.BlockSpec((2, PAIR, WIDE), lambda g: (0, 0, g))
turned_wide = pl.BlockSpec((WIDE, ROWS * PAIR), lambda g: (g, 0))
edge_turned_wide = pl.BlockSpec((2, WIDE, PAIR), lambda g: (0, g, 0))
held_wide = pl.BlockSpec((2, 2, 3 * PAIR, WIDE), lambda g: (g, 0, 0, 0))
halo_wide = pl.BlockSpec((1, 2, 3 * CELLS, WIDE), lambda g: (g, 0, 0, 0))
halo_shape = struct((GROUPS, 2, 3 * CELLS, WIDE), F32)
weight_shape = struct((GROUPS, 2, 3 * CELLS, WIDE), BF16)


def own_scores(rows, side_a, side_b, kd, vd, edges, part, s_out, d_out):
    masks = head_masks(PAIR)
    for place, t in enumerate(rows):
        at = at_tokens(place)
        queries = stacked([side_a[0, at], side_b[0, at]], masks)
        grads = stacked([side_a[1, at], side_b[1, at]], masks)
        scores = score_block(window(kd, edges, 0, t), queries, t)
        dprobs = matmul(window(vd, edges, 1, t), grads, (1, 1))
        s_out[0, place] = scores
        d_out[0, place] = dprobs
        for w, values in enumerate(row_stats(scores, dprobs)):
            for c in range(2):
                index = 4 * c + 2 * w + place
                part[0, index:index + 1] = values[:, pair_lanes(c)]


def mid_scores_kernel(side_0, side_1, kd, vd, part, s_out, d_out, turned):
    own_scores(MID_ROWS, side_0, side_1, kd, vd, None, part, s_out, d_out)
    turned[...] = kd[...].T


def edge_scores_kernel(side_0, side_1, kd, vd, edge_a, edge_b, part, s_out, d_out):
    own_scores(EDGE_ROWS, side_0, side_1, kd, vd, (edge_a, edge_b), part, s_out, d_out)


def mid_scores(*operands):
    return pl.pallas_call(
        mid_scores_kernel,
        grid=(PAIRS,),
        in_specs=[tokens_spec(MID)] * 2 + [keys_spec] * 2,
        out_specs=[part_spec] + [held_spec] * 2 + [pl.BlockSpec((PAIR, ROWS * PAIR), lambda p: (p, 0))],
        out_shape=[part_shape] + [held_shape] * 2 + [struct((FEAT, ROWS * PAIR), BF16)],
        compiler_params=params(),
        cost_estimate=cost(2e9, 1 << 10),
        name="mid_scores",
    )(*operands)


def edge_scores(*operands):
    return pl.pallas_call(
        edge_scores_kernel,
        grid=(PAIRS,),
        in_specs=[tokens_spec(EDGE)] * 2 + [keys_spec] * 2 + [edge_spec] * 2,
        out_specs=[part_spec] + [held_spec] * 2,
        out_shape=[part_shape] + [held_shape] * 2,
        compiler_params=params(),
        cost_estimate=cost(2e9, 1 << 10),
        name="edge_scores",
    )(*operands)


def turn_edges_kernel(edge_a, edge_b, turned):
    turned[0] = edge_a[0].T
    turned[1] = edge_b[0].T


def turn_edges(*operands):
    return pl.pallas_call(
        turn_edges_kernel,
        grid=(PAIRS,),
        in_specs=[edge_spec] * 2,
        out_specs=pl.BlockSpec((2, PAIR, PAIR), lambda p: (0, p, 0)),
        out_shape=struct((2, FEAT, PAIR), BF16),
        compiler_params=params(),
        cost_estimate=cost(1e9, 1 << 10),
        name="turn_edges",
    )(*operands)


def halo_scores_kernel(c, q_in, kd, vd, edge_a, edge_b, edge_part, mid_part, send, s_edge, d_edge, s_mid, d_mid):
    masks = head_masks(WIDE)
    groups = ((EDGE_ROWS, edge_part, s_edge, d_edge), (MID_ROWS, mid_part, s_mid, d_mid))
    for group, (rows, part, s_out, d_out) in enumerate(groups):
        base = 8 * group
        for j in range(2):
            send[j, base:base + 4] = part[j, 4 * c:4 * c + 4]
        for place, t in enumerate(rows):
            at = at_tokens(2 * group + place)
            queries = stacked([q_in[0, at]], masks)
            grads = stacked([q_in[1, at]], masks)
            scores = score_block(column_window(c, kd, (edge_a, edge_b), 0, t), queries, t)
            dprobs = matmul(column_window(c, vd, (edge_a, edge_b), 1, t), grads, (1, 1))
            s_out[0, place] = scores
            d_out[0, place] = dprobs
            for w, values in enumerate(row_stats(scores, dprobs)):
                index = base + 4 + 2 * w + place
                for j in range(2):
                    send[j, index:index + 1] = values[:, pair_lanes(j)]


def halo_scores(c, *operands):
    part = pl.BlockSpec((2, 8, PAIR), lambda g: (g, 0, 0))
    return pl.pallas_call(
        functools.partial(halo_scores_kernel, c),
        grid=(GROUPS,),
        in_specs=[all_tokens] + [keys_wide] * 2 + [edge_wide] * 2 + [part] * 2,
        out_specs=[all_stats] + [halo_wide] * 4,
        out_shape=[stats_shape] + [halo_shape] * 4,
        compiler_params=params(),
        cost_estimate=cost(2e9, 1 << 10),
        name="halo_scores_" + "ab"[c],
    )(*operands)


def halo_queries_kernel(c, send, recv, s_edge, d_edge, s_mid, d_mid, own_turned, edges_turned,
                        out, p_edge, ds_edge, p_mid, ds_mid):
    lane = lax.broadcasted_iota(jnp.int32, (1, PAIR), 1)
    none = jnp.zeros((CELLS, PAIR), BF16)
    groups = ((EDGE_ROWS, s_edge, d_edge, p_edge, ds_edge), (MID_ROWS, s_mid, d_mid, p_mid, ds_mid))
    for group, (rows, s_in, d_in, p_out, ds_out) in enumerate(groups):
        mine, theirs = [ref.at[:, pl.ds(8 * group, 8)] for ref in (send, recv)]
        both = [both_parts(mine, theirs, j, 4) for j in range(2)]
        log_total, delta = [jnp.concatenate([one[w] for one in both], axis=1) for w in range(2)]
        for place, t in enumerate(rows):
            probs = jnp.exp2(s_in[0, place] - log_total[place:place + 1])
            dscores = (probs * (d_in[0, place] - delta[place:place + 1])).astype(BF16)
            p_out[0, place] = probs.astype(BF16)
            ds_out[0, place] = dscores
            for j in range(2):
                pieces = []
                for i in range(3):
                    part = dscores[at_tokens(i), pair_lanes(j)]
                    pieces += [none, part] if c else [part, none]
                turned = matmul(turned_window(own_turned, edges_turned, t, j), jnp.concatenate(pieces, axis=0), (1, 0))
                grad = turned.T * SCALE
                out[at_tokens(2 * group + place), pair_lanes(j)] = jnp.where(lane < 64, grad[:CELLS], grad[CELLS:]).astype(BF16)


def halo_queries(c, *operands):
    return pl.pallas_call(
        functools.partial(halo_queries_kernel, c),
        grid=(GROUPS,),
        in_specs=[all_stats] * 2 + [halo_wide] * 4 + [turned_wide, edge_turned_wide],
        out_specs=[all_parts] + [halo_wide] * 4,
        out_shape=[struct((2 * CHUNK, FEAT), BF16)] + [weight_shape] * 4,
        compiler_params=params(),
        cost_estimate=cost(0, 1 << 10),
        name="halo_queries_" + "ab"[c],
    )(*operands)


def row_gradients(places, side_0, side_1, q_0, q_1, send_0, send_1, recv_0, recv_1, s_own, d_own, p_0, ds_0, p_1, ds_1,
                  own_turned, edges_turned, dq_ref):
    masks, wide_masks = head_masks(PAIR), head_masks(WIDE)
    lane = lax.broadcasted_iota(jnp.int32, (1, PAIR), 1)
    merged_rows = []
    for j in range(2):
        both = [both_parts(send_0, recv_0, j, 0), both_parts(send_1, recv_1, j, 0)]
        merged_rows.append([jnp.concatenate([one[w] for one in both], axis=1) for w in range(2)])
    results = []
    for index, (place, t) in enumerate(places):
        at, row = at_tokens(place), slice(place, place + 1)
        sums = [[], []]
        for j in range(2):
            lanes = pair_lanes(j)
            queries = stacked([side_0[0, at, lanes], side_1[0, at, lanes]], masks)
            grads = stacked([side_0[1, at, lanes], side_1[1, at, lanes]], masks)
            log_total, delta = merged_rows[j]
            probs = jnp.exp2(s_own[j, place] - log_total[row])
            dscores = (probs * (d_own[j, place] - delta[row])).astype(BF16)
            for c, part in enumerate(query_parts(turned_window(own_turned, edges_turned, t, j), dscores, lane)):
                dq_ref[c, at_tokens(index), lanes] = part
            sums[0].append(matmul(dscores, queries, (1, 0)))
            sums[1].append(matmul(probs.astype(BF16), grads, (1, 0)))
        sums = [jnp.concatenate(parts, axis=1) for parts in sums]
        edge_parts = []
        for q_in, p_halo, ds_halo in ((q_0, p_0, ds_0), (q_1, p_1, ds_1)):
            edge_parts.append((matmul(ds_halo[0, place], stacked([q_in[0, at]], wide_masks), (1, 0)),
                               matmul(p_halo[0, place], stacked([q_in[1, at]], wide_masks), (1, 0))))
        results.append([jnp.concatenate([sums[w][at_tokens(2 * i + c)] + edge_parts[c][w][at_tokens(i)]
                                         for i in range(3) for c in range(2)], axis=0) for w in range(2)])
    return results


def edge_kernel(place, *refs):
    operands, (_, _, dq_ref, dk_ref, dv_ref, out) = refs[:16], refs[16:]
    parts, = row_gradients(((place, EDGE_ROWS[place]),), *operands, dq_ref)
    for which, (sums, scale) in enumerate(((dk_ref, SCALE), (dv_ref, 1.0))):
        part = parts[which] * scale
        out[which] = (part[2 * PAIR:] if place else part[:PAIR]).astype(BF16)
        sums[...] = part[:2 * PAIR] if place else part[PAIR:]


def mid_kernel(*refs):
    operands, (dk_a, dv_a, dk_b, dv_b, dq_ref, dk_ref, dv_ref) = refs[:15], refs[15:]
    upper, lower = row_gradients(tuple(enumerate(MID_ROWS)), *operands, None, dq_ref)
    for which, (top, bottom, out, scale) in enumerate(((dk_a, dk_b, dk_ref, SCALE), (dv_a, dv_b, dv_ref, 1.0))):
        both = upper[which][PAIR:] + lower[which][:2 * PAIR]
        out[0:PAIR] = top[:PAIR] + upper[which][:PAIR] * scale
        out[PAIR:2 * PAIR] = top[PAIR:] + both[:PAIR] * scale
        out[2 * PAIR:3 * PAIR] = bottom[:PAIR] + both[PAIR:] * scale
        out[3 * PAIR:] = bottom[PAIR:] + lower[which][2 * PAIR:] * scale


def row_specs(group):
    return ([tokens_wide(group)] * 4 + [stats_wide(group)] * 4 + [held_wide] * 2 + [halo_wide] * 4 + [turned_wide])


GRAD_SPECS = [sums_wide] + [keys_wide] * 2
GRAD_SHAPES = [struct((2, CHUNK, FEAT), F32)] + [struct((ROWS * PAIR, FEAT), F32)] * 2


def edge_gradients(place, *operands):
    half = pl.BlockSpec((2 * PAIR, WIDE), lambda g: (0, g))
    return pl.pallas_call(
        functools.partial(edge_kernel, place),
        grid=(GROUPS,),
        in_specs=row_specs(EDGE) + [edge_turned_wide, any_spec, any_spec],
        out_specs=[pl.BlockSpec((2, CELLS, WIDE), lambda g: (0, 0, g))] + [half] * 2 + [edge_wide],
        out_shape=[struct((2, CELLS, FEAT), F32)] + [struct((2 * PAIR, FEAT), F32)] * 2 + [struct((2, PAIR, FEAT), BF16)],
        compiler_params=params(),
        cost_estimate=cost(2e9, 1 << 10),
        name="edge_gradients_" + "ab"[place],
    )(*operands)


def mid_gradients(*operands):
    half = pl.BlockSpec((2 * PAIR, WIDE), lambda g: (0, g))
    return pl.pallas_call(
        mid_kernel,
        grid=(GROUPS,),
        in_specs=row_specs(MID) + [half] * 4,
        out_specs=GRAD_SPECS,
        out_shape=GRAD_SHAPES,
        compiler_params=params(),
        cost_estimate=cost(3e9, 1 << 10),
        name="mid_gradients",
    )(*operands)


def join_columns(side_a, side_b):
    parts = ordered(side_a, side_b)
    return jnp.concatenate([part.reshape(8, 8, FEAT) for part in parts], axis=1).astype(BF16)


def sender(refs, buffers, sems):
    copies = []

    def send(i, t, value):
        buffers[i, t] = value
        copies.append(pltpu.make_async_copy(buffers.at[i, t], refs[i].at[pl.ds(8 * grid_row(t), 8)], sems.at[i, t]))
        copies[-1].start()

    return copies, send


def inner_kernel(dq_a, dq_b, dq_mid, dk, dv, dq_0, dq_1, q_ref, k_ref, v_ref, buffers, sems):
    copies, send = sender((q_ref, k_ref, v_ref), buffers, sems)
    for t in MID_ROWS:
        for which, own in enumerate((dk, dv)):
            full = own[t * PAIR:(t + 1) * PAIR]
            send(1 + which, t, join_columns(full[:CELLS], full[CELLS:]))
    for place, t in enumerate(ORDER):
        dq = (dq_a, dq_b, dq_mid, dq_mid)[place]
        at, there = at_tokens(max(place - 2, 0)), at_tokens(place)
        send(0, t, join_columns(dq[0, at] + dq_0[there].astype(F32), dq[1, at] + dq_1[there].astype(F32)))
    for copy in copies:
        copy.wait()


def outer_kernel(dk, dv, from_a, from_b, _k, _v, k_ref, v_ref, buffers, sems):
    copies, send = sender((k_ref, v_ref), buffers, sems)
    for t, part in zip(EDGE_ROWS, (from_a, from_b)):
        for which, own in enumerate((dk, dv)):
            full = own[t * PAIR:(t + 1) * PAIR] + part[which].astype(F32)
            send(which, t, join_columns(full[:CELLS], full[CELLS:]))
    for copy in copies:
        copy.wait()


def finish(dq_a, dq_b, dq_mid, dk, dv, dq_0, dq_1, from_a, from_b):
    out = struct((8 * ROWS, 16, FEAT), BF16)
    q_out, k_inner, v_inner = pl.pallas_call(
        inner_kernel,
        out_specs=[any_spec] * 3,
        out_shape=[out] * 3,
        scratch_shapes=[pltpu.VMEM((3, ROWS, 8, 16, FEAT), BF16), pltpu.SemaphoreType.DMA((3, ROWS))],
        compiler_params=params(),
        cost_estimate=cost(0, 1 << 10),
        name="finish_inner",
    )(dq_a, dq_b, dq_mid, dk, dv, dq_0, dq_1)
    whole = pl.BlockSpec(memory_space=pltpu.VMEM)
    k_out, v_out = pl.pallas_call(
        outer_kernel,
        in_specs=[whole] * 4 + [any_spec] * 2,
        out_specs=[any_spec] * 2,
        out_shape=[out] * 2,
        input_output_aliases={4: 0, 5: 1},
        scratch_shapes=[pltpu.VMEM((2, ROWS, 8, 16, FEAT), BF16), pltpu.SemaphoreType.DMA((2, ROWS))],
        compiler_params=params(),
        cost_estimate=cost(0, 1 << 10),
        name="finish_outer",
    )(dk, dv, from_a, from_b, k_inner, v_inner)
    return q_out, k_out, v_out


def swap_a(x, axis):
    return lax.ppermute(x, axis, [(i, i ^ 1) for i in range(lax.axis_size(axis))])


def swap_b(x, axis, wrap):
    count = lax.axis_size(axis)
    pairs = []
    for i in range(1, count if wrap else count - 1, 2):
        pairs += [(i, (i + 1) % count), ((i + 1) % count, i)]
    return lax.ppermute(x, axis, pairs)


def swap_lon(c, x):
    return swap_b(x, "lon", True) if c else swap_a(x, "lon")


def on_device(query_vectors, key_vectors, value_vectors, output_grads):
    *sides, own_edge_a, own_edge_b = pack_queries(query_vectors, output_grads, key_vectors, value_vectors)
    kd, vd = pack_keys(key_vectors, value_vectors)
    edge_b = swap_b(own_edge_b, "lat", False)
    halos = [swap_lon(c, side) for c, side in enumerate(sides)]
    edges = (swap_a(own_edge_a, "lat"), edge_b)
    mid_part, *mid_own, turned = mid_scores(*sides, kd, vd)
    edge_part, *edge_own = edge_scores(*sides, kd, vd, *edges)
    edges_turned = turn_edges(*edges)
    sends, recvs, halo_dq, dq_parts, weights = [], [], [], [], []
    for c in range(2):
        send, *held = halo_scores(c, halos[c], kd, vd, *edges, edge_part, mid_part)
        recv = swap_lon(c, send)
        grad, *weight = halo_queries(c, send, recv, *held, turned, edges_turned)
        sends.append(send)
        recvs.append(recv)
        halo_dq.append(grad)
        dq_parts.append(swap_lon(c, grad))
        weights.append(weight)
    shared = (*sides, *halos, *sends, *recvs)
    edge_operands = (*shared, *edge_own, *weights[0][:2], *weights[1][:2], turned, edges_turned)
    dq_b, dk_b, dv_b, out_b = edge_gradients(1, *edge_operands, *halo_dq)
    from_b = swap_b(out_b, "lat", False)
    dq_a, dk_a, dv_a, out_a = edge_gradients(0, *edge_operands, out_b, halo_dq[1])
    from_a = swap_a(out_a, "lat")
    dq_mid, dk, dv = mid_gradients(*shared, *mid_own, *weights[0][2:], *weights[1][2:], turned, dk_a, dv_a, dk_b, dv_b)
    return tuple(finish(dq_a, dq_b, dq_mid, dk, dv, *dq_parts, from_a, from_b))


def solution(mesh):
    spec = P("lat", "lon", None)
    return jax.shard_map(on_device, mesh=mesh, in_specs=(spec,) * 4, out_specs=(spec,) * 3, check_vma=False)
```

```python
import functools

import jax
import jax.numpy as jnp
from jax import lax
from jax.experimental import pallas as pl
from jax.experimental.pallas import tpu as pltpu
from jax.sharding import PartitionSpec as P

ROWS = 4
CELLS = 64
CHUNK = 2 * CELLS
PAIR = 128
WIDE = 256
PAIRS = 4
GROUPS = 2
FEAT = 512
SCALE = 64 ** -0.5
LOG2E = 1.4426950408889634
MASKED = -1e30
F32 = jnp.float32
BF16 = jnp.bfloat16
VMEM_LIMIT = 20 * 1024 * 1024
PACK_LIMIT = 62 * 1024 * 1024
any_spec = pl.BlockSpec(memory_space=pl.ANY)
EDGE_ROWS = (0, 3)
MID_ROWS = (1, 2)
ORDER = EDGE_ROWS + MID_ROWS
EDGE, MID = 0, 1


def matmul(a, b, contract):
    return lax.dot_general(a, b, ((contract[:1], contract[1:]), ((), ())), preferred_element_type=F32)


def params(limit=VMEM_LIMIT):
    return pltpu.CompilerParams(vmem_limit_bytes=limit)


def cost(flops, size):
    return pl.CostEstimate(flops=int(flops), bytes_accessed=int(size), transcendentals=0)


def struct(shape, dtype):
    return jax.ShapeDtypeStruct(shape, dtype)


def grid_row(t):
    return jnp.where(lax.axis_index("lat") % 2 == 0, ROWS - 1 - t, t)


def ordered(first, second):
    swap = lax.axis_index("lon") % 2 == 0
    return jnp.where(swap, second, first), jnp.where(swap, first, second)


def split_columns(block):
    wide = block.astype(F32)
    parts = ordered(*[wide[:, c * 8:(c + 1) * 8].reshape(CELLS, FEAT) for c in range(2)])
    return [part.astype(BF16) for part in parts]


def fetch(refs, rows, buffers, sems):
    copies = [[pltpu.make_async_copy(ref.at[pl.ds(8 * grid_row(t), 8)], buffers.at[i, place], sems.at[i, place])
               for place, t in enumerate(rows)] for i, ref in enumerate(refs)]
    for place in range(len(rows)):
        for copy in copies:
            copy[place].start()
    return copies


def key_tile(buffer):
    return jnp.concatenate(split_columns(buffer), axis=0)


def pack_queries_kernel(q_ref, g_ref, k_ref, v_ref, side_0, side_1, edge_a, edge_b, buffers, sems, key_buffers, key_sems,
                        packed, out_sems, packed_keys, key_out_sems):
    key_copies = fetch((k_ref, v_ref), EDGE_ROWS, key_buffers, key_sems)
    copies = fetch((q_ref, g_ref), ORDER, buffers, sems)
    sends = []

    def send(source, out, sem):
        sends.append(pltpu.make_async_copy(source, out, sem))
        sends[-1].start()

    for place, edge in enumerate((edge_a, edge_b)):
        for i in range(2):
            key_copies[i][place].wait()
            packed_keys[place, i] = key_tile(key_buffers[i, place])
            send(packed_keys.at[place, i], edge.at[i], key_out_sems.at[place, i])
    for place in range(ROWS):
        for i in range(2):
            copies[i][place].wait()
            for side, (value, out) in enumerate(zip(split_columns(buffers[i, place]), (side_0, side_1))):
                packed[side, i, place] = value
                send(packed.at[side, i, place], out.at[i, pl.ds(place * CELLS, CELLS)], out_sems.at[side, i, place])
    for copy in sends:
        copy.wait()


def pack_queries(*operands):
    return pl.pallas_call(
        pack_queries_kernel,
        in_specs=[any_spec] * 4,
        out_specs=[any_spec] * 4,
        out_shape=[struct((2, ROWS * CELLS, FEAT), BF16)] * 2 + [struct((2, PAIR, FEAT), BF16)] * 2,
        scratch_shapes=[
            pltpu.VMEM((2, ROWS, 8, 16, FEAT), BF16), pltpu.SemaphoreType.DMA((2, ROWS)),
            pltpu.VMEM((2, 2, 8, 16, FEAT), BF16), pltpu.SemaphoreType.DMA((2, 2)),
            pltpu.VMEM((2, 2, ROWS, CELLS, FEAT), BF16), pltpu.SemaphoreType.DMA((2, 2, ROWS)),
            pltpu.VMEM((2, 2, PAIR, FEAT), BF16), pltpu.SemaphoreType.DMA((2, 2)),
        ],
        compiler_params=params(PACK_LIMIT),
        cost_estimate=cost(0, 3 << 20),
        name="pack_queries",
    )(*operands)


def pack_keys_kernel(k_ref, v_ref, kd, vd, buffers, sems):
    copies = fetch((k_ref, v_ref), range(ROWS), buffers, sems)
    for t in range(ROWS):
        for i, out in enumerate((kd, vd)):
            copies[i][t].wait()
            out[t * PAIR:(t + 1) * PAIR] = key_tile(buffers[i, t])


def pack_keys(*operands):
    return pl.pallas_call(
        pack_keys_kernel,
        in_specs=[any_spec] * 2,
        out_shape=[struct((ROWS * PAIR, FEAT), BF16)] * 2,
        scratch_shapes=[pltpu.VMEM((2, ROWS, 8, 16, FEAT), BF16), pltpu.SemaphoreType.DMA((2, ROWS))],
        compiler_params=params(),
        cost_estimate=cost(0, 3 << 20),
        name="pack_keys",
    )(*operands)


def head_masks(lanes):
    lane = lax.broadcasted_iota(jnp.int32, (1, lanes), 1)
    return [jnp.where((lane >= 64 * h) & (lane < 64 * (h + 1)), 1.0, 0.0).astype(F32).astype(BF16)
            for h in range(lanes // 64)]


def stacked(parts, masks):
    return jnp.concatenate([part * mask for part in parts for mask in masks], axis=0)


def key_rows(own, edges, which, t, lanes=slice(None)):
    rows = []
    for row in range(t, t + 3):
        if row == 0:
            rows.append(edges[0][which, :, lanes])
        elif row == ROWS + 1:
            rows.append(edges[1][which, :, lanes])
        else:
            rows.append(own[(row - 1) * PAIR:row * PAIR, lanes])
    return rows


def window(*where):
    return jnp.concatenate(key_rows(*where), axis=0)


def column_window(column, *where):
    return jnp.concatenate([row[column * CELLS:(column + 1) * CELLS] for row in key_rows(*where)], axis=0)


def score_block(keys, queries, t):
    scores = matmul(keys, queries, (1, 1)) * (SCALE * LOG2E)
    if t == ROWS - 1:
        lat = lax.axis_index("lat")
        outside = (lat == 0) | (lat == lax.axis_size("lat") - 1)
        cut = 2 * (keys.shape[0] // 3)
        bias = jnp.where(outside, MASKED, 0.0).astype(F32)
        scores = jnp.concatenate([scores[:cut], scores[cut:] + bias], axis=0)
    return scores


def row_stats(scores, dprobs):
    top = jnp.max(scores, axis=0, keepdims=True)
    weights = jnp.exp2(scores - top)
    total = jnp.sum(weights, axis=0, keepdims=True)
    delta = jnp.sum(weights * dprobs, axis=0, keepdims=True) / total
    return top + jnp.log(total) * LOG2E, delta


def merged(log_a, delta_a, log_b, delta_b):
    top = jnp.maximum(log_a, log_b)
    weight_a = jnp.exp2(log_a - top)
    weight_b = jnp.exp2(log_b - top)
    total = weight_a + weight_b
    return top + jnp.log(total) * LOG2E, (weight_a * delta_a + weight_b * delta_b) / total


def both_parts(mine, theirs, pair, base):
    other = 4 - base
    return merged(mine[pair, base:base + 2], mine[pair, base + 2:base + 4],
                  theirs[pair, other:other + 2], theirs[pair, other + 2:other + 4])


def turned_window(own_turned, edges_turned, t, j):
    at = slice(j * PAIR, (j + 1) * PAIR)
    rows = []
    for row in range(t, t + 3):
        if row in (0, ROWS + 1):
            rows.append(edges_turned[row // (ROWS + 1), at])
        else:
            rows.append(own_turned[at, (row - 1) * PAIR:row * PAIR])
    return jnp.concatenate(rows, axis=1)


def query_parts(keys_turned, dscores, lane):
    turned = matmul(keys_turned, dscores, (1, 0)) * SCALE
    parts = [turned[:, c * PAIR:(c + 1) * PAIR].T for c in range(2)]
    return [jnp.where(lane < 64, part[:CELLS], part[CELLS:]) for part in parts]


def at_tokens(place):
    return slice(place * CELLS, (place + 1) * CELLS)


def pair_lanes(j):
    return slice(j * PAIR, (j + 1) * PAIR)


def tokens_spec(group):
    return pl.BlockSpec((2, CHUNK, PAIR), lambda p: (0, group, p))


keys_spec = pl.BlockSpec((ROWS * PAIR, PAIR), lambda p: (0, p))
edge_spec = pl.BlockSpec((2, PAIR, PAIR), lambda p: (0, 0, p))
part_spec = pl.BlockSpec((1, 8, PAIR), lambda p: (p, 0, 0))
held_spec = pl.BlockSpec((1, 2, 3 * PAIR, WIDE), lambda p: (p, 0, 0, 0))
part_shape = struct((PAIRS, 8, PAIR), F32)
stats_shape = struct((PAIRS, 16, PAIR), F32)
held_shape = struct((PAIRS, 2, 3 * PAIR, WIDE), F32)


def tokens_wide(group):
    return pl.BlockSpec((2, CHUNK, WIDE), lambda g: (0, group, g))


def stats_wide(group):
    return pl.BlockSpec((2, 8, PAIR), lambda g: (g, group, 0))


all_tokens = pl.BlockSpec((2, 2 * CHUNK, WIDE), lambda g: (0, 0, g))
all_stats = pl.BlockSpec((2, 16, PAIR), lambda g: (g, 0, 0))
all_parts = pl.BlockSpec((2 * CHUNK, WIDE), lambda g: (0, g))
sums_wide = pl.BlockSpec((2, CHUNK, WIDE), lambda g: (0, 0, g))
keys_wide = pl.BlockSpec((ROWS * PAIR, WIDE), lambda g: (0, g))
edge_wide = pl.BlockSpec((2, PAIR, WIDE), lambda g: (0, 0, g))
turned_wide = pl.BlockSpec((WIDE, ROWS * PAIR), lambda g: (g, 0))
edge_turned_wide = pl.BlockSpec((2, WIDE, PAIR), lambda g: (0, g, 0))
held_wide = pl.BlockSpec((2, 2, 3 * PAIR, WIDE), lambda g: (g, 0, 0, 0))
halo_wide = pl.BlockSpec((1, 2, 3 * CELLS, WIDE), lambda g: (g, 0, 0, 0))
halo_shape = struct((GROUPS, 2, 3 * CELLS, WIDE), F32)
weight_shape = struct((GROUPS, 2, 3 * CELLS, WIDE), BF16)


def own_scores(rows, side_a, side_b, kd, vd, edges, part, s_out, d_out):
    masks = head_masks(PAIR)
    for place, t in enumerate(rows):
        at = at_tokens(place)
        queries = stacked([side_a[0, at], side_b[0, at]], masks)
        grads = stacked([side_a[1, at], side_b[1, at]], masks)
        scores = score_block(window(kd, edges, 0, t), queries, t)
        dprobs = matmul(window(vd, edges, 1, t), grads, (1, 1))
        s_out[0, place] = scores
        d_out[0, place] = dprobs
        for w, values in enumerate(row_stats(scores, dprobs)):
            for c in range(2):
                index = 4 * c + 2 * w + place
                part[0, index:index + 1] = values[:, pair_lanes(c)]


def mid_scores_kernel(side_0, side_1, kd, vd, part, s_out, d_out, turned):
    own_scores(MID_ROWS, side_0, side_1, kd, vd, None, part, s_out, d_out)
    turned[...] = kd[...].T


def edge_scores_kernel(side_0, side_1, kd, vd, edge_a, edge_b, part, s_out, d_out):
    own_scores(EDGE_ROWS, side_0, side_1, kd, vd, (edge_a, edge_b), part, s_out, d_out)


def mid_scores(*operands):
    return pl.pallas_call(
        mid_scores_kernel,
        grid=(PAIRS,),
        in_specs=[tokens_spec(MID)] * 2 + [keys_spec] * 2,
        out_specs=[part_spec] + [held_spec] * 2 + [pl.BlockSpec((PAIR, ROWS * PAIR), lambda p: (p, 0))],
        out_shape=[part_shape] + [held_shape] * 2 + [struct((FEAT, ROWS * PAIR), BF16)],
        compiler_params=params(),
        cost_estimate=cost(2e9, 1 << 10),
        name="mid_scores",
    )(*operands)


def edge_scores(*operands):
    return pl.pallas_call(
        edge_scores_kernel,
        grid=(PAIRS,),
        in_specs=[tokens_spec(EDGE)] * 2 + [keys_spec] * 2 + [edge_spec] * 2,
        out_specs=[part_spec] + [held_spec] * 2,
        out_shape=[part_shape] + [held_shape] * 2,
        compiler_params=params(),
        cost_estimate=cost(2e9, 1 << 10),
        name="edge_scores",
    )(*operands)


def turn_edges_kernel(edge_a, edge_b, _, turned):
    turned[0] = edge_a[0].T
    turned[1] = edge_b[0].T


def turn_edges(*operands):
    return pl.pallas_call(
        turn_edges_kernel,
        grid=(PAIRS,),
        in_specs=[edge_spec] * 2 + [any_spec],
        out_specs=pl.BlockSpec((2, PAIR, PAIR), lambda p: (0, p, 0)),
        out_shape=struct((2, FEAT, PAIR), BF16),
        compiler_params=params(),
        cost_estimate=cost(1e9, 1 << 10),
        name="turn_edges",
    )(*operands)


def halo_scores_kernel(c, q_in, kd, vd, edge_a, edge_b, edge_part, mid_part, *refs):
    send, s_edge, d_edge, s_mid, d_mid = refs[-5:]
    masks = head_masks(WIDE)
    groups = ((EDGE_ROWS, edge_part, s_edge, d_edge), (MID_ROWS, mid_part, s_mid, d_mid))
    for group, (rows, part, s_out, d_out) in enumerate(groups):
        base = 8 * group
        for j in range(2):
            send[j, base:base + 4] = part[j, 4 * c:4 * c + 4]
        for place, t in enumerate(rows):
            at = at_tokens(2 * group + place)
            queries = stacked([q_in[0, at]], masks)
            grads = stacked([q_in[1, at]], masks)
            scores = score_block(column_window(c, kd, (edge_a, edge_b), 0, t), queries, t)
            dprobs = matmul(column_window(c, vd, (edge_a, edge_b), 1, t), grads, (1, 1))
            s_out[0, place] = scores
            d_out[0, place] = dprobs
            for w, values in enumerate(row_stats(scores, dprobs)):
                index = base + 4 + 2 * w + place
                for j in range(2):
                    send[j, index:index + 1] = values[:, pair_lanes(j)]


def halo_scores(c, *operands):
    part = pl.BlockSpec((2, 8, PAIR), lambda g: (g, 0, 0))
    return pl.pallas_call(
        functools.partial(halo_scores_kernel, c),
        grid=(GROUPS,),
        in_specs=[all_tokens] + [keys_wide] * 2 + [edge_wide] * 2 + [part] * 2 + [any_spec] * (len(operands) - 7),
        out_specs=[all_stats] + [halo_wide] * 4,
        out_shape=[stats_shape] + [halo_shape] * 4,
        compiler_params=params(),
        cost_estimate=cost(2e9, 1 << 10),
        name="halo_scores_" + "ab"[c],
    )(*operands)


def halo_queries_kernel(c, send, recv, s_edge, d_edge, s_mid, d_mid, own_turned, edges_turned,
                        out, p_edge, ds_edge, p_mid, ds_mid):
    lane = lax.broadcasted_iota(jnp.int32, (1, PAIR), 1)
    none = jnp.zeros((CELLS, PAIR), BF16)
    groups = ((EDGE_ROWS, s_edge, d_edge, p_edge, ds_edge), (MID_ROWS, s_mid, d_mid, p_mid, ds_mid))
    for group, (rows, s_in, d_in, p_out, ds_out) in enumerate(groups):
        mine, theirs = [ref.at[:, pl.ds(8 * group, 8)] for ref in (send, recv)]
        both = [both_parts(mine, theirs, j, 4) for j in range(2)]
        log_total, delta = [jnp.concatenate([one[w] for one in both], axis=1) for w in range(2)]
        for place, t in enumerate(rows):
            probs = jnp.exp2(s_in[0, place] - log_total[place:place + 1])
            dscores = (probs * (d_in[0, place] - delta[place:place + 1])).astype(BF16)
            p_out[0, place] = probs.astype(BF16)
            ds_out[0, place] = dscores
            for j in range(2):
                pieces = []
                for i in range(3):
                    part = dscores[at_tokens(i), pair_lanes(j)]
                    pieces += [none, part] if c else [part, none]
                turned = matmul(turned_window(own_turned, edges_turned, t, j), jnp.concatenate(pieces, axis=0), (1, 0))
                grad = turned.T * SCALE
                out[at_tokens(2 * group + place), pair_lanes(j)] = jnp.where(lane < 64, grad[:CELLS], grad[CELLS:]).astype(BF16)


def halo_queries(c, *operands):
    return pl.pallas_call(
        functools.partial(halo_queries_kernel, c),
        grid=(GROUPS,),
        in_specs=[all_stats] * 2 + [halo_wide] * 4 + [turned_wide, edge_turned_wide],
        out_specs=[all_parts] + [halo_wide] * 4,
        out_shape=[struct((2 * CHUNK, FEAT), BF16)] + [weight_shape] * 4,
        compiler_params=params(),
        cost_estimate=cost(0, 1 << 10),
        name="halo_queries_" + "ab"[c],
    )(*operands)


def row_gradients(rows, side_0, side_1, q_0, q_1, send_0, send_1, recv_0, recv_1, s_own, d_own, p_0, ds_0, p_1, ds_1,
                  own_turned, edges_turned, dq_ref):
    masks, wide_masks = head_masks(PAIR), head_masks(WIDE)
    lane = lax.broadcasted_iota(jnp.int32, (1, PAIR), 1)
    merged_rows = []
    for j in range(2):
        both = [both_parts(send_0, recv_0, j, 0), both_parts(send_1, recv_1, j, 0)]
        merged_rows.append([jnp.concatenate([one[w] for one in both], axis=1) for w in range(2)])
    results = []
    for place, t in enumerate(rows):
        at, row = at_tokens(place), slice(place, place + 1)
        sums = [[], []]
        for j in range(2):
            lanes = pair_lanes(j)
            queries = stacked([side_0[0, at, lanes], side_1[0, at, lanes]], masks)
            grads = stacked([side_0[1, at, lanes], side_1[1, at, lanes]], masks)
            log_total, delta = merged_rows[j]
            probs = jnp.exp2(s_own[j, place] - log_total[row])
            dscores = (probs * (d_own[j, place] - delta[row])).astype(BF16)
            for c, part in enumerate(query_parts(turned_window(own_turned, edges_turned, t, j), dscores, lane)):
                dq_ref[c, at, lanes] = part
            sums[0].append(matmul(dscores, queries, (1, 0)))
            sums[1].append(matmul(probs.astype(BF16), grads, (1, 0)))
        sums = [jnp.concatenate(parts, axis=1) for parts in sums]
        edge_parts = []
        for q_in, p_halo, ds_halo in ((q_0, p_0, ds_0), (q_1, p_1, ds_1)):
            edge_parts.append((matmul(ds_halo[0, place], stacked([q_in[0, at]], wide_masks), (1, 0)),
                               matmul(p_halo[0, place], stacked([q_in[1, at]], wide_masks), (1, 0))))
        results.append([jnp.concatenate([sums[w][at_tokens(2 * i + c)] + edge_parts[c][w][at_tokens(i)]
                                         for i in range(3) for c in range(2)], axis=0) for w in range(2)])
    return results


def edge_kernel(*refs):
    operands, (_, _, dq_ref, dk_ref, dv_ref, out_a, out_b) = refs[:16], refs[16:]
    upper, lower = row_gradients(EDGE_ROWS, *operands, dq_ref)
    for which, (out, scale) in enumerate(((dk_ref, SCALE), (dv_ref, 1.0))):
        top, bottom = upper[which] * scale, lower[which] * scale
        out_a[which] = top[:PAIR].astype(BF16)
        out[0:2 * PAIR] = top[PAIR:]
        out_b[which] = bottom[2 * PAIR:].astype(BF16)
        out[2 * PAIR:] = bottom[:2 * PAIR]


def mid_kernel(*refs):
    operands, (dk_in, dv_in, dq_ref, dk_ref, dv_ref) = refs[:15], refs[15:]
    upper, lower = row_gradients(MID_ROWS, *operands, None, dq_ref)
    for which, (sums, out, scale) in enumerate(((dk_in, dk_ref, SCALE), (dv_in, dv_ref, 1.0))):
        out[0:PAIR] = sums[0:PAIR] + upper[which][:PAIR] * scale
        out[PAIR:3 * PAIR] = sums[PAIR:3 * PAIR] + (upper[which][PAIR:] + lower[which][:2 * PAIR]) * scale
        out[3 * PAIR:] = sums[3 * PAIR:] + lower[which][2 * PAIR:] * scale


def row_specs(group):
    return ([tokens_wide(group)] * 4 + [stats_wide(group)] * 4 + [held_wide] * 2 + [halo_wide] * 4 + [turned_wide])


GRAD_SPECS = [sums_wide] + [keys_wide] * 2
GRAD_SHAPES = [struct((2, CHUNK, FEAT), F32)] + [struct((ROWS * PAIR, FEAT), F32)] * 2


def edge_gradients(*operands):
    return pl.pallas_call(
        edge_kernel,
        grid=(GROUPS,),
        in_specs=row_specs(EDGE) + [edge_turned_wide, any_spec, any_spec],
        out_specs=GRAD_SPECS + [edge_wide] * 2,
        out_shape=GRAD_SHAPES + [struct((2, PAIR, FEAT), BF16)] * 2,
        compiler_params=params(),
        cost_estimate=cost(3e9, 1 << 10),
        name="edge_gradients",
    )(*operands)


def mid_gradients(*operands):
    return pl.pallas_call(
        mid_kernel,
        grid=(GROUPS,),
        in_specs=row_specs(MID) + [keys_wide] * 2,
        out_specs=GRAD_SPECS,
        out_shape=GRAD_SHAPES,
        compiler_params=params(),
        cost_estimate=cost(3e9, 1 << 10),
        name="mid_gradients",
    )(*operands)


def join_columns(side_a, side_b):
    parts = ordered(side_a, side_b)
    return jnp.concatenate([part.reshape(8, 8, FEAT) for part in parts], axis=1).astype(BF16)


def sender(refs, buffers, sems):
    copies = []

    def send(i, t, value):
        buffers[i, t] = value
        copies.append(pltpu.make_async_copy(buffers.at[i, t], refs[i].at[pl.ds(8 * grid_row(t), 8)], sems.at[i, t]))
        copies[-1].start()

    return copies, send


def inner_kernel(dq_edge, dq_mid, dk, dv, dq_0, dq_1, q_ref, k_ref, v_ref, buffers, sems):
    copies, send = sender((q_ref, k_ref, v_ref), buffers, sems)
    for t in MID_ROWS:
        for which, own in enumerate((dk, dv)):
            full = own[t * PAIR:(t + 1) * PAIR]
            send(1 + which, t, join_columns(full[:CELLS], full[CELLS:]))
    for place, t in enumerate(ORDER):
        dq = (dq_edge, dq_mid)[place // 2]
        at, there = at_tokens(place % 2), at_tokens(place)
        send(0, t, join_columns(dq[0, at] + dq_0[there].astype(F32), dq[1, at] + dq_1[there].astype(F32)))
    for copy in copies:
        copy.wait()


def outer_kernel(dk, dv, from_a, from_b, _k, _v, k_ref, v_ref, buffers, sems):
    copies, send = sender((k_ref, v_ref), buffers, sems)
    for t, part in zip(EDGE_ROWS, (from_a, from_b)):
        for which, own in enumerate((dk, dv)):
            full = own[t * PAIR:(t + 1) * PAIR] + part[which].astype(F32)
            send(which, t, join_columns(full[:CELLS], full[CELLS:]))
    for copy in copies:
        copy.wait()


def finish(dq_edge, dq_mid, dk, dv, dq_0, dq_1, from_a, from_b):
    out = struct((8 * ROWS, 16, FEAT), BF16)
    q_out, k_inner, v_inner = pl.pallas_call(
        inner_kernel,
        out_specs=[any_spec] * 3,
        out_shape=[out] * 3,
        scratch_shapes=[pltpu.VMEM((3, ROWS, 8, 16, FEAT), BF16), pltpu.SemaphoreType.DMA((3, ROWS))],
        compiler_params=params(),
        cost_estimate=cost(0, 1 << 10),
        name="finish_inner",
    )(dq_edge, dq_mid, dk, dv, dq_0, dq_1)
    whole = pl.BlockSpec(memory_space=pltpu.VMEM)
    k_out, v_out = pl.pallas_call(
        outer_kernel,
        in_specs=[whole] * 4 + [any_spec] * 2,
        out_specs=[any_spec] * 2,
        out_shape=[out] * 2,
        input_output_aliases={4: 0, 5: 1},
        scratch_shapes=[pltpu.VMEM((2, ROWS, 8, 16, FEAT), BF16), pltpu.SemaphoreType.DMA((2, ROWS))],
        compiler_params=params(),
        cost_estimate=cost(0, 1 << 10),
        name="finish_outer",
    )(dk, dv, from_a, from_b, k_inner, v_inner)
    return q_out, k_out, v_out


def swap_a(x, axis):
    return lax.ppermute(x, axis, [(i, i ^ 1) for i in range(lax.axis_size(axis))])


def swap_b(x, axis, wrap):
    count = lax.axis_size(axis)
    pairs = []
    for i in range(1, count if wrap else count - 1, 2):
        pairs += [(i, (i + 1) % count), ((i + 1) % count, i)]
    return lax.ppermute(x, axis, pairs)


def swap_lon(c, x):
    return swap_b(x, "lon", True) if c else swap_a(x, "lon")


def on_device(query_vectors, key_vectors, value_vectors, output_grads):
    *sides, own_edge_a, own_edge_b = pack_queries(query_vectors, output_grads, key_vectors, value_vectors)
    kd, vd = pack_keys(key_vectors, value_vectors)
    edge_b = swap_b(own_edge_b, "lat", False)
    halos = [swap_lon(c, side) for c, side in enumerate(sides)]
    edges = (swap_a(own_edge_a, "lat"), edge_b)
    mid_part, *mid_own, turned = mid_scores(*sides, kd, vd)
    edge_part, *edge_own = edge_scores(*sides, kd, vd, *edges)
    sends, recvs, halo_dq, dq_parts, weights = [{} for _ in range(5)]
    for c in (1, 0):
        before = () if c else (edges_turned,)
        sends[c], *held = halo_scores(c, halos[c], kd, vd, *edges, edge_part, mid_part, *before)
        if c:
            edges_turned = turn_edges(*edges, sends[c])
        recvs[c] = swap_lon(c, sends[c])
        halo_dq[c], *weights[c] = halo_queries(c, sends[c], recvs[c], *held, turned, edges_turned)
        dq_parts[c] = swap_lon(c, halo_dq[c])
    sends, recvs, halo_dq, dq_parts = [[one[0], one[1]] for one in (sends, recvs, halo_dq, dq_parts)]
    shared = (*sides, *halos, *sends, *recvs)
    dq_edge, dk, dv, out_a, out_b = edge_gradients(*shared, *edge_own, *weights[0][:2], *weights[1][:2], turned, edges_turned,
                                                   *halo_dq)
    key_parts = (swap_a(out_a, "lat"), swap_b(out_b, "lat", False))
    dq_mid, dk, dv = mid_gradients(*shared, *mid_own, *weights[0][2:], *weights[1][2:], turned, dk, dv)
    return tuple(finish(dq_edge, dq_mid, dk, dv, *dq_parts, *key_parts))


def solution(mesh):
    spec = P("lat", "lon", None)
    return jax.shard_map(on_device, mesh=mesh, in_specs=(spec,) * 4, out_specs=(spec,) * 3, check_vma=False)
```
